32 devices in a mesh: dp: 16 (over z, y, x), mp: 2 (over core).
Axes of the slice: x: 2, y: 2, z: 4, core: 2. Of those that a mesh axis runs over, the one named last changes fastest.
Arguments:
- inputs: bfloat16 [32768, 1024], P('dp', 'mp'), may hold values from -6 to 6
- lengths: int32 [64], P('dp'), may hold values from 80 to 512, as said below
- w_query: bfloat16 [1024, 1024], P(None, 'mp'), may hold values from -0.1875 to 0.1875
- b_query: bfloat16 [1024], P('mp'), may hold values from -3 to 3
- w_key: bfloat16 [1024, 1024], P(None, 'mp'), may hold values from -0.1875 to 0.1875
- w_value: bfloat16 [1024, 1024], P(None, 'mp'), may hold values from -0.1875 to 0.1875
- b_value: bfloat16 [1024], P('mp'), may hold values from -3 to 3
- w_out: bfloat16 [1024, 1024], P('mp'), may hold values from -1.5 to 1.5
- b_out: bfloat16 [1024], P('mp'), may hold values from -3 to 3
- gain_one: bfloat16 [1024], P('mp'), may hold values from 0.5 to 1.5
- shift_one: bfloat16 [1024], P('mp'), may hold values from -3 to 3
- w_in: bfloat16 [1024, 4096], P(None, 'mp'), may hold values from -0.1875 to 0.1875
- b_in: bfloat16 [4096], P('mp'), may hold values from -3 to 3
- w_back: bfloat16 [4096, 1024], P('mp'), may hold values from -0.09375 to 0.09375
- b_back: bfloat16 [1024], P('mp'), may hold values from -3 to 3
- gain_two: bfloat16 [1024], P('mp'), may hold values from 0.5 to 1.5
- shift_two: bfloat16 [1024], P('mp'), may hold values from -3 to 3
- cotangent: bfloat16 [32768, 1024], P('dp', 'mp'), may hold values from -6 to 6
Outputs:
- output: bfloat16 [32768, 1024], P('dp', 'mp')
- input_grad: bfloat16 [32768, 1024], P('dp', 'mp')
- grad_w_query: float32 [1024, 1024], P(None, 'mp')
- grad_b_query: float32 [1024], P('mp')
- grad_w_key: float32 [1024, 1024], P(None, 'mp')
- grad_w_value: float32 [1024, 1024], P(None, 'mp')
- grad_b_value: float32 [1024], P('mp')
- grad_w_out: float32 [1024, 1024], P('mp')
- grad_b_out: float32 [1024], P('mp')
- grad_gain_one: float32 [1024], P('mp')
- grad_shift_one: float32 [1024], P('mp')
- grad_w_in: float32 [1024, 4096], P(None, 'mp')
- grad_b_in: float32 [4096], P('mp')
- grad_w_back: float32 [4096, 1024], P('mp')
- grad_b_back: float32 [1024], P('mp')
- grad_gain_two: float32 [1024], P('mp')
- grad_shift_two: float32 [1024], P('mp')
The draws below stay inside these ranges and needn't reach their ends.
Inputs may be any that keep to these rules, and one draw needn't show every extreme that they name: `lengths`: real tokens of each page; some page has exactly 512 and some exactly 80.
All inputs are finite; a program needn't handle non-finite values.
Results may differ from the reference program's by a relative error of at most 0.02.
Values may be sent and summed in bfloat16 or wider, within the bound.
A program may use at most 192 MiB of HBM per device.

```python
import math
import jax
import jax.numpy as jnp
from jax import lax

D = 1024
HEADS = 16
HDIM = 64
FF = 4096
SEQ = 512
PAGES = 64
TOKENS = 32768
MIN_LEN = 80


def draw_lengths(key, part):
    key = jax.random.fold_in(key, 11)
    key_long, key_short, key_rest = jax.random.split(key, 3)
    values = jax.random.randint(key_rest, (PAGES,), MIN_LEN, SEQ + 1)
    longest = jax.random.randint(key_long, (), 0, PAGES)
    shortest = (longest + 1 + jax.random.randint(key_short, (), 0, PAGES - 1)) % PAGES
    positions = jnp.arange(PAGES)
    values = jnp.where(positions == longest, SEQ, values)
    values = jnp.where(positions == shortest, MIN_LEN, values)
    return values.astype(jnp.int32)


def steps_of(stream_key, shape, cuts, low, top_value):
    def one(axis_at, parts):
        draws = jax.random.uniform(jax.random.fold_in(jax.random.fold_in(stream_key, 6), axis_at), (parts,), jnp.float32, low / len(cuts), top_value / len(cuts))
        return jnp.repeat(jnp.exp(draws), shape[axis_at] // parts).reshape((-1,) + (1,) * (len(shape) - axis_at - 1))

    loudness = one(*cuts[0])
    for cut in cuts[1:]:
        loudness = loudness * one(*cut)
    return loudness


def bell_draw(rng, dims, width, bound, cuts=(), held_as=jnp.bfloat16):
    array = jax.random.normal(rng, dims, jnp.float32) * width
    if len(cuts) > 0:
        array = steps_of(rng, dims, cuts, -0.22, 0.18) * array
    return jnp.clip(array, min=-bound, max=bound).astype(held_as)


def setup_inputs(seed: int = 0) -> dict:
    streams_of = jax.random.split(jax.random.key(seed), 19)
    return {
        "inputs": bell_draw(streams_of[0], (TOKENS, D), 1.0, 6.0, ((0, 16), (1, 2))),
        "lengths": draw_lengths(jax.random.fold_in(streams_of[18], 71), 0),
        "w_query": bell_draw(streams_of[2], (D, D), D ** -0.5, 0.1875, ((1, 2),)),
        "b_query": bell_draw(streams_of[3], (D,), 0.5, 3.0, ((0, 2),)),
        "w_key": bell_draw(streams_of[4], (D, D), D ** -0.5, 0.1875, ((1, 2),)),
        "w_value": bell_draw(streams_of[5], (D, D), D ** -0.5, 0.1875, ((1, 2),)),
        "b_value": bell_draw(streams_of[6], (D,), 0.5, 3.0, ((0, 2),)),
        "w_out": bell_draw(streams_of[7], (D, D), (D // 64) ** -0.5, 1.5, ((0, 2),)),
        "b_out": bell_draw(streams_of[8], (D,), 0.5, 3.0, ((0, 2),)),
        "gain_one": jnp.clip(1.0 + 0.1 * jax.random.normal(streams_of[9], (D,), jnp.float32), 0.5, 1.5).astype(jnp.bfloat16),
        "shift_one": bell_draw(streams_of[10], (D,), 0.5, 3.0, ((0, 2),)),
        "w_in": bell_draw(streams_of[11], (D, FF), D ** -0.5, 0.1875, ((1, 2),)),
        "b_in": bell_draw(streams_of[12], (FF,), 0.5, 3.0, ((0, 2),)),
        "w_back": bell_draw(streams_of[13], (FF, D), FF ** -0.5, 0.09375, ((0, 2),)),
        "b_back": bell_draw(streams_of[14], (D,), 0.5, 3.0, ((0, 2),)),
        "gain_two": jnp.clip(1.0 + 0.1 * jax.random.normal(streams_of[15], (D,), jnp.float32), 0.5, 1.5).astype(jnp.bfloat16),
        "shift_two": bell_draw(streams_of[16], (D,), 0.5, 3.0, ((0, 2),)),
        "cotangent": bell_draw(streams_of[17], (TOKENS, D), 1.0, 6.0, ((0, 16), (1, 2))),
    }


HIGHEST = lax.Precision.HIGHEST
eps = 1e-05

@jax.custom_vjp
def low(v):
    return lax.optimization_barrier(v.astype(jnp.bfloat16)).astype(jnp.float32)

@jax.custom_vjp
def low_back(v):
    return v

def low_keep(v):
    return (low(v), None)

def low_pass(kept, grad):
    return (grad,)

def back_keep(v):
    return (v, None)

def back_low(kept, grad):
    return (low(grad),)
low.defvjp(low_keep, low_pass)
low_back.defvjp(back_keep, back_low)

def matmul(left_side, right_side):
    return jnp.dot(left_side, right_side, precision=HIGHEST)

def normalize(hidden, gain_vec, shift_vec):
    average = lax.optimization_barrier(jnp.mean(hidden, axis=-1, keepdims=True))
    centred = hidden - average
    variance = lax.optimization_barrier(jnp.mean(centred * centred, axis=-1, keepdims=True))
    return centred * lax.rsqrt(variance + eps) * gain_vec + shift_vec

def layer_group(params, inputs, lengths):
    w_query, b_query, w_key, w_value, b_value, w_out, b_out, gain_one, shift_one, w_in, b_in, w_back, b_back, gain_two, shift_two = params
    page_count = lengths.shape[0]
    queries = low_back(low(matmul(inputs, w_query) + b_query)).reshape(page_count, SEQ, HEADS, HDIM)
    keys_all = low_back(low(matmul(inputs, w_key))).reshape(page_count, SEQ, HEADS, HDIM)
    values = low_back(low(matmul(inputs, w_value) + b_value)).reshape(page_count, SEQ, HEADS, HDIM)
    scores = jnp.einsum('pqhd,pkhd->phqk', queries, keys_all, precision=HIGHEST) * HDIM ** (-0.5)
    scores = low_back(scores)
    key_valid = jnp.arange(SEQ).astype(jnp.int32)[None, :] < lengths[:, None]
    scores = jnp.where(key_valid[:, None, None, :], scores, -1e+30)
    weights = low(jax.nn.softmax(scores, axis=-1))
    context = jnp.einsum('phqk,pkhd->pqhd', weights, values, precision=HIGHEST)
    context = low_back(low(context.reshape(page_count * SEQ, D)))
    attended = inputs + low_back(matmul(context, w_out)) + b_out
    hidden_one = normalize(attended, gain_one, shift_one)
    ffn_inner = low_back(matmul(low(hidden_one), w_in) + b_in)
    activated = low(jax.nn.gelu(ffn_inner, approximate=False))
    summed = hidden_one + low_back(matmul(activated, w_back)) + b_back
    return normalize(summed, gain_two, shift_two)

def reference(inputs, lengths, w_query, b_query, w_key, w_value, b_value, w_out, b_out, gain_one, shift_one, w_in, b_in, w_back, b_back, gain_two, shift_two, cotangent):
    params = tuple((weight_arg.astype(jnp.float32) for weight_arg in (w_query, b_query, w_key, w_value, b_value, w_out, b_out, gain_one, shift_one, w_in, b_in, w_back, b_back, gain_two, shift_two)))
    group_pages = math.gcd(PAGES, 8)
    group_count = PAGES // group_pages

    def forward_all(params, tokens_in):
        blocks = tokens_in.reshape(group_count, group_pages * SEQ, D)
        page_lengths = lengths.reshape(group_count, group_pages)

        def per_group(packed):
            return layer_group(params, packed[0], packed[1])
        result = lax.map(jax.checkpoint(per_group), (blocks, page_lengths))
        return result.reshape(TOKENS, D)
    row_valid = (jnp.arange(SEQ).astype(jnp.int32)[None, :] < lengths[:, None]).reshape(TOKENS, 1)
    output, pullback = jax.vjp(forward_all, params, inputs.astype(jnp.float32))
    grads, input_grad = pullback(cotangent.astype(jnp.float32) * row_valid.astype(jnp.float32))
    return (output.astype(jnp.bfloat16), input_grad.astype(jnp.bfloat16), grads[0], grads[1], grads[2], grads[3], grads[4], grads[5], grads[6], grads[7], grads[8], grads[9], grads[10], grads[11], grads[12], grads[13], grads[14])
```

```python
import functools

import jax
import jax.numpy as jnp
from jax import lax
from jax.experimental import pallas as pl
from jax.experimental.pallas import tpu as pltpu
from jax.sharding import PartitionSpec as P

MESH = pl.DeviceIdType.MESH

HDIM = 64


eps = 1e-05


SLOTS = 16
STAGES = (0, 2, 4, 6, 8, 10, 12, 14)


def sum_over_chips(src, out, grads, land_a, land_z, land_m, land_b, ssem, rsem, osem, isem):
    pairs = grads.shape[0]
    dp = lax.axis_index("dp")
    mp = lax.axis_index("mp")
    z, y, x = dp // 4, (dp // 2) % 2, dp % 2
    inner = (z == 1) | (z == 2)
    outer = jnp.logical_not(inner)
    quarter = jnp.where(z == 1, 0, 1)

    def chip(cz, cy, cx):
        return (cz * 4 + cy * 2 + cx, mp)

    first_peer = (chip(z, y, 1 - x), chip(z, 1 - y, x))
    second_peer = (chip(z, 1 - y, x), chip(z, y, 1 - x))
    side = (x, y)
    inward = chip(jnp.where(z == 0, 1, 2), y, x)
    outward = chip(jnp.where(z == 1, 0, 3), y, x)
    across = chip(3 - z, y, x)

    load = pltpu.make_async_copy(src, grads, isem)
    load.start()
    barrier = pltpu.get_barrier_semaphore()
    for peer in first_peer:
        pl.semaphore_signal(barrier, 1, device_id=peer, device_id_type=MESH)

    @pl.when(inner)
    def _():
        for peer in (outward, across):
            pl.semaphore_signal(barrier, 1, device_id=peer, device_id_type=MESH)
        pl.semaphore_wait(barrier, 4)

    @pl.when(outer)
    def _():
        pl.semaphore_signal(barrier, 1, device_id=inward, device_id_type=MESH)
        pl.semaphore_wait(barrier, 3)

    load.wait()

    def half(kind, k, which):
        return grads.at[k, kind, pl.ds(which * 2, 2)]

    def own(kind, k):
        return half(kind, k, side[kind])

    def part(kind, k, which):
        return grads.at[k, kind, side[kind] * 2 + which]

    def send(stage, kind, k, source, target, peer):
        slot = lax.rem(k, SLOTS)
        return pltpu.make_async_remote_copy(
            source,
            target,
            ssem.at[stage, kind, slot],
            rsem.at[stage, kind, slot],
            device_id=peer,
            device_id_type=MESH,
        )

    def landing(buffer, kind, k):
        return buffer.at[lax.rem(k, SLOTS), kind]

    def scatter_first(kind, k):
        return send(0, kind, k, half(kind, k, 1 - side[kind]), landing(land_a, kind, k), first_peer[kind])

    def go_in(kind, k):
        return send(1, kind, k, own(kind, k), landing(land_z, kind, k), inward)

    def scatter_across(kind, k):
        return send(2, kind, k, part(kind, k, 1 - quarter), landing(land_m, kind, k), across)

    def swap_second(kind, k):
        return send(3, kind, k, part(kind, k, quarter), landing(land_b, kind, k), second_peer[kind])

    def own_out(kind, k):
        return out.at[k, kind, pl.ds(side[kind] * 2, 2)]

    def part_out(kind, k):
        return out.at[k, kind, side[kind] * 2 + quarter]

    def keep(kind, k):
        return pltpu.make_async_copy(
            part(kind, k, quarter), part_out(kind, k), osem.at[kind, lax.rem(k, SLOTS)]
        )

    def gather_across(kind, k):
        return send(4, kind, k, part(kind, k, quarter), part_out(kind, k), across)

    def go_out(kind, k):
        return send(5, kind, k, own_out(kind, k), own_out(kind, k), outward)

    def gather_first(kind, k):
        return send(6, kind, k, own_out(kind, k), own_out(kind, k), first_peer[kind])

    def add(target, arrived):
        total = target[...].astype(jnp.float32) + arrived[...].astype(jnp.float32)
        target[...] = total.astype(jnp.bfloat16)

    def step(t, carry):
        ks = [t - offset for offset in STAGES]
        live = [(k >= 0) & (k < pairs) for k in ks]

        @pl.when(live[7])
        def _():
            for kind in (0, 1):
                gather_first(kind, ks[7]).wait()

        @pl.when(live[6] & inner)
        def _():
            for kind in (0, 1):
                go_out(kind, ks[6]).wait_send()

        @pl.when(live[6] & outer)
        def _():
            for kind in (0, 1):
                go_out(kind, ks[6]).wait_recv()
                gather_first(kind, ks[6]).start()

        @pl.when(live[5] & inner)
        def _():
            for kind in (0, 1):
                gather_across(kind, ks[5]).wait()
                keep(kind, ks[5]).wait()
                go_out(kind, ks[5]).start()
                gather_first(kind, ks[5]).start()

        @pl.when(live[4] & inner)
        def _():
            for kind in (0, 1):
                swap_second(kind, ks[4]).wait()
                add(part(kind, ks[4], quarter), landing(land_b, kind, ks[4]))
                gather_across(kind, ks[4]).start()
                keep(kind, ks[4]).start()

        @pl.when(live[3] & inner)
        def _():
            for kind in (0, 1):
                scatter_across(kind, ks[3]).wait()
                add(part(kind, ks[3], quarter), landing(land_m, kind, ks[3]))
                swap_second(kind, ks[3]).start()

        @pl.when(live[2] & inner)
        def _():
            for kind in (0, 1):
                go_in(kind, ks[2]).wait_recv()
                add(own(kind, ks[2]), landing(land_z, kind, ks[2]))
                scatter_across(kind, ks[2]).start()

        @pl.when(live[2] & outer)
        def _():
            for kind in (0, 1):
                go_in(kind, ks[2]).wait_send()

        @pl.when(live[1])
        def _():
            for kind in (0, 1):
                scatter_first(kind, ks[1]).wait()
                add(own(kind, ks[1]), landing(land_a, kind, ks[1]))

                @pl.when(outer)
                def _():
                    go_in(kind, ks[1]).start()

        @pl.when(live[0])
        def _():
            for kind in (0, 1):
                scatter_first(kind, ks[0]).start()

        return carry

    lax.fori_loop(0, pairs + STAGES[-1], step, 0)


def reduce_grads(packed):
    pairs, _, _, rows, cols = packed.shape
    return pl.pallas_call(
        sum_over_chips,
        out_shape=jax.ShapeDtypeStruct(packed.shape, jnp.bfloat16),
        in_specs=[pl.BlockSpec(memory_space=pltpu.HBM)],
        out_specs=pl.BlockSpec(memory_space=pltpu.HBM),
        scratch_shapes=[
            pltpu.VMEM(packed.shape, jnp.bfloat16),
            pltpu.VMEM((SLOTS, 2, 2, rows, cols), jnp.bfloat16),
            pltpu.VMEM((SLOTS, 2, 2, rows, cols), jnp.bfloat16),
            pltpu.VMEM((SLOTS, 2, rows, cols), jnp.bfloat16),
            pltpu.VMEM((SLOTS, 2, rows, cols), jnp.bfloat16),
            pltpu.SemaphoreType.DMA((7, 2, SLOTS)),
            pltpu.SemaphoreType.DMA((7, 2, SLOTS)),
            pltpu.SemaphoreType.DMA((2, SLOTS)),
            pltpu.SemaphoreType.DMA,
        ],
        name="sum_over_chips",
        compiler_params=pltpu.CompilerParams(
            collective_id=0, has_side_effects=True, vmem_limit_bytes=48 << 20
        ),
    )(packed)


def sum_over_pages(grads, dp_size, mp_size):
    if (dp_size, mp_size) != (16, 2):
        return tuple(lax.psum(g.astype(jnp.bfloat16), "dp").astype(jnp.float32) for g in grads)
    cols, rows = 1024, 16
    flat = jnp.concatenate([g.astype(jnp.bfloat16).reshape(-1) for g in grads])
    unit = 8 * rows * cols
    pairs = -(-flat.size // unit)
    flat = jnp.pad(flat, (0, pairs * unit - flat.size))
    flat = reduce_grads(flat.reshape(pairs, 2, 4, rows, cols)).reshape(-1)
    summed = []
    at = 0
    for g in grads:
        summed.append(flat[at : at + g.size].reshape(g.shape).astype(jnp.float32))
        at += g.size
    return tuple(summed)


def gelu_exact(ffn_inner):
    return jax.nn.gelu(ffn_inner, approximate=False)


def normalize_rows(summed, gain_vec, shift_vec):
    average = jnp.mean(summed, axis=-1, keepdims=True)
    centred = summed - average
    inv_std = lax.rsqrt(jnp.mean(centred * centred, axis=-1, keepdims=True) + eps)
    normed = centred * inv_std
    return (normed * gain_vec + shift_vec, normed, inv_std)


def normalize_back(grad_out, normed, inv_std, gain_vec):
    scaled = grad_out * gain_vec
    centred = scaled - jnp.mean(scaled, axis=-1, keepdims=True)
    return inv_std * (centred - normed * jnp.mean(scaled * normed, axis=-1, keepdims=True))


def on_device(
    dp_size,
    mp_size,
    inputs,
    lengths,
    w_query,
    b_query,
    w_key,
    w_value,
    b_value,
    w_out,
    b_out,
    gain_one,
    shift_one,
    w_in,
    b_in,
    w_back,
    b_back,
    gain_two,
    shift_two,
    cotangent,
):
    token_count, part_cols = inputs.shape
    page_count = lengths.shape[0]
    seq_len = token_count // page_count
    head_size = HDIM
    local_heads = w_query.shape[1] // head_size
    score_scale = head_size ** (-0.5)
    offset = lax.axis_index("mp") * part_cols

    def own_cols(full_array):
        return lax.dynamic_slice_in_dim(full_array, offset, part_cols, full_array.ndim - 1)

    vectors = jnp.stack([b_out, gain_one, shift_one, b_back, gain_two, shift_two])
    token_rows, vector_rows = (
        lax.all_gather(inputs, "mp", axis=1, tiled=True),
        lax.all_gather(vectors, "mp", axis=1, tiled=True),
    )
    vector_rows = vector_rows.astype(jnp.float32)
    full_b_out, full_gain_one, full_shift_one = (vector_rows[0], vector_rows[1], vector_rows[2])
    full_b_back, full_gain_two, full_shift_two = (vector_rows[3], vector_rows[4], vector_rows[5])
    positions = jnp.arange(seq_len, dtype=jnp.int32)
    key_valid = positions[None, :] < lengths[:, None]
    row_valid = key_valid.reshape(token_count, 1).astype(jnp.float32)
    head_shape = (page_count, seq_len, local_heads, head_size)
    queries = (
        (
            jnp.dot(token_rows, w_query, preferred_element_type=jnp.float32)
            + b_query.astype(jnp.float32)
        )
        .astype(jnp.bfloat16)
        .reshape(head_shape)
    )
    keys_all = (
        jnp.dot(token_rows, w_key, preferred_element_type=jnp.float32)
        .astype(jnp.bfloat16)
        .reshape(head_shape)
    )
    values = (
        (
            jnp.dot(token_rows, w_value, preferred_element_type=jnp.float32)
            + b_value.astype(jnp.float32)
        )
        .astype(jnp.bfloat16)
        .reshape(head_shape)
    )

    def masked_scores(page_queries, page_keys, page_valid):
        scores = (
            jnp.einsum("qhd,khd->hqk", page_queries, page_keys, preferred_element_type=jnp.float32)
            * score_scale
        )
        return jnp.where(page_valid[None, None, :], scores, -1e30)

    def attend(packed):
        page_queries, page_keys, page_values, page_valid = packed
        scores = masked_scores(page_queries, page_keys, page_valid)
        row_max = jnp.max(scores, axis=-1, keepdims=True)
        shifted = jnp.exp(scores - row_max)
        row_sum = jnp.sum(shifted, axis=-1, keepdims=True)
        weights = (shifted / row_sum).astype(jnp.bfloat16)
        context = jnp.einsum(
            "hqk,khd->qhd", weights, page_values, preferred_element_type=jnp.float32
        )
        return (context.astype(jnp.bfloat16), (row_max + jnp.log(row_sum))[..., 0])

    context, log_total = lax.map(attend, (queries, keys_all, values, key_valid))
    context = context.reshape(token_count, local_heads * head_size)
    attn_part = jnp.dot(context, w_out, preferred_element_type=jnp.float32)
    attended = token_rows.astype(jnp.float32) + lax.psum(attn_part, "mp") + full_b_out
    hidden_one, normed_one, inv_std_one = normalize_rows(attended, full_gain_one, full_shift_one)
    hidden_low = hidden_one.astype(jnp.bfloat16)
    ffn_inner = jnp.dot(hidden_low, w_in, preferred_element_type=jnp.float32) + b_in.astype(
        jnp.float32
    )
    gelu_value, gelu_pull = jax.vjp(gelu_exact, ffn_inner)
    activated = gelu_value.astype(jnp.bfloat16)
    ffn_part = jnp.dot(activated, w_back, preferred_element_type=jnp.float32)
    summed = hidden_one + lax.psum(ffn_part, "mp") + full_b_back
    out_full, normed_two, inv_std_two = normalize_rows(summed, full_gain_two, full_shift_two)
    output = own_cols(out_full).astype(jnp.bfloat16)
    grad_out = lax.all_gather(cotangent, "mp", axis=1, tiled=True).astype(jnp.float32) * row_valid
    grad_summed = normalize_back(grad_out, normed_two, inv_std_two, full_gain_two)
    grad_gain_two = own_cols(jnp.sum(grad_out * normed_two, axis=0))
    grad_shift_two = own_cols(jnp.sum(grad_out, axis=0))
    grad_b_back = own_cols(jnp.sum(grad_summed, axis=0))
    round_summed = grad_summed.astype(jnp.bfloat16)
    grad_act = jnp.einsum("rd,fd->rf", round_summed, w_back, preferred_element_type=jnp.float32)
    grad_inner = gelu_pull(grad_act)[0].astype(jnp.bfloat16)
    grad_w_back = jnp.einsum(
        "rf,rd->fd", activated, round_summed, preferred_element_type=jnp.float32
    )
    grad_w_in = jnp.einsum("rd,rf->df", hidden_low, grad_inner, preferred_element_type=jnp.float32)
    grad_b_in = jnp.sum(grad_inner.astype(jnp.float32), axis=0)
    ffn_grads = (grad_w_in, grad_b_in, grad_w_back, grad_b_back, grad_gain_two, grad_shift_two)
    back_part = jnp.einsum("rf,df->rd", grad_inner, w_in, preferred_element_type=jnp.float32)
    grad_hidden = lax.psum(back_part, "mp") + grad_summed
    grad_gain_one = own_cols(jnp.sum(grad_hidden * normed_one, axis=0))
    grad_shift_one = own_cols(jnp.sum(grad_hidden, axis=0))
    grad_attended = normalize_back(grad_hidden, normed_one, inv_std_one, full_gain_one)
    grad_b_out = own_cols(jnp.sum(grad_attended, axis=0))
    own_attended = own_cols(grad_attended)
    round_attended = grad_attended.astype(jnp.bfloat16)
    grad_w_out = jnp.einsum(
        "rc,rd->cd", context, round_attended, preferred_element_type=jnp.float32
    )
    grad_context = (
        jnp.einsum("rd,cd->rc", round_attended, w_out, preferred_element_type=jnp.float32)
        .astype(jnp.bfloat16)
        .reshape(head_shape)
    )

    def attend_back(packed):
        page_queries, page_keys, page_values, page_valid, page_total, page_grad = packed
        scores = masked_scores(page_queries, page_keys, page_valid)
        probabilities = jnp.exp(scores - page_total[..., None])
        weights = probabilities.astype(jnp.bfloat16)
        grad_values = jnp.einsum(
            "hqk,qhd->khd", weights, page_grad, preferred_element_type=jnp.float32
        )
        grad_weights = jnp.einsum(
            "qhd,khd->hqk", page_grad, page_values, preferred_element_type=jnp.float32
        )
        grad_scores = (
            probabilities
            * (grad_weights - jnp.sum(probabilities * grad_weights, axis=-1, keepdims=True))
        ).astype(jnp.bfloat16)
        grad_queries = (
            jnp.einsum("hqk,khd->qhd", grad_scores, page_keys, preferred_element_type=jnp.float32)
            * score_scale
        )
        grad_keys = (
            jnp.einsum(
                "hqk,qhd->khd", grad_scores, page_queries, preferred_element_type=jnp.float32
            )
            * score_scale
        )
        return (
            grad_queries.astype(jnp.bfloat16),
            grad_keys.astype(jnp.bfloat16),
            grad_values.astype(jnp.bfloat16),
        )

    grad_queries, grad_keys, grad_values = lax.map(
        attend_back, (queries, keys_all, values, key_valid, log_total, grad_context)
    )
    grad_queries = grad_queries.reshape(token_count, local_heads * head_size)
    grad_keys = grad_keys.reshape(token_count, local_heads * head_size)
    grad_values = grad_values.reshape(token_count, local_heads * head_size)
    grad_w_query = jnp.einsum(
        "rd,rc->dc", token_rows, grad_queries, preferred_element_type=jnp.float32
    )
    grad_w_key = jnp.einsum("rd,rc->dc", token_rows, grad_keys, preferred_element_type=jnp.float32)
    grad_w_value = jnp.einsum(
        "rd,rc->dc", token_rows, grad_values, preferred_element_type=jnp.float32
    )
    grad_b_query = jnp.sum(grad_queries.astype(jnp.float32), axis=0)
    grad_b_value = jnp.sum(grad_values.astype(jnp.float32), axis=0)
    input_part = (
        jnp.einsum("rc,dc->rd", grad_queries, w_query, preferred_element_type=jnp.float32)
        + jnp.einsum("rc,dc->rd", grad_keys, w_key, preferred_element_type=jnp.float32)
        + jnp.einsum("rc,dc->rd", grad_values, w_value, preferred_element_type=jnp.float32)
    )
    input_grad = (
        lax.psum_scatter(
            input_part.astype(jnp.bfloat16), "mp", scatter_dimension=1, tiled=True
        ).astype(jnp.float32)
        + own_attended
    ).astype(jnp.bfloat16)
    all_grads = sum_over_pages(
        (
            grad_w_query,
            grad_b_query,
            grad_w_key,
            grad_w_value,
            grad_b_value,
            grad_w_out,
            grad_b_out,
            grad_gain_one,
            grad_shift_one,
            grad_w_in,
            grad_b_in,
            grad_w_back,
            grad_b_back,
            grad_gain_two,
            grad_shift_two,
        ),
        dp_size,
        mp_size,
    )
    attn_grads = all_grads[:9]
    ffn_grads = all_grads[9:]
    return (
        output,
        input_grad,
        attn_grads[0],
        attn_grads[1],
        attn_grads[2],
        attn_grads[3],
        attn_grads[4],
        attn_grads[5],
        attn_grads[6],
        attn_grads[7],
        attn_grads[8],
        ffn_grads[0],
        ffn_grads[1],
        ffn_grads[2],
        ffn_grads[3],
        ffn_grads[4],
        ffn_grads[5],
    )


def solution(mesh):
    placed = (
        P("dp", "mp"),
        P("dp"),
        P(None, "mp"),
        P("mp"),
        P(None, "mp"),
        P(None, "mp"),
        P("mp"),
        P("mp", None),
        P("mp"),
        P("mp"),
        P("mp"),
        P(None, "mp"),
        P("mp"),
        P("mp", None),
        P("mp"),
        P("mp"),
        P("mp"),
        P("dp", "mp"),
    )
    return jax.shard_map(
        functools.partial(on_device, mesh.shape["dp"], mesh.shape["mp"]),
        mesh=mesh,
        in_specs=placed,
        out_specs=(
            P("dp", "mp"),
            P("dp", "mp"),
            P(None, "mp"),
            P("mp"),
            P(None, "mp"),
            P(None, "mp"),
            P("mp"),
            P("mp", None),
            P("mp"),
            P("mp"),
            P("mp"),
            P(None, "mp"),
            P("mp"),
            P("mp", None),
            P("mp"),
            P("mp"),
            P("mp"),
        ),
        check_vma=False,
    )
```

```python
import functools

import jax
import jax.numpy as jnp
from jax import lax
from jax.experimental import pallas as pl
from jax.experimental.pallas import tpu as pltpu
from jax.sharding import PartitionSpec as P

MESH = pl.DeviceIdType.MESH
HDIM = 64
HALF = 512
eps = 1e-05
QT = 512
RT = 512


def vector_rows(own, oth, nat):
    mp = lax.axis_index("mp")
    nat[:, pl.ds(pl.multiple_of(mp * HALF, HALF), HALF)] = own[...]
    nat[:, pl.ds(pl.multiple_of((1 - mp) * HALF, HALF), HALF)] = oth[...]


def lane_of(rows):
    return lax.broadcasted_iota(jnp.int32, (rows, 128), 1)


def key_lanes(length, rows):
    lane = lane_of(rows) % 64
    slot = lax.broadcasted_iota(jnp.int32, (rows, 128), 0)
    bias = jnp.where(slot < length, 0.0, -1e30)
    return jnp.where(lane < 3, 1.0, jnp.where(lane == 3, bias, 0.0)).astype(jnp.bfloat16)


def attention_kernel(
    inputs, x_other, w_q, w_qo, w_k, w_ko, w_v, w_vo, w_o, w_oo, biases, own, oth, lens,
    x_out, qkv_out, ctx_out, aux_out, hid_out, low_out, normed_out, inv_out,
    xb, w, wo, qkv, ctx, aux, nat, kl, sem, osem,
):
    mp = lax.axis_index("mp")
    tokens = xb.shape[0]
    seq = kl.shape[0]
    pages = tokens // seq

    def fetch(i, src, dst):
        return pltpu.make_async_copy(src, dst, sem.at[i])

    loads = [
        fetch(0, inputs.at[pl.ds(pl.multiple_of(mp * tokens, tokens), tokens)],
              xb.at[:, pl.ds(pl.multiple_of(mp * HALF, HALF), HALF)]),
        fetch(1, x_other, xb.at[:, pl.ds(pl.multiple_of((1 - mp) * HALF, HALF), HALF)]),
    ]
    loads += [fetch(2 + i, src, w.at[i]) for i, src in enumerate((w_q, w_qo, w_k, w_ko, w_v, w_vo))]
    loads += [fetch(8 + i, src, wo.at[i]) for i, src in enumerate((w_o, w_oo))]
    for load in loads:
        load.start()
    vector_rows(own, oth, nat)
    loads[0].wait()
    loads[1].wait()
    pltpu.make_async_copy(xb, x_out, osem.at[0]).start()
    for load in loads[2:8]:
        load.wait()

    def project(i, carry):
        out = jnp.dot(xb[...], w[i], preferred_element_type=jnp.float32)
        qkv[i] = (out + biases[pl.ds(i, 1), :]).astype(jnp.bfloat16)
        return carry

    lax.fori_loop(0, 6, project, 0)
    pltpu.make_async_copy(qkv, qkv_out, osem.at[1]).start()

    lane = lane_of(seq)
    low = lane < 64
    q_one = jnp.where(lane % 64 == 3, 1.0, 0.0).astype(jnp.bfloat16)
    tile = QT

    def page_loop(page, carry):
        kl[...] = key_lanes(lens[mp * pages + page], seq)
        rows = pl.ds(pl.multiple_of(page * seq, seq), seq)

        def pair_loop(pair, carry):
            half = pair // 4
            cols = pl.ds(pl.multiple_of((pair % 4) * 128, 128), 128)
            kp = qkv[2 + half, rows, cols]
            vp = qkv[4 + half, rows, cols]
            qp = qkv[half, rows, cols] * jnp.bfloat16(0.125)
            one = jnp.ones_like(vp)
            keys = (jnp.where(low, kp, kl[...]), jnp.where(low, kl[...], kp))
            vals = (jnp.where(low, vp, one), jnp.where(low, one, vp))
            qs = (jnp.where(low, qp, q_one), jnp.where(low, q_one, qp))
            for r in range(0, seq, tile):
                outs = []
                for h in (0, 1):
                    scores = lax.dot_general(
                        qs[h][r : r + tile], keys[h], (((1,), (1,)), ((), ())),
                        preferred_element_type=jnp.float32,
                    )
                    top = jnp.max(scores, axis=1, keepdims=True)
                    weights = jnp.exp(scores - top).astype(jnp.bfloat16)
                    outs.append((top, jnp.dot(weights, vals[h], preferred_element_type=jnp.float32)))
                low_r = low[r : r + tile]
                lane_r = lane[r : r + tile] % 64
                (top0, out0), (top1, out1) = outs
                total = jnp.where(low_r, out1, out0)
                value = jnp.where(low_r, out0, out1)
                value = value / pltpu.roll(total, 64, 1)
                neg = -(jnp.where(low_r, top1, top0) + jnp.log(total))
                first = neg.astype(jnp.bfloat16)
                rest = neg - first.astype(jnp.float32)
                second = rest.astype(jnp.bfloat16)
                third = (rest - second.astype(jnp.float32)).astype(jnp.bfloat16)
                zero = jnp.zeros_like(first)
                mixed = jnp.where(lane_r == 0, first, jnp.where(lane_r == 1, second, jnp.where(lane_r == 2, third, jnp.where(lane_r == 3, zero + 1, zero))))
                out_rows = pl.ds(pl.multiple_of(page * seq + r, tile), tile)
                ctx[half, out_rows, cols] = value.astype(jnp.bfloat16)
                aux[half, out_rows, cols] = mixed
            return carry

        return lax.fori_loop(0, 8, pair_loop, carry)

    lax.fori_loop(0, pages, page_loop, 0)
    pltpu.make_async_copy(ctx, ctx_out, osem.at[2]).start()
    pltpu.make_async_copy(aux, aux_out, osem.at[3]).start()
    for load in loads[8:]:
        load.wait()
    step = 256

    def finish(i, carry):
        rows = pl.ds(pl.multiple_of(i * step, step), step)
        attended = (
            xb[rows, :].astype(jnp.float32)
            + jnp.dot(ctx[0, rows, :], wo[0], preferred_element_type=jnp.float32)
            + jnp.dot(ctx[1, rows, :], wo[1], preferred_element_type=jnp.float32)
            + nat[6:7, :]
        )
        average = jnp.mean(attended, axis=1, keepdims=True)
        centred = attended - average
        inv = lax.rsqrt(jnp.mean(centred * centred, axis=1, keepdims=True) + eps)
        normed = centred * inv
        hidden = normed * nat[7:8, :] + nat[8:9, :]
        hid_out[rows, :] = hidden
        low_out[rows, :] = hidden.astype(jnp.bfloat16)
        normed_out[rows, :] = normed.astype(jnp.bfloat16)
        inv_out[rows, :] = jnp.broadcast_to(inv, (step, 128))
        return carry

    lax.fori_loop(0, tokens // step, finish, 0)
    pltpu.make_async_copy(xb, x_out, osem.at[0]).wait()
    pltpu.make_async_copy(qkv, qkv_out, osem.at[1]).wait()
    pltpu.make_async_copy(ctx, ctx_out, osem.at[2]).wait()
    pltpu.make_async_copy(aux, aux_out, osem.at[3]).wait()


HBM = pl.BlockSpec(memory_space=pltpu.HBM)
VMEM = pl.BlockSpec(memory_space=pltpu.VMEM)
SMEM = pl.BlockSpec(memory_space=pltpu.SMEM)


def shape(dims, dtype=jnp.bfloat16):
    return jax.ShapeDtypeStruct(dims, dtype)


def run_attention(inputs, x_other, weights, biases, own, oth, lengths, seq):
    tokens, half = x_other.shape
    full = 2 * half
    f32 = jnp.float32
    return pl.pallas_call(
        attention_kernel,
        name="attention_block",
        out_shape=(
            shape((tokens, full)), shape((6, tokens, half)), shape((2, tokens, half)), shape((2, tokens, half)),
            shape((tokens, full), f32), shape((tokens, full)), shape((tokens, full)), shape((tokens, 128), f32),
        ),
        in_specs=[HBM] * 10 + [VMEM] * 3 + [SMEM],
        out_specs=(HBM,) * 4 + (VMEM,) * 4,
        scratch_shapes=[
            pltpu.VMEM((tokens, full), jnp.bfloat16),
            pltpu.VMEM((6, full, half), jnp.bfloat16),
            pltpu.VMEM((2, half, full), jnp.bfloat16),
            pltpu.VMEM((6, tokens, half), jnp.bfloat16),
            pltpu.VMEM((2, tokens, half), jnp.bfloat16),
            pltpu.VMEM((2, tokens, half), jnp.bfloat16),
            pltpu.VMEM((12, full), f32),
            pltpu.VMEM((seq, 128), jnp.bfloat16),
            pltpu.SemaphoreType.DMA((10,)),
            pltpu.SemaphoreType.DMA((4,)),
        ],
        compiler_params=pltpu.CompilerParams(vmem_limit_bytes=56 << 20),
        cost_estimate=pl.CostEstimate(flops=17 << 30, bytes_accessed=30 << 20, transcendentals=8 << 20),
    )(inputs, x_other, *weights, biases, own, oth, lengths)


def gelu_and_slope(v):
    size = jnp.abs(v)
    t = 1.0 / (1.0 + (0.3275911 * 0.7071067811865476) * size)
    bell = jnp.exp(-0.5 * v * v)
    poly = ((((0.5 * 1.061405429) * t - 0.5 * 1.453152027) * t + 0.5 * 1.421413741) * t - 0.5 * 0.284496736) * t + 0.5 * 0.254829592
    tail = poly * t * bell
    cdf = jnp.where(v < 0, tail, 1.0 - tail)
    return v * cdf, cdf + v * (bell * 0.3989422804014327)


def ffn_kernel(
    low, hid_in, w_in, w_ino, w_back, w_backo, bias, own, oth, cot, cot_other, lens,
    act_out, slope_out, out_own, out_other, round_out, grad_out, sums_out,
    wi, wb, act, slope, acc, nat, cotb, isem, osem, csem, hsem,
):
    mp = lax.axis_index("mp")
    tokens = low.shape[0]
    tiles = act_out.shape[0]
    part = act_out.shape[2] // 2
    step = 256

    def loads(j):
        slot = lax.rem(j, 2)
        at = pl.ds(pl.multiple_of(j * part, part), part)
        return (
            pltpu.make_async_copy(w_in.at[:, at], wi.at[slot, :, pl.ds(0, part)], isem.at[slot, 0]),
            pltpu.make_async_copy(w_ino.at[:, at], wi.at[slot, :, pl.ds(part, part)], isem.at[slot, 1]),
            pltpu.make_async_copy(w_back.at[at], wb.at[slot, pl.ds(0, part)], isem.at[slot, 2]),
            pltpu.make_async_copy(w_backo.at[at], wb.at[slot, pl.ds(part, part)], isem.at[slot, 3]),
        )

    def stores(j):
        slot = lax.rem(j, 2)
        return (
            pltpu.make_async_copy(act.at[slot], act_out.at[j], osem.at[slot, 0]),
            pltpu.make_async_copy(slope.at[slot], slope_out.at[j], osem.at[slot, 1]),
        )

    for load in loads(0):
        load.start()
    fetch_hid = pltpu.make_async_copy(hid_in, acc, hsem)
    fetch_hid.start()
    own_cols = pl.ds(pl.multiple_of(mp * HALF, HALF), HALF)
    other_cols = pl.ds(pl.multiple_of((1 - mp) * HALF, HALF), HALF)
    cot_loads = (
        pltpu.make_async_copy(
            cot.at[pl.ds(pl.multiple_of(mp * tokens, tokens), tokens)], cotb.at[:, own_cols], csem.at[0]
        ),
        pltpu.make_async_copy(cot_other, cotb.at[:, other_cols], csem.at[1]),
    )
    for load in cot_loads:
        load.start()
    vector_rows(own, oth, nat)

    fetch_hid.wait()

    def tile_loop(j, carry):
        slot = lax.rem(j, 2)
        for load in loads(j):
            load.wait()

        @pl.when(j + 1 < tiles)
        def _():
            for load in loads(j + 1):
                load.start()

        @pl.when(j >= 2)
        def _():
            for store in stores(j - 2):
                store.wait()

        row_bias = bias[pl.ds(j, 1), :]
        for r in range(0, tokens, RT):
            rows = pl.ds(r, RT)
            inner = jnp.dot(low[rows, :], wi[slot], preferred_element_type=jnp.float32) + row_bias
            value, grad = gelu_and_slope(inner)
            value = value.astype(jnp.bfloat16)
            act[slot, rows, :] = value
            slope[slot, rows, :] = grad.astype(jnp.bfloat16)
            acc[rows, :] += jnp.dot(value, wb[slot], preferred_element_type=jnp.float32)
        for store in stores(j):
            store.start()
        return carry

    lax.fori_loop(0, tiles, tile_loop, 0)
    for load in cot_loads:
        load.wait()
    seq = tokens * 2 // lens.shape[0]

    def finish(i, sums):
        at = pl.multiple_of(i * step, step)
        rows = pl.ds(at, step)
        summed = acc[rows, :] + nat[9:10, :]
        average = jnp.mean(summed, axis=1, keepdims=True)
        centred = summed - average
        inv = lax.rsqrt(jnp.mean(centred * centred, axis=1, keepdims=True) + eps)
        normed = centred * inv
        out_full = (normed * nat[10:11, :] + nat[11:12, :]).astype(jnp.bfloat16)
        acc[rows, :] = out_full.astype(jnp.float32)
        out_own[rows, :] = acc[rows, own_cols].astype(jnp.bfloat16)
        out_other[rows, :] = acc[rows, other_cols].astype(jnp.bfloat16)
        page = (i * step) // seq
        slots = lax.broadcasted_iota(jnp.int32, (step, 1), 0) + (i * step) % seq
        valid = jnp.where(slots < lens[mp * (tokens // seq) + page], 1.0, 0.0)
        grad = cotb[rows, :].astype(jnp.float32) * valid
        scaled = grad * nat[10:11, :]
        mean_one = jnp.mean(scaled, axis=1, keepdims=True)
        mean_two = jnp.mean(scaled * normed, axis=1, keepdims=True)
        back = inv * (scaled - mean_one - normed * mean_two)
        grad_out[rows, :] = back
        round_out[rows, :] = back.astype(jnp.bfloat16)
        return (
            sums[0] + jnp.sum(back, axis=0, keepdims=True),
            sums[1] + jnp.sum(grad * normed, axis=0, keepdims=True),
            sums[2] + jnp.sum(grad, axis=0, keepdims=True),
        )

    zero = jnp.zeros((1, 2 * HALF), jnp.float32)
    sums = lax.fori_loop(0, tokens // step, finish, (zero, zero, zero))
    for i, row in enumerate(sums):
        sums_out[i : i + 1, :] = row
    for j in (tiles - 2, tiles - 1):
        for store in stores(j):
            store.wait()


def run_ffn(low, hid, w_in, w_ino, w_back, w_backo, bias, own, oth, cot, cot_other, lengths):
    tokens, full = low.shape
    tiles, wide = bias.shape
    f32 = jnp.float32
    half = full // 2
    return pl.pallas_call(
        ffn_kernel,
        name="ffn_block",
        out_shape=(
            shape((tiles, tokens, wide)), shape((tiles, tokens, wide)), shape((tokens, half)), shape((tokens, half)),
            shape((tokens, full)), shape((tokens, full), f32), shape((8, full), f32),
        ),
        in_specs=[VMEM] + [HBM] * 5 + [VMEM] * 3 + [HBM] * 2 + [SMEM],
        out_specs=(HBM,) * 2 + (VMEM,) * 5,
        scratch_shapes=[
            pltpu.VMEM((2, full, wide), jnp.bfloat16),
            pltpu.VMEM((2, wide, full), jnp.bfloat16),
            pltpu.VMEM((2, tokens, wide), jnp.bfloat16),
            pltpu.VMEM((2, tokens, wide), jnp.bfloat16),
            pltpu.VMEM((tokens, full), f32),
            pltpu.VMEM((12, full), f32),
            pltpu.VMEM((tokens, full), jnp.bfloat16),
            pltpu.SemaphoreType.DMA((2, 4)),
            pltpu.SemaphoreType.DMA((2, 2)),
            pltpu.SemaphoreType.DMA((2,)),
            pltpu.SemaphoreType.DMA,
        ],
        compiler_params=pltpu.CompilerParams(vmem_limit_bytes=56 << 20),
        cost_estimate=pl.CostEstimate(flops=17 << 30, bytes_accessed=50 << 20, transcendentals=8 << 20),
    )(low, hid, w_in, w_ino, w_back, w_backo, bias, own, oth, cot, cot_other, lengths)


QUARTER = 16
CHUNK = 4 * QUARTER
PAIR = 2 * CHUNK
BLOCK = 4 * PAIR
SLOTS = 16
STAGES = (0, 2, 4, 6, 8, 10, 12, 14)


def rows_at(start, size):
    return pl.ds(pl.multiple_of(start, QUARTER), size)


def chip_sum(pairs, grads, out, land_a, land_z, land_m, land_b, ssem, rsem, osem):
    dp = lax.axis_index("dp")
    mp = lax.axis_index("mp")
    z, y, x = dp // 4, (dp // 2) % 2, dp % 2
    inner = (z == 1) | (z == 2)
    outer = jnp.logical_not(inner)
    quarter = jnp.where(z == 1, 0, 1)

    def chip(cz, cy, cx):
        return (cz * 4 + cy * 2 + cx, mp)

    first_peer = (chip(z, y, 1 - x), chip(z, 1 - y, x))
    second_peer = (chip(z, 1 - y, x), chip(z, y, 1 - x))
    side = (x, y)
    inward = chip(jnp.where(z == 0, 1, 2), y, x)
    outward = chip(jnp.where(z == 1, 0, 3), y, x)
    across = chip(3 - z, y, x)
    twin = (dp, 1 - mp)

    def meet():
        barrier = pltpu.get_barrier_semaphore()
        for peer in first_peer + (twin,):
            pl.semaphore_signal(barrier, 1, device_id=peer, device_id_type=MESH)

        @pl.when(inner)
        def _():
            for peer in (outward, across):
                pl.semaphore_signal(barrier, 1, device_id=peer, device_id_type=MESH)
            pl.semaphore_wait(barrier, 5)

        @pl.when(outer)
        def _():
            pl.semaphore_signal(barrier, 1, device_id=inward, device_id_type=MESH)
            pl.semaphore_wait(barrier, 4)

    def half(ref, kind, k, which):
        return ref.at[rows_at(k * PAIR + kind * CHUNK + which * 2 * QUARTER, 2 * QUARTER)]

    def own(kind, k):
        return half(grads, kind, k, side[kind])

    def own_out(kind, k):
        return half(out, kind, k, side[kind])

    def part_of(ref, kind, k, which):
        return ref.at[rows_at(k * PAIR + kind * CHUNK + (side[kind] * 2 + which) * QUARTER, QUARTER)]

    def part(kind, k, which):
        return part_of(grads, kind, k, which)

    def keep(kind, k):
        return pltpu.make_async_copy(
            part(kind, k, quarter), part_of(out, kind, k, quarter), osem.at[kind, lax.rem(k, SLOTS)]
        )

    def send(stage, kind, k, source, target, peer):
        slot = lax.rem(k, SLOTS)
        return pltpu.make_async_remote_copy(
            source,
            target,
            ssem.at[stage, kind, slot],
            rsem.at[stage, kind, slot],
            device_id=peer,
            device_id_type=MESH,
        )

    def landing(buffer, kind, k):
        return buffer.at[lax.rem(k, SLOTS), kind]

    def scatter_first(kind, k):
        return send(0, kind, k, half(grads, kind, k, 1 - side[kind]), landing(land_a, kind, k), first_peer[kind])

    def go_in(kind, k):
        return send(1, kind, k, own(kind, k), landing(land_z, kind, k), inward)

    def scatter_across(kind, k):
        return send(2, kind, k, part(kind, k, 1 - quarter), landing(land_m, kind, k), across)

    def swap_second(kind, k):
        return send(3, kind, k, part(kind, k, quarter), landing(land_b, kind, k), second_peer[kind])

    def gather_across(kind, k):
        return send(4, kind, k, part(kind, k, quarter), part_of(out, kind, k, quarter), across)

    def go_out(kind, k):
        return send(5, kind, k, own_out(kind, k), own_out(kind, k), outward)

    def gather_first(kind, k):
        return send(6, kind, k, own_out(kind, k), own_out(kind, k), first_peer[kind])

    def step(t):
        ks = [t - offset for offset in STAGES]
        live = [(k >= 0) & (k < pairs) for k in ks]

        @pl.when(live[7])
        def _():
            for kind in (0, 1):
                gather_first(kind, ks[7]).wait()

        @pl.when(live[6] & inner)
        def _():
            for kind in (0, 1):
                go_out(kind, ks[6]).wait_send()

        @pl.when(live[6] & outer)
        def _():
            for kind in (0, 1):
                go_out(kind, ks[6]).wait_recv()
                gather_first(kind, ks[6]).start()

        @pl.when(live[5] & inner)
        def _():
            for kind in (0, 1):
                gather_across(kind, ks[5]).wait()
                keep(kind, ks[5]).wait()
                go_out(kind, ks[5]).start()
                gather_first(kind, ks[5]).start()

        @pl.when(live[4] & inner)
        def _():
            for kind in (0, 1):
                swap_second(kind, ks[4]).wait()
                add_into(part(kind, ks[4], quarter), landing(land_b, kind, ks[4]))
                gather_across(kind, ks[4]).start()
                keep(kind, ks[4]).start()

        @pl.when(live[3] & inner)
        def _():
            for kind in (0, 1):
                scatter_across(kind, ks[3]).wait()
                add_into(part(kind, ks[3], quarter), landing(land_m, kind, ks[3]))
                swap_second(kind, ks[3]).start()

        @pl.when(live[2] & inner)
        def _():
            for kind in (0, 1):
                go_in(kind, ks[2]).wait_recv()
                add_into(own(kind, ks[2]), landing(land_z, kind, ks[2]))
                scatter_across(kind, ks[2]).start()

        @pl.when(live[2] & outer)
        def _():
            for kind in (0, 1):
                go_in(kind, ks[2]).wait_send()

        @pl.when(live[1])
        def _():
            for kind in (0, 1):
                scatter_first(kind, ks[1]).wait()
                add_into(own(kind, ks[1]), landing(land_a, kind, ks[1]))

                @pl.when(outer)
                def _():
                    go_in(kind, ks[1]).start()

        @pl.when(live[0])
        def _():
            for kind in (0, 1):
                scatter_first(kind, ks[0]).start()

    return meet, step


def add_into(target, arrived):
    total = target[...].astype(jnp.float32) + arrived[...].astype(jnp.float32)
    target[...] = total.astype(jnp.bfloat16)


def dot_tn(left, right):
    return lax.dot_general(left, right, (((0,), (0,)), ((), ())), preferred_element_type=jnp.float32)


def dot_nt(left, right):
    return lax.dot_general(left, right, (((1,), (1,)), ((), ())), preferred_element_type=jnp.float32)


def backward_kernel(
    act_in, slope_in, round_in, grad_in, low_in, w_in, w_ino, w_back, w_backo, normed_in, inv, own_vec, oth_vec,
    sums_in, x_in, qkv_in, ctx_in, aux_in, w_q, w_qo, w_k, w_ko, w_v, w_vo, w_o, w_oo, lens,
    out, ig_own, ig_recv,
    grads, land_a, land_z, land_m, land_b, send_t, land_t, send_v, land_v, acc, buf_a, buf_b, buf_c, buf_d, buf_e,
    buf_f, inner_g, qkv, xb, nat, bias_in, kl,
    ssem, rsem, osem, tsem, trsem, vsem, vrsem, isem, lsem, gsem,
):
    dp = lax.axis_index("dp")
    mp = lax.axis_index("mp")
    tokens, full = buf_a.shape
    half = full // 2
    tiles = act_in.shape[0]
    wide = act_in.shape[2]
    part = wide // 2
    pairs = grads.shape[0] // PAIR
    last_rows = (pairs - 1) * PAIR
    meet, tick = chip_sum(pairs, grads, out, land_a, land_z, land_m, land_b, ssem, rsem, osem)
    own_cols = pl.ds(pl.multiple_of(mp * half, half), half)
    other_cols = pl.ds(pl.multiple_of((1 - mp) * half, half), half)
    twin = (dp, 1 - mp)

    def tile_loads(j):
        slot = lax.rem(j, 2)
        at = pl.ds(pl.multiple_of(j * part, part), part)
        copies = (
            (act_in.at[j], buf_c.at[slot]),
            (slope_in.at[j], buf_d.at[slot]),
            (w_in.at[:, at], buf_e.at[slot, :, pl.ds(0, part)]),
            (w_ino.at[:, at], buf_e.at[slot, :, pl.ds(part, part)]),
            (w_back.at[at], buf_f.at[slot, pl.ds(0, part)]),
            (w_backo.at[at], buf_f.at[slot, pl.ds(part, part)]),
        )
        return [pltpu.make_async_copy(src, dst, isem.at[slot, i]) for i, (src, dst) in enumerate(copies)]

    def load(i, src, dst):
        return pltpu.make_async_copy(src, dst, lsem.at[i])

    first = [load(0, round_in, buf_a), load(1, low_in, buf_b), load(2, grad_in, acc)]
    later = [load(3, qkv_in, qkv), load(4, x_in, xb)]
    for copy in first[:1] + tile_loads(0) + first[1:] + later:
        copy.start()
    vector_rows(own_vec, oth_vec, nat)
    grads[last_rows : last_rows + PAIR, :] = jnp.zeros((PAIR, full), jnp.bfloat16)
    meet()
    for copy in first:
        copy.wait()

    def to_twin(b):
        slot = lax.rem(b, 2)
        return pltpu.make_async_remote_copy(
            send_t.at[slot], land_t.at[slot], tsem.at[slot], trsem.at[slot], device_id=twin, device_id_type=MESH
        )

    def take_twin(b):
        to_twin(b).wait_recv()
        slot = lax.rem(b, 2)

        def piece(i, carry):
            add_into(grads.at[rows_at(b * BLOCK + i * CHUNK, CHUNK)], land_t.at[slot, rows_at(i * CHUNK, CHUNK)])
            return carry

        lax.fori_loop(0, BLOCK // CHUNK, piece, 0)

    def tile_loop(j, carry):
        slot = lax.rem(j, 2)
        for copy in tile_loads(j):
            copy.wait()

        @pl.when(j + 1 < tiles)
        def _():
            for copy in tile_loads(j + 1):
                copy.start()

        @pl.when(j >= 2)
        def _():
            to_twin(j - 2).wait_send()

        base = j * BLOCK
        for c in range(0, full, half):
            made = dot_tn(buf_c[slot], buf_a[:, c : c + half]).astype(jnp.bfloat16)
            grads[rows_at(base, part), c : c + half] = made[:part]
            send_t[slot, :part, c : c + half] = made[part:]

        @pl.when(j >= 1)
        def _():
            take_twin(j - 1)
            tick(2 * j - 2)

        total = jnp.zeros((1, wide), jnp.float32)
        for r in range(0, tokens, half):
            rows = pl.ds(r, half)
            made = dot_nt(buf_a[rows, :], buf_f[slot]) * buf_d[slot, rows, :].astype(jnp.float32)
            made = made.astype(jnp.bfloat16)
            inner_g[rows, :] = made
            total = total + jnp.sum(made.astype(jnp.float32), axis=0, keepdims=True)
            acc[rows, :] += dot_nt(made, buf_e[slot])
        bias_in[pl.ds(j, 1), :] = total
        for c in range(0, full, part):
            made = dot_tn(buf_b[:, c : c + part], inner_g[...]).astype(jnp.bfloat16)
            grads[rows_at(base + part, part), c : c + part] = made[:, :part]
            send_t[slot, part:, c : c + part] = made[:, part:]

        to_twin(j).start()

        @pl.when(j >= 1)
        def _():
            tick(2 * j - 1)

        return carry

    lax.fori_loop(0, tiles, tile_loop, 0)
    t = 2 * tiles - 2

    second = [
        load(5, normed_in, buf_b),
        load(6, aux_in, buf_c),
        load(7, ctx_in, buf_d),
        load(8, w_o, buf_f.at[0]),
        load(9, w_oo, buf_f.at[1]),
    ]
    for copy in second:
        copy.start()
    second[0].wait()
    step = 256

    def norm_back(i, sums):
        rows = pl.ds(pl.multiple_of(i * step, step), step)
        grad = acc[rows, :]
        normed = buf_b[rows, :].astype(jnp.float32)
        scaled = grad * nat[7:8, :]
        mean_one = jnp.mean(scaled, axis=1, keepdims=True)
        mean_two = jnp.mean(scaled * normed, axis=1, keepdims=True)
        back = inv[rows, 0:1] * (scaled - mean_one - normed * mean_two)
        acc[rows, :] = back
        buf_a[rows, :] = back.astype(jnp.bfloat16)
        return (
            sums[0] + jnp.sum(back, axis=0, keepdims=True),
            sums[1] + jnp.sum(grad * normed, axis=0, keepdims=True),
            sums[2] + jnp.sum(grad, axis=0, keepdims=True),
        )

    zero = jnp.zeros((1, full), jnp.float32)
    bias_o, gain_one, shift_one = lax.fori_loop(0, tokens // step, norm_back, (zero, zero, zero))
    tick(t)

    b = tiles
    to_twin(b - 2).wait_send()
    for copy in second[1:]:
        copy.wait()
    for h in (0, 1):
        for c in range(0, full, half):
            made = dot_tn(buf_d[h], buf_a[:, c : c + half]).astype(jnp.bfloat16)
            if h == 0:
                grads[b * BLOCK : b * BLOCK + half, c : c + half] = made
            else:
                send_t[b % 2, :, c : c + half] = made
    take_twin(b - 1)
    to_twin(b).start()
    tick(t + 1)
    for h in (0, 1):
        for r in range(0, tokens, half):
            buf_e[h, r : r + half, :] = dot_nt(buf_a[r : r + half, :], buf_f[h]).astype(jnp.bfloat16)
    take_twin(b)
    tick(t + 2)
    t = t + 3
    for copy in later:
        copy.wait()

    seq = kl.shape[0]
    pages = tokens // seq
    lane = lane_of(seq)
    low_lanes = lane < 64

    def pair_loop(i, carry):
        page, pair = i // 8, lax.rem(i, 8)

        @pl.when(pair == 0)
        def _():
            kl[...] = key_lanes(lens[mp * pages + page], seq)

        side = pair // 4
        rows = pl.ds(pl.multiple_of(page * seq, seq), seq)
        cols = pl.ds(pl.multiple_of(lax.rem(pair, 4) * 128, 128), 128)
        qp = qkv[side, rows, cols] * jnp.bfloat16(0.125)
        kp = qkv[2 + side, rows, cols]
        vp = qkv[4 + side, rows, cols]
        extra = buf_c[side, rows, cols]
        gp = buf_e[side, rows, cols]
        cp = buf_d[side, rows, cols]
        zero = jnp.zeros_like(gp)
        made = []
        for h in (0, 1):
            mine = low_lanes if h == 0 else jnp.logical_not(low_lanes)
            scores = dot_nt(jnp.where(mine, qp, extra), jnp.where(mine, kp, kl[...]))
            probs = jnp.exp(scores)
            gh = jnp.where(mine, gp, zero)
            grad_weights = dot_nt(gh, vp)
            delta = jnp.sum(gh.astype(jnp.float32) * cp.astype(jnp.float32), axis=1, keepdims=True)
            grad_scores = (probs * (grad_weights - delta)).astype(jnp.bfloat16)
            grad_v = dot_tn(probs.astype(jnp.bfloat16), gh)
            grad_q = jnp.dot(grad_scores, jnp.where(mine, kp, zero), preferred_element_type=jnp.float32)
            grad_k = dot_tn(grad_scores, jnp.where(mine, qp, zero))
            made.append((grad_q * 0.125, grad_k, grad_v))
        for n in range(3):
            qkv[2 * n + side, rows, cols] = (made[0][n] + made[1][n]).astype(jnp.bfloat16)
        tick(t + i)
        return carry

    lax.fori_loop(0, 8 * pages, pair_loop, 0)
    t = t + 8 * pages

    third = [
        load(10 + i, src, dst)
        for i, (src, dst) in enumerate(
            zip(
                (w_q, w_qo, w_k, w_ko, w_v, w_vo),
                (buf_c.at[0], buf_c.at[1], buf_d.at[0], buf_d.at[1], buf_e.at[0], buf_e.at[1]),
            )
        )
    ]
    for copy in third:
        copy.start()
    b = tiles + 1

    def weights_loop(i, carry):
        at = b + i
        slot = lax.rem(at, 2)
        to_twin(at - 2).wait_send()
        for r in range(0, full, half):
            made = dot_tn(xb[:, r : r + half], qkv[2 * i]).astype(jnp.bfloat16)
            grads[rows_at(at * BLOCK, BLOCK), r : r + half] = made
            made = dot_tn(xb[:, r : r + half], qkv[2 * i + 1]).astype(jnp.bfloat16)
            send_t[slot, :, r : r + half] = made

        @pl.when(i >= 1)
        def _():
            take_twin(at - 1)

        to_twin(at).start()
        tick(t + i)
        return carry

    lax.fori_loop(0, 3, weights_loop, 0)
    t = t + 3
    b = b + 3

    def sum_rows(n):
        total = jnp.sum(qkv[n].astype(jnp.float32), axis=0, keepdims=True)
        return total

    mine = mp == 0
    owned, others = [], []
    for n in (0, 4):
        owned.append(sum_rows(n))
        others.append(sum_rows(n + 1))
    for row in (bias_o, gain_one, shift_one, sums_in[0:1, :], sums_in[1:2, :], sums_in[2:3, :]):
        owned.append(jnp.where(mine, row[:, :half], row[:, half:]))
        others.append(jnp.where(mine, row[:, half:], row[:, :half]))
    for n in range(0, tiles, 2):
        owned.append(jnp.concatenate([bias_in[n : n + 1, :part], bias_in[n + 1 : n + 2, :part]], axis=1))
        others.append(jnp.concatenate([bias_in[n : n + 1, part:], bias_in[n + 1 : n + 2, part:]], axis=1))
    fill = jnp.zeros((QUARTER - len(owned), half), jnp.float32)
    grads[last_rows : last_rows + QUARTER, :half] = jnp.concatenate(owned + [fill], axis=0).astype(jnp.bfloat16)
    send_v[...] = jnp.concatenate(others + [fill], axis=0).astype(jnp.bfloat16)
    vectors = pltpu.make_async_remote_copy(send_v, land_v, vsem, vrsem, device_id=twin, device_id_type=MESH)
    vectors.start()
    take_twin(b - 1)
    vectors.wait()
    add_into(grads.at[last_rows : last_rows + QUARTER, :half], land_v)
    to_twin(b - 2).wait_send()
    to_twin(b - 1).wait_send()
    tick(t)
    for copy in third:
        copy.wait()

    def input_loop(i, carry):
        rows = pl.ds(pl.multiple_of(i * step, step), step)
        total = acc[rows, :]
        for n, ref in enumerate((buf_c, buf_d, buf_e)):
            for h in (0, 1):
                total = total + dot_nt(qkv[2 * n + h, rows, :], ref[h])
        buf_a[rows, :] = total.astype(jnp.bfloat16)
        tick(t + 1 + i)
        return carry

    lax.fori_loop(0, tokens // step, input_loop, 0)
    t = t + 1 + tokens // step
    ig_keep = pltpu.make_async_copy(buf_a.at[:, own_cols], ig_own, gsem.at[0])
    ig_send = pltpu.make_async_remote_copy(
        buf_a.at[:, other_cols], ig_recv, gsem.at[1], gsem.at[2], device_id=twin, device_id_type=MESH
    )
    ig_keep.start()
    ig_send.start()

    def rest(i, carry):
        tick(i)
        return carry

    lax.fori_loop(t, pairs + STAGES[-1], rest, 0)
    ig_keep.wait()
    ig_send.wait()


def run_backward(
    act, slope, rounded, grad_summed, low, w_in, w_ino, w_back, w_backo, normed, inv, own, oth, sums, x, qkv, ctx, aux,
    weights, lengths, seq,
):
    tokens, full = low.shape
    half = full // 2
    tiles, _, wide = act.shape
    rows = (tiles + 4) * BLOCK + PAIR
    f32 = jnp.float32
    bf16 = jnp.bfloat16
    return pl.pallas_call(
        backward_kernel,
        name="backward_and_sum",
        out_shape=(shape((rows, full)), shape((tokens, half)), shape((tokens, half))),
        in_specs=[HBM] * 10 + [VMEM] * 4 + [HBM] * 12 + [SMEM],
        out_specs=(HBM,) * 3,
        scratch_shapes=[
            pltpu.VMEM((rows, full), bf16),
            pltpu.VMEM((SLOTS, 2, 2 * QUARTER, full), bf16),
            pltpu.VMEM((SLOTS, 2, 2 * QUARTER, full), bf16),
            pltpu.VMEM((SLOTS, 2, QUARTER, full), bf16),
            pltpu.VMEM((SLOTS, 2, QUARTER, full), bf16),
            pltpu.VMEM((2, BLOCK, full), bf16),
            pltpu.VMEM((2, BLOCK, full), bf16),
            pltpu.VMEM((QUARTER, half), bf16),
            pltpu.VMEM((QUARTER, half), bf16),
            pltpu.VMEM((tokens, full), f32),
            pltpu.VMEM((tokens, full), bf16),
            pltpu.VMEM((tokens, full), bf16),
            pltpu.VMEM((2, tokens, half), bf16),
            pltpu.VMEM((2, tokens, half), bf16),
            pltpu.VMEM((2, tokens, half), bf16),
            pltpu.VMEM((2, half, full), bf16),
            pltpu.VMEM((tokens, wide), bf16),
            pltpu.VMEM((6, tokens, half), bf16),
            pltpu.VMEM((tokens, full), bf16),
            pltpu.VMEM((12, full), f32),
            pltpu.VMEM((tiles, wide), f32),
            pltpu.VMEM((seq, 128), bf16),
            pltpu.SemaphoreType.DMA((7, 2, SLOTS)),
            pltpu.SemaphoreType.DMA((7, 2, SLOTS)),
            pltpu.SemaphoreType.DMA((2, SLOTS)),
            pltpu.SemaphoreType.DMA((2,)),
            pltpu.SemaphoreType.DMA((2,)),
            pltpu.SemaphoreType.DMA,
            pltpu.SemaphoreType.DMA,
            pltpu.SemaphoreType.DMA((2, 6)),
            pltpu.SemaphoreType.DMA((16,)),
            pltpu.SemaphoreType.DMA((3,)),
        ],
        compiler_params=pltpu.CompilerParams(
            collective_id=0, has_side_effects=True, vmem_limit_bytes=60 << 20
        ),
        cost_estimate=pl.CostEstimate(flops=60 << 30, bytes_accessed=80 << 20, transcendentals=8 << 20),
    )(
        act, slope, rounded, grad_summed, low, w_in, w_ino, w_back, w_backo, normed, inv, own, oth, sums, x, qkv, ctx,
        aux, *weights, lengths,
    )


def unpack_kernel(
    packed, out_mine, out_got, ig_mine, ig_got,
    output, input_grad, g_q, g_k, g_v, g_o, g_in, g_back,
    loaded, wide, isem, osem, csem,
):
    mp = lax.axis_index("mp")
    tokens, half = out_mine.shape
    mine = pl.ds(pl.multiple_of(mp * tokens, tokens), tokens)
    other = pl.ds(pl.multiple_of((1 - mp) * tokens, tokens), tokens)
    moves = [
        pltpu.make_async_copy(src, dst, csem.at[i])
        for i, (src, dst) in enumerate(
            (
                (out_mine, output.at[mine]),
                (out_got, output.at[other]),
                (ig_mine, input_grad.at[mine]),
                (ig_got, input_grad.at[other]),
            )
        )
    ]
    for move in moves:
        move.start()
    part = BLOCK // 2
    full = packed.shape[1]
    tiles = g_back.shape[0] // part
    blocks = tiles + 4

    def fetch(b):
        return pltpu.make_async_copy(packed.at[b * BLOCK : (b + 1) * BLOCK], loaded.at[b % 2], isem.at[b % 2])

    def stores(b):
        ref = wide.at[b % 2]
        if b < tiles:
            pieces = [(ref.at[:part], g_back.at[b * part : (b + 1) * part])]
            for c in range(0, full, part):
                pieces.append((ref.at[part:, c : c + part], g_in.at[c : c + part, b * part : (b + 1) * part]))
        elif b == tiles:
            pieces = [(ref, g_o)]
        else:
            target = (g_q, g_k, g_v)[b - tiles - 1]
            pieces = [(ref.at[:, :half], target.at[:half]), (ref.at[:, half:], target.at[half:])]
        return [pltpu.make_async_copy(src, dst, osem.at[b % 2, i]) for i, (src, dst) in enumerate(pieces)]

    fetch(0).start()
    for b in range(blocks):
        if b + 1 < blocks:
            fetch(b + 1).start()
        fetch(b).wait()
        if b >= 2:
            for store in stores(b - 2):
                store.wait()
        for r in range(0, BLOCK, CHUNK):
            wide[b % 2, r : r + CHUNK, :] = loaded[b % 2, r : r + CHUNK, :].astype(jnp.float32)
        for store in stores(b):
            store.start()
    for b in (blocks - 2, blocks - 1):
        for store in stores(b):
            store.wait()
    for move in moves:
        move.wait()


def run_unpack(packed, out_mine, out_got, ig_mine, ig_got, tiles):
    tokens, half = out_mine.shape
    full = 2 * half
    ff_half = tiles * (BLOCK // 2)
    f32 = jnp.float32
    return pl.pallas_call(
        unpack_kernel,
        name="unpack",
        out_shape=(
            shape((2 * tokens, half)), shape((2 * tokens, half)),
            shape((full, half), f32), shape((full, half), f32), shape((full, half), f32), shape((half, full), f32),
            shape((full, ff_half), f32), shape((ff_half, full), f32),
        ),
        in_specs=[HBM] * 5,
        out_specs=(HBM,) * 8,
        scratch_shapes=[
            pltpu.VMEM((2, BLOCK, full), jnp.bfloat16),
            pltpu.VMEM((2, BLOCK, full), f32),
            pltpu.SemaphoreType.DMA((2,)),
            pltpu.SemaphoreType.DMA((2, 5)),
            pltpu.SemaphoreType.DMA((4,)),
        ],
        compiler_params=pltpu.CompilerParams(vmem_limit_bytes=32 << 20),
        cost_estimate=pl.CostEstimate(flops=0, bytes_accessed=60 << 20, transcendentals=0),
    )(packed, out_mine, out_got, ig_mine, ig_got)


def on_core(
    inputs, lengths, w_query, b_query, w_key, w_value, b_value, w_out, b_out, gain_one, shift_one, w_in, b_in, w_back,
    b_back, gain_two, shift_two, cotangent,
):
    tokens = inputs.shape[0] // 2
    half = inputs.shape[1]
    seq = inputs.shape[0] // lengths.shape[0]
    tiles = w_in.shape[1] // (BLOCK // 2)
    mp = lax.axis_index("mp")

    def swap(array):
        return lax.ppermute(array, "mp", [(0, 1), (1, 0)])

    def for_other(array):
        return lax.dynamic_slice_in_dim(array, (1 - mp) * tokens, tokens, 0)

    vectors = jnp.concatenate(
        [b_query, b_value, b_in, b_out, gain_one, shift_one, b_back, gain_two, shift_two]
    ).reshape(12, half)
    x_other = swap(for_other(inputs))
    oth = swap(vectors)
    other = [swap(w) for w in (w_query, w_key, w_value, w_out)]
    cot_other = swap(for_other(cotangent))
    w_ino, w_backo = swap(w_in), swap(w_back)
    own = vectors.astype(jnp.float32)
    oth = oth.astype(jnp.float32)
    zero = jnp.zeros_like(own[0])
    biases = jnp.stack([own[0], oth[0], zero, zero, own[1], oth[1]])
    weights = [w for both in zip((w_query, w_key, w_value, w_out), other) for w in both]
    x, qkv, ctx, aux, hid, low, normed, inv = run_attention(
        inputs, x_other, weights, biases, own, oth, lengths, seq
    )
    part = BLOCK // 2
    bias = jnp.concatenate([own[2:6].reshape(tiles, part), oth[2:6].reshape(tiles, part)], axis=1)
    act, slope, out_mine, out_other, rounded, grad_summed, sums = run_ffn(
        low, hid, w_in, w_ino, w_back, w_backo, bias, own, oth, cotangent, cot_other, lengths
    )
    out_got = swap(out_other)
    packed, ig_mine, ig_got = run_backward(
        act, slope, rounded, grad_summed, low, w_in, w_ino, w_back, w_backo, normed, inv, own, oth, sums, x, qkv, ctx,
        aux, weights, lengths, seq,
    )
    output, input_grad, g_q, g_k, g_v, g_o, g_in, g_back = run_unpack(packed, out_mine, out_got, ig_mine, ig_got, tiles)
    at = (tiles + 4) * BLOCK
    v = packed[at : at + 12, :half].astype(jnp.float32)
    return (
        output, input_grad, g_q, v[0], g_k, g_v, v[1], g_o, v[2], v[3], v[4], g_in, v[8:12].reshape(-1), g_back, v[5],
        v[6], v[7],
    )


def gelu_exact(ffn_inner):
    return jax.nn.gelu(ffn_inner, approximate=False)


def normalize_rows(summed, gain_vec, shift_vec):
    average = jnp.mean(summed, axis=-1, keepdims=True)
    centred = summed - average
    inv_std = lax.rsqrt(jnp.mean(centred * centred, axis=-1, keepdims=True) + eps)
    normed = centred * inv_std
    return (normed * gain_vec + shift_vec, normed, inv_std)


def normalize_back(grad_out, normed, inv_std, gain_vec):
    scaled = grad_out * gain_vec
    centred = scaled - jnp.mean(scaled, axis=-1, keepdims=True)
    return inv_std * (centred - normed * jnp.mean(scaled * normed, axis=-1, keepdims=True))


def on_device(
    inputs,
    lengths,
    w_query,
    b_query,
    w_key,
    w_value,
    b_value,
    w_out,
    b_out,
    gain_one,
    shift_one,
    w_in,
    b_in,
    w_back,
    b_back,
    gain_two,
    shift_two,
    cotangent,
):
    token_count, part_cols = inputs.shape
    page_count = lengths.shape[0]
    seq_len = token_count // page_count
    head_size = HDIM
    local_heads = w_query.shape[1] // head_size
    score_scale = head_size ** (-0.5)
    offset = lax.axis_index("mp") * part_cols

    def own_cols(full_array):
        return lax.dynamic_slice_in_dim(full_array, offset, part_cols, full_array.ndim - 1)

    vectors = jnp.stack([b_out, gain_one, shift_one, b_back, gain_two, shift_two])
    token_rows, vector_rows = (
        lax.all_gather(inputs, "mp", axis=1, tiled=True),
        lax.all_gather(vectors, "mp", axis=1, tiled=True),
    )
    vector_rows = vector_rows.astype(jnp.float32)
    full_b_out, full_gain_one, full_shift_one = (vector_rows[0], vector_rows[1], vector_rows[2])
    full_b_back, full_gain_two, full_shift_two = (vector_rows[3], vector_rows[4], vector_rows[5])
    positions = jnp.arange(seq_len, dtype=jnp.int32)
    key_valid = positions[None, :] < lengths[:, None]
    row_valid = key_valid.reshape(token_count, 1).astype(jnp.float32)
    head_shape = (page_count, seq_len, local_heads, head_size)
    queries = (
        (
            jnp.dot(token_rows, w_query, preferred_element_type=jnp.float32)
            + b_query.astype(jnp.float32)
        )
        .astype(jnp.bfloat16)
        .reshape(head_shape)
    )
    keys_all = (
        jnp.dot(token_rows, w_key, preferred_element_type=jnp.float32)
        .astype(jnp.bfloat16)
        .reshape(head_shape)
    )
    values = (
        (
            jnp.dot(token_rows, w_value, preferred_element_type=jnp.float32)
            + b_value.astype(jnp.float32)
        )
        .astype(jnp.bfloat16)
        .reshape(head_shape)
    )

    def masked_scores(page_queries, page_keys, page_valid):
        scores = (
            jnp.einsum("qhd,khd->hqk", page_queries, page_keys, preferred_element_type=jnp.float32)
            * score_scale
        )
        return jnp.where(page_valid[None, None, :], scores, -1e30)

    def attend(packed):
        page_queries, page_keys, page_values, page_valid = packed
        scores = masked_scores(page_queries, page_keys, page_valid)
        row_max = jnp.max(scores, axis=-1, keepdims=True)
        shifted = jnp.exp(scores - row_max)
        row_sum = jnp.sum(shifted, axis=-1, keepdims=True)
        weights = (shifted / row_sum).astype(jnp.bfloat16)
        context = jnp.einsum(
            "hqk,khd->qhd", weights, page_values, preferred_element_type=jnp.float32
        )
        return (context.astype(jnp.bfloat16), (row_max + jnp.log(row_sum))[..., 0])

    context, log_total = lax.map(attend, (queries, keys_all, values, key_valid))
    context = context.reshape(token_count, local_heads * head_size)
    attn_part = jnp.dot(context, w_out, preferred_element_type=jnp.float32)
    attended = token_rows.astype(jnp.float32) + lax.psum(attn_part, "mp") + full_b_out
    hidden_one, normed_one, inv_std_one = normalize_rows(attended, full_gain_one, full_shift_one)
    hidden_low = hidden_one.astype(jnp.bfloat16)
    ffn_inner = jnp.dot(hidden_low, w_in, preferred_element_type=jnp.float32) + b_in.astype(
        jnp.float32
    )
    gelu_value, gelu_pull = jax.vjp(gelu_exact, ffn_inner)
    activated = gelu_value.astype(jnp.bfloat16)
    ffn_part = jnp.dot(activated, w_back, preferred_element_type=jnp.float32)
    summed = hidden_one + lax.psum(ffn_part, "mp") + full_b_back
    out_full, normed_two, inv_std_two = normalize_rows(summed, full_gain_two, full_shift_two)
    output = own_cols(out_full).astype(jnp.bfloat16)
    grad_out = lax.all_gather(cotangent, "mp", axis=1, tiled=True).astype(jnp.float32) * row_valid
    grad_summed = normalize_back(grad_out, normed_two, inv_std_two, full_gain_two)
    grad_gain_two = own_cols(jnp.sum(grad_out * normed_two, axis=0))
    grad_shift_two = own_cols(jnp.sum(grad_out, axis=0))
    grad_b_back = own_cols(jnp.sum(grad_summed, axis=0))
    round_summed = grad_summed.astype(jnp.bfloat16)
    grad_act = jnp.einsum("rd,fd->rf", round_summed, w_back, preferred_element_type=jnp.float32)
    grad_inner = gelu_pull(grad_act)[0].astype(jnp.bfloat16)
    grad_w_back = jnp.einsum(
        "rf,rd->fd", activated, round_summed, preferred_element_type=jnp.float32
    )
    grad_w_in = jnp.einsum("rd,rf->df", hidden_low, grad_inner, preferred_element_type=jnp.float32)
    grad_b_in = jnp.sum(grad_inner.astype(jnp.float32), axis=0)
    ffn_grads = (grad_w_in, grad_b_in, grad_w_back, grad_b_back, grad_gain_two, grad_shift_two)
    back_part = jnp.einsum("rf,df->rd", grad_inner, w_in, preferred_element_type=jnp.float32)
    grad_hidden = lax.psum(back_part, "mp") + grad_summed
    grad_gain_one = own_cols(jnp.sum(grad_hidden * normed_one, axis=0))
    grad_shift_one = own_cols(jnp.sum(grad_hidden, axis=0))
    grad_attended = normalize_back(grad_hidden, normed_one, inv_std_one, full_gain_one)
    grad_b_out = own_cols(jnp.sum(grad_attended, axis=0))
    own_attended = own_cols(grad_attended)
    round_attended = grad_attended.astype(jnp.bfloat16)
    grad_w_out = jnp.einsum(
        "rc,rd->cd", context, round_attended, preferred_element_type=jnp.float32
    )
    grad_context = (
        jnp.einsum("rd,cd->rc", round_attended, w_out, preferred_element_type=jnp.float32)
        .astype(jnp.bfloat16)
        .reshape(head_shape)
    )

    def attend_back(packed):
        page_queries, page_keys, page_values, page_valid, page_total, page_grad = packed
        scores = masked_scores(page_queries, page_keys, page_valid)
        probabilities = jnp.exp(scores - page_total[..., None])
        weights = probabilities.astype(jnp.bfloat16)
        grad_values = jnp.einsum(
            "hqk,qhd->khd", weights, page_grad, preferred_element_type=jnp.float32
        )
        grad_weights = jnp.einsum(
            "qhd,khd->hqk", page_grad, page_values, preferred_element_type=jnp.float32
        )
        grad_scores = (
            probabilities
            * (grad_weights - jnp.sum(probabilities * grad_weights, axis=-1, keepdims=True))
        ).astype(jnp.bfloat16)
        grad_queries = (
            jnp.einsum("hqk,khd->qhd", grad_scores, page_keys, preferred_element_type=jnp.float32)
            * score_scale
        )
        grad_keys = (
            jnp.einsum(
                "hqk,qhd->khd", grad_scores, page_queries, preferred_element_type=jnp.float32
            )
            * score_scale
        )
        return (
            grad_queries.astype(jnp.bfloat16),
            grad_keys.astype(jnp.bfloat16),
            grad_values.astype(jnp.bfloat16),
        )

    grad_queries, grad_keys, grad_values = lax.map(
        attend_back, (queries, keys_all, values, key_valid, log_total, grad_context)
    )
    grad_queries = grad_queries.reshape(token_count, local_heads * head_size)
    grad_keys = grad_keys.reshape(token_count, local_heads * head_size)
    grad_values = grad_values.reshape(token_count, local_heads * head_size)
    grad_w_query = jnp.einsum(
        "rd,rc->dc", token_rows, grad_queries, preferred_element_type=jnp.float32
    )
    grad_w_key = jnp.einsum("rd,rc->dc", token_rows, grad_keys, preferred_element_type=jnp.float32)
    grad_w_value = jnp.einsum(
        "rd,rc->dc", token_rows, grad_values, preferred_element_type=jnp.float32
    )
    grad_b_query = jnp.sum(grad_queries.astype(jnp.float32), axis=0)
    grad_b_value = jnp.sum(grad_values.astype(jnp.float32), axis=0)
    input_part = (
        jnp.einsum("rc,dc->rd", grad_queries, w_query, preferred_element_type=jnp.float32)
        + jnp.einsum("rc,dc->rd", grad_keys, w_key, preferred_element_type=jnp.float32)
        + jnp.einsum("rc,dc->rd", grad_values, w_value, preferred_element_type=jnp.float32)
    )
    input_grad = (
        lax.psum_scatter(
            input_part.astype(jnp.bfloat16), "mp", scatter_dimension=1, tiled=True
        ).astype(jnp.float32)
        + own_attended
    ).astype(jnp.bfloat16)
    all_grads = (
        lax.psum(grad_w_query.astype(jnp.bfloat16), "dp").astype(jnp.float32),
        lax.psum(grad_b_query.astype(jnp.bfloat16), "dp").astype(jnp.float32),
        lax.psum(grad_w_key.astype(jnp.bfloat16), "dp").astype(jnp.float32),
        lax.psum(grad_w_value.astype(jnp.bfloat16), "dp").astype(jnp.float32),
        lax.psum(grad_b_value.astype(jnp.bfloat16), "dp").astype(jnp.float32),
        lax.psum(grad_w_out.astype(jnp.bfloat16), "dp").astype(jnp.float32),
        lax.psum(grad_b_out.astype(jnp.bfloat16), "dp").astype(jnp.float32),
        lax.psum(grad_gain_one.astype(jnp.bfloat16), "dp").astype(jnp.float32),
        lax.psum(grad_shift_one.astype(jnp.bfloat16), "dp").astype(jnp.float32),
        lax.psum(grad_w_in.astype(jnp.bfloat16), "dp").astype(jnp.float32),
        lax.psum(grad_b_in.astype(jnp.bfloat16), "dp").astype(jnp.float32),
        lax.psum(grad_w_back.astype(jnp.bfloat16), "dp").astype(jnp.float32),
        lax.psum(grad_b_back.astype(jnp.bfloat16), "dp").astype(jnp.float32),
        lax.psum(grad_gain_two.astype(jnp.bfloat16), "dp").astype(jnp.float32),
        lax.psum(grad_shift_two.astype(jnp.bfloat16), "dp").astype(jnp.float32),
    )
    attn_grads = all_grads[:9]
    ffn_grads = all_grads[9:]
    return (
        output,
        input_grad,
        attn_grads[0],
        attn_grads[1],
        attn_grads[2],
        attn_grads[3],
        attn_grads[4],
        attn_grads[5],
        attn_grads[6],
        attn_grads[7],
        attn_grads[8],
        ffn_grads[0],
        ffn_grads[1],
        ffn_grads[2],
        ffn_grads[3],
        ffn_grads[4],
        ffn_grads[5],
    )


def solution(mesh):
    placed = (
        P("dp", "mp"),
        P("dp"),
        P(None, "mp"),
        P("mp"),
        P(None, "mp"),
        P(None, "mp"),
        P("mp"),
        P("mp", None),
        P("mp"),
        P("mp"),
        P("mp"),
        P(None, "mp"),
        P("mp"),
        P("mp", None),
        P("mp"),
        P("mp"),
        P("mp"),
        P("dp", "mp"),
    )
    return jax.shard_map(
        on_core if dict(mesh.shape) == {"dp": 16, "mp": 2} else on_device,
        mesh=mesh,
        in_specs=placed,
        out_specs=(
            P("dp", "mp"),
            P("dp", "mp"),
            P(None, "mp"),
            P("mp"),
            P(None, "mp"),
            P(None, "mp"),
            P("mp"),
            P("mp", None),
            P("mp"),
            P("mp"),
            P("mp"),
            P(None, "mp"),
            P("mp"),
            P("mp", None),
            P("mp"),
            P("mp"),
            P("mp"),
        ),
        check_vma=False,
    )
```

```python
import functools

import jax
import jax.numpy as jnp
from jax import lax
from jax.experimental import pallas as pl
from jax.experimental.pallas import tpu as pltpu
from jax.sharding import PartitionSpec as P

MESH = pl.DeviceIdType.MESH
HDIM = 64
eps = 1e-05
LOG2_E = 1.4426950408889634
CDF_TERMS = (
    7.97884941e-01, 3.63330844e-02, -3.25946972e-05, -5.53063392e-05, 3.96477773e-06, -1.32266680e-07, 1.75628964e-09,
)


QUARTER = 16
CHUNK = 4 * QUARTER
PAIR = 2 * CHUNK
BLOCK = 4 * PAIR
SLOTS = 16
STAGES = (0, 2, 4, 6, 8, 10, 12, 14)


def rows_at(start, size):
    return pl.ds(pl.multiple_of(start, QUARTER), size)


def chip_sum(pairs, grads, out, land_a, land_z, land_m, land_b, ssem, rsem, osem):
    dp = lax.axis_index("dp")
    mp = lax.axis_index("mp")
    z, y, x = dp // 4, (dp // 2) % 2, dp % 2
    inner = (z == 1) | (z == 2)
    outer = jnp.logical_not(inner)
    quarter = jnp.where(z == 1, 0, 1)

    def chip(cz, cy, cx):
        return (cz * 4 + cy * 2 + cx, mp)

    first_peer = (chip(z, y, 1 - x), chip(z, 1 - y, x))
    second_peer = (chip(z, 1 - y, x), chip(z, y, 1 - x))
    side = (x, y)
    inward = chip(jnp.where(z == 0, 1, 2), y, x)
    outward = chip(jnp.where(z == 1, 0, 3), y, x)
    across = chip(3 - z, y, x)
    twin = (dp, 1 - mp)

    def meet():
        barrier = pltpu.get_barrier_semaphore()
        for peer in first_peer + (twin,):
            pl.semaphore_signal(barrier, 1, device_id=peer, device_id_type=MESH)

        @pl.when(inner)
        def _():
            for peer in (outward, across):
                pl.semaphore_signal(barrier, 1, device_id=peer, device_id_type=MESH)
            pl.semaphore_wait(barrier, 5)

        @pl.when(outer)
        def _():
            pl.semaphore_signal(barrier, 1, device_id=inward, device_id_type=MESH)
            pl.semaphore_wait(barrier, 4)

    def half(ref, kind, k, which):
        return ref.at[rows_at(k * PAIR + kind * CHUNK + which * 2 * QUARTER, 2 * QUARTER)]

    def own(kind, k):
        return half(grads, kind, k, side[kind])

    def own_out(kind, k):
        return half(out, kind, k, side[kind])

    def part_of(ref, kind, k, which):
        return ref.at[rows_at(k * PAIR + kind * CHUNK + (side[kind] * 2 + which) * QUARTER, QUARTER)]

    def part(kind, k, which):
        return part_of(grads, kind, k, which)

    def keep(kind, k):
        return pltpu.make_async_copy(
            part(kind, k, quarter), part_of(out, kind, k, quarter), osem.at[kind, lax.rem(k, SLOTS)]
        )

    def send(stage, kind, k, source, target, peer):
        slot = lax.rem(k, SLOTS)
        return pltpu.make_async_remote_copy(
            source,
            target,
            ssem.at[stage, kind, slot],
            rsem.at[stage, kind, slot],
            device_id=peer,
            device_id_type=MESH,
        )

    def landing(buffer, kind, k):
        return buffer.at[lax.rem(k, SLOTS), kind]

    def scatter_first(kind, k):
        return send(0, kind, k, half(grads, kind, k, 1 - side[kind]), landing(land_a, kind, k), first_peer[kind])

    def go_in(kind, k):
        return send(1, kind, k, own(kind, k), landing(land_z, kind, k), inward)

    def scatter_across(kind, k):
        return send(2, kind, k, part(kind, k, 1 - quarter), landing(land_m, kind, k), across)

    def swap_second(kind, k):
        return send(3, kind, k, part(kind, k, quarter), landing(land_b, kind, k), second_peer[kind])

    def gather_across(kind, k):
        return send(4, kind, k, part(kind, k, quarter), part_of(out, kind, k, quarter), across)

    def go_out(kind, k):
        return send(5, kind, k, own_out(kind, k), own_out(kind, k), outward)

    def gather_first(kind, k):
        return send(6, kind, k, own_out(kind, k), own_out(kind, k), first_peer[kind])

    def step(t):
        ks = [t - offset for offset in STAGES]
        live = [(k >= 0) & (k < pairs) for k in ks]

        @pl.when(live[7])
        def _():
            for kind in (0, 1):
                gather_first(kind, ks[7]).wait()

        @pl.when(live[6] & inner)
        def _():
            for kind in (0, 1):
                go_out(kind, ks[6]).wait_send()

        @pl.when(live[6] & outer)
        def _():
            for kind in (0, 1):
                go_out(kind, ks[6]).wait_recv()
                gather_first(kind, ks[6]).start()

        @pl.when(live[5] & inner)
        def _():
            for kind in (0, 1):
                gather_across(kind, ks[5]).wait()
                keep(kind, ks[5]).wait()
                go_out(kind, ks[5]).start()
                gather_first(kind, ks[5]).start()

        @pl.when(live[4] & inner)
        def _():
            for kind in (0, 1):
                swap_second(kind, ks[4]).wait()
                add_into(part(kind, ks[4], quarter), landing(land_b, kind, ks[4]))
                gather_across(kind, ks[4]).start()
                keep(kind, ks[4]).start()

        @pl.when(live[3] & inner)
        def _():
            for kind in (0, 1):
                scatter_across(kind, ks[3]).wait()
                add_into(part(kind, ks[3], quarter), landing(land_m, kind, ks[3]))
                swap_second(kind, ks[3]).start()

        @pl.when(live[2] & inner)
        def _():
            for kind in (0, 1):
                go_in(kind, ks[2]).wait_recv()
                add_into(own(kind, ks[2]), landing(land_z, kind, ks[2]))
                scatter_across(kind, ks[2]).start()

        @pl.when(live[2] & outer)
        def _():
            for kind in (0, 1):
                go_in(kind, ks[2]).wait_send()

        @pl.when(live[1])
        def _():
            for kind in (0, 1):
                scatter_first(kind, ks[1]).wait()
                add_into(own(kind, ks[1]), landing(land_a, kind, ks[1]))

                @pl.when(outer)
                def _():
                    go_in(kind, ks[1]).start()

        @pl.when(live[0])
        def _():
            for kind in (0, 1):
                scatter_first(kind, ks[0]).start()

    return meet, step


def add_into(target, arrived):
    total = target[...].astype(jnp.float32) + arrived[...].astype(jnp.float32)
    target[...] = total.astype(jnp.bfloat16)


def dot_tn(left, right):
    return lax.dot_general(left, right, (((0,), (0,)), ((), ())), preferred_element_type=jnp.float32)


def dot_nt(left, right):
    return lax.dot_general(left, right, (((1,), (1,)), ((), ())), preferred_element_type=jnp.float32)


def gelu_and_slope(v):
    square = v * v
    q = CDF_TERMS[-1] * square + CDF_TERMS[-2]
    for term in CDF_TERMS[-3::-1]:
        q = q * square + term
    cdf = 0.5 * jnp.tanh(v * q) + 0.5
    pdf = jnp.exp2(square * (-0.5 * LOG2_E)) * 0.3989422804014327
    return v * cdf, cdf + v * pdf


def lane_of(rows):
    return lax.broadcasted_iota(jnp.int32, (rows, 128), 1)


def key_lanes(length, rows):
    lane = lane_of(rows) % 64
    slot = lax.broadcasted_iota(jnp.int32, (rows, 128), 0)
    bias = jnp.where(slot < length, 0.0, -1e30)
    return jnp.where(lane < 3, 1.0, jnp.where(lane == 3, bias, 0.0)).astype(jnp.bfloat16)


def layer_kernel(
    inputs, cotangent, w_q, w_k, w_v, w_o, w_in, w_back,
    b_q, b_v, b_in, b_o, g_one, s_one, b_back, g_two, s_two, lens,
    out, out_own, out_recv, ig_own, ig_recv, act_hbm, slope_hbm, w_other, w_oo, w_ino, w_backo,
    grads, land_a, land_z, land_m, land_b, send_t, land_t, send_v, land_v, acc, buf_a, low, buf_c, buf_d, buf_e,
    buf_f, inner_g, qkv, xb, ctx, aux, normed_b, inv_b, vec_own, vec_oth, nat, bias_qkv, bias_ff, bias_in, sums_b, kl,
    ssem, rsem, osem, tsem, trsem, vsem, vrsem, isem, psem, lsem, gsem, xsem, xrsem, fsem, frsem,
):
    dp = lax.axis_index("dp")
    mp = lax.axis_index("mp")
    tokens, full = buf_a.shape
    half = full // 2
    tiles = act_hbm.shape[0]
    wide = act_hbm.shape[2]
    part = wide // 2
    seq = kl.shape[0]
    pages = tokens // seq
    pairs = grads.shape[0] // PAIR
    last_rows = (pairs - 1) * PAIR
    meet, tick = chip_sum(pairs, grads, out, land_a, land_z, land_m, land_b, ssem, rsem, osem)
    own_cols = pl.ds(pl.multiple_of(mp * half, half), half)
    other_cols = pl.ds(pl.multiple_of((1 - mp) * half, half), half)
    own_tokens = pl.ds(pl.multiple_of(mp * tokens, tokens), tokens)
    other_tokens = pl.ds(pl.multiple_of((1 - mp) * tokens, tokens), tokens)
    twin = (dp, 1 - mp)

    def load(i, src, dst):
        return pltpu.make_async_copy(src, dst, lsem.at[i])

    def give(i, src, dst, sends, gets):
        return pltpu.make_async_remote_copy(
            src, dst, sends.at[i], gets.at[i], device_id=twin, device_id_type=MESH
        )

    def weight_rows(n):
        return pl.ds(n * full, full)

    loads = [load(0, inputs.at[own_tokens], xb.at[:, own_cols])]
    loads += [load(1 + n, w, grads.at[weight_rows(n), pl.ds(0, half)]) for n, w in enumerate((w_q, w_k, w_v))]
    loads += [load(4, w_o, buf_f.at[0]), load(5, cotangent.at[own_tokens], buf_a.at[:, own_cols])]
    for copy in loads:
        copy.start()
    vec_own[...] = jnp.zeros_like(vec_own)
    at_row = 0
    for ref in (b_q, b_v, b_in, b_o, g_one, s_one, b_back, g_two, s_two):
        for c in range(0, ref.shape[0], half):
            vec_own[at_row : at_row + 1, :] = ref[c : c + half].astype(jnp.float32).reshape(1, half)
            at_row += 1
    meet()
    gifts = [
        give(0, inputs.at[other_tokens], xb.at[:, own_cols], xsem, xrsem),
        give(1, vec_own, vec_oth, xsem, xrsem),
    ]
    gifts += [
        give(2 + n, w, grads.at[weight_rows(n), pl.ds(half, half)], xsem, xrsem)
        for n, w in enumerate((w_q, w_k, w_v))
    ]
    gifts += [
        give(5, w_o, buf_f.at[1], xsem, xrsem),
        give(6, cotangent.at[other_tokens], buf_a.at[:, own_cols], xsem, xrsem),
    ]
    for gift in gifts:
        gift.start()

    def ff_gifts(j):
        at = pl.ds(pl.multiple_of(j * part, part), part)
        return (
            pltpu.make_async_remote_copy(
                w_in.at[:, at], w_ino.at[:, at], fsem.at[j, 0], frsem.at[j, 0], device_id=twin, device_id_type=MESH
            ),
            pltpu.make_async_remote_copy(
                w_back.at[at], w_backo.at[at], fsem.at[j, 1], frsem.at[j, 1], device_id=twin, device_id_type=MESH
            ),
        )

    gifts[1].wait_recv()
    nat[:, own_cols] = vec_own[...]
    nat[:, other_cols] = vec_oth[...]
    for n, row in enumerate((0, None, 1)):
        for h, ref in enumerate((vec_own, vec_oth)):
            at = slice(h * half, (h + 1) * half)
            if row is None:
                bias_qkv[n : n + 1, at] = jnp.zeros((1, half), jnp.float32)
            else:
                bias_qkv[n : n + 1, at] = ref[row : row + 1, :]
    for j in range(tiles):
        at = slice((j % 2) * part, (j % 2 + 1) * part)
        row = 2 + j // 2
        bias_ff[j : j + 1, :part] = vec_own[row : row + 1, at]
        bias_ff[j : j + 1, part:] = vec_oth[row : row + 1, at]
    loads[0].wait()
    gifts[0].wait_recv()

    for n in range(3):
        loads[1 + n].wait()
        gifts[2 + n].wait_recv()
        if n == 2:
            def start_gifts(j, carry):
                for gift in ff_gifts(j):
                    gift.start()
                return carry

            lax.fori_loop(0, tiles, start_gifts, 0)

        for h in (0, 1):
            at = slice(h * half, (h + 1) * half)
            made = jnp.dot(xb[...], grads[n * full : (n + 1) * full, at], preferred_element_type=jnp.float32)
            qkv[2 * n + h] = (made + bias_qkv[n : n + 1, at]).astype(jnp.bfloat16)

    keeps = [load(6 + n, grads.at[weight_rows(n), pl.ds(half, half)], w_other.at[n]) for n in range(3)]
    for copy in keeps:
        copy.start()
    gifts[5].wait_recv()
    keeps.append(load(9, buf_f.at[1], w_oo))
    keeps[3].start()
    loads[4].wait()

    lane = lane_of(seq)
    low_lanes = lane < 64
    q_one = jnp.where(lane % 64 == 3, 1.0, 0.0).astype(jnp.bfloat16)

    def pair_forward(i, carry):
        page, pair = i // 8, lax.rem(i, 8)

        @pl.when(pair == 0)
        def _():
            kl[...] = key_lanes(lens[mp * pages + page], seq)

        rows = pl.ds(pl.multiple_of(page * seq, seq), seq)
        side = pair // 4
        cols = pl.ds(pl.multiple_of(lax.rem(pair, 4) * 128, 128), 128)
        kp = qkv[2 + side, rows, cols]
        vp = qkv[4 + side, rows, cols]
        qp = qkv[side, rows, cols] * jnp.bfloat16(0.125)
        one = jnp.ones_like(vp)
        outs = []
        for h in (0, 1):
            mine = low_lanes if h == 0 else jnp.logical_not(low_lanes)
            scores = dot_nt(jnp.where(mine, qp, q_one), jnp.where(mine, kp, kl[...]))
            top = jnp.max(scores, axis=1, keepdims=True)
            weights = jnp.exp(scores - top).astype(jnp.bfloat16)
            outs.append((top, jnp.dot(weights, jnp.where(mine, vp, one), preferred_element_type=jnp.float32)))
        (top0, out0), (top1, out1) = outs
        total = jnp.where(low_lanes, out1, out0)
        value = jnp.where(low_lanes, out0, out1) / pltpu.roll(total, 64, 1)
        neg = -(jnp.where(low_lanes, top1, top0) + jnp.log(total))
        first = neg.astype(jnp.bfloat16)
        rest = neg - first.astype(jnp.float32)
        second = rest.astype(jnp.bfloat16)
        third = (rest - second.astype(jnp.float32)).astype(jnp.bfloat16)
        at = lane % 64
        mixed = jnp.where(at == 0, first, jnp.where(at == 1, second, jnp.where(at == 2, third, q_one)))
        ctx[side, rows, cols] = value.astype(jnp.bfloat16)
        aux[side, rows, cols] = mixed
        return carry

    lax.fori_loop(0, 8 * pages, pair_forward, 0)

    def fetch_in(j, slot):
        at = pl.ds(pl.multiple_of(j * part, part), part)
        return [
            pltpu.make_async_copy(w_in.at[:, at], buf_e.at[slot, :, pl.ds(0, part)], isem.at[slot, 2]),
            pltpu.make_async_copy(w_ino.at[:, at], buf_e.at[slot, :, pl.ds(part, part)], isem.at[slot, 3]),
        ]

    def fetch_back(j, slot):
        at = pl.ds(pl.multiple_of(j * part, part), part)
        return [
            pltpu.make_async_copy(w_back.at[at], buf_f.at[slot, pl.ds(0, part)], isem.at[slot, 4]),
            pltpu.make_async_copy(w_backo.at[at], buf_f.at[slot, pl.ds(part, part)], isem.at[slot, 5]),
        ]

    def fetch_made(j, slot):
        return [
            pltpu.make_async_copy(act_hbm.at[j], buf_c.at[slot], isem.at[slot, 0]),
            pltpu.make_async_copy(slope_hbm.at[j], buf_d.at[slot], isem.at[slot, 1]),
        ]

    def start(copies):
        for copy in copies:
            copy.start()

    def finish(copies):
        for copy in copies:
            copy.wait()

    def got_gifts(j):
        for gift in ff_gifts(j):
            gift.wait_recv()

    got_gifts(0)
    start(fetch_in(0, 0))
    step = 256

    def norm_one(i, carry):
        rows = pl.ds(pl.multiple_of(i * step, step), step)
        attended = (
            xb[rows, :].astype(jnp.float32)
            + jnp.dot(ctx[0, rows, :], buf_f[0], preferred_element_type=jnp.float32)
            + jnp.dot(ctx[1, rows, :], buf_f[1], preferred_element_type=jnp.float32)
            + nat[6:7, :]
        )
        average = jnp.mean(attended, axis=1, keepdims=True)
        centred = attended - average
        inv = lax.rsqrt(jnp.mean(centred * centred, axis=1, keepdims=True) + eps)
        normed = centred * inv
        hidden = normed * nat[7:8, :] + nat[8:9, :]
        acc[rows, :] = hidden
        low[rows, :] = hidden.astype(jnp.bfloat16)
        normed_b[rows, :] = normed.astype(jnp.bfloat16)
        inv_b[rows, :] = jnp.broadcast_to(inv, (step, 128))
        return carry

    lax.fori_loop(0, tokens // step, norm_one, 0)
    keeps[3].wait()
    start(fetch_back(0, 0))

    def saves(j, slot):
        return [
            pltpu.make_async_copy(buf_c.at[slot], act_hbm.at[j], psem.at[slot, 0]),
            pltpu.make_async_copy(buf_d.at[slot], slope_hbm.at[j], psem.at[slot, 1]),
        ]

    def forward_tile(j, carry):
        slot = lax.rem(j, 2)

        @pl.when(j + 1 < tiles)
        def _():
            got_gifts(j + 1)
            start(fetch_in(j + 1, 1 - slot) + fetch_back(j + 1, 1 - slot))

        finish(fetch_in(j, slot) + fetch_back(j, slot))

        @pl.when(j >= 2)
        def _():
            finish(saves(j - 2, slot))

        for r in range(0, tokens, half):
            rows = pl.ds(r, half)
            inner = jnp.dot(low[rows, :], buf_e[slot], preferred_element_type=jnp.float32) + bias_ff[pl.ds(j, 1), :]
            value, grad = gelu_and_slope(inner)
            value = value.astype(jnp.bfloat16)
            buf_c[slot, rows, :] = value
            buf_d[slot, rows, :] = grad.astype(jnp.bfloat16)
            acc[rows, :] += jnp.dot(value, buf_f[slot], preferred_element_type=jnp.float32)
        start(saves(j, slot))
        return carry

    lax.fori_loop(0, tiles, forward_tile, 0)
    loads[5].wait()
    gifts[6].wait_recv()
    stage_rows = tiles * BLOCK

    def norm_two(i, sums):
        at = pl.multiple_of(i * step, step)
        rows = pl.ds(at, step)
        summed = acc[rows, :] + nat[9:10, :]
        average = jnp.mean(summed, axis=1, keepdims=True)
        centred = summed - average
        inv = lax.rsqrt(jnp.mean(centred * centred, axis=1, keepdims=True) + eps)
        normed = centred * inv
        grads[pl.ds(pl.multiple_of(stage_rows + i * step, step), step), :] = (
            normed * nat[10:11, :] + nat[11:12, :]
        ).astype(jnp.bfloat16)
        page = (i * step) // seq
        slots = lax.broadcasted_iota(jnp.int32, (step, 1), 0) + lax.rem(i * step, seq)
        valid = jnp.where(slots < lens[mp * pages + page], 1.0, 0.0)
        grad = buf_a[rows, :].astype(jnp.float32) * valid
        scaled = grad * nat[10:11, :]
        mean_one = jnp.mean(scaled, axis=1, keepdims=True)
        mean_two = jnp.mean(scaled * normed, axis=1, keepdims=True)
        back = inv * (scaled - mean_one - normed * mean_two)
        acc[rows, :] = back
        buf_a[rows, :] = back.astype(jnp.bfloat16)
        return (
            sums[0] + jnp.sum(back, axis=0, keepdims=True),
            sums[1] + jnp.sum(grad * normed, axis=0, keepdims=True),
            sums[2] + jnp.sum(grad, axis=0, keepdims=True),
        )

    zero = jnp.zeros((1, full), jnp.float32)
    for n, row in enumerate(lax.fori_loop(0, tokens // step, norm_two, (zero, zero, zero))):
        sums_b[n : n + 1, :] = row
    finish(keeps[:3])
    staged = grads.at[pl.ds(stage_rows, tokens)]
    out_keep = pltpu.make_async_copy(staged.at[:, own_cols], out_own, gsem.at[3])
    out_send = pltpu.make_async_remote_copy(
        staged.at[:, other_cols], out_recv, gsem.at[4], gsem.at[5], device_id=twin, device_id_type=MESH
    )
    out_keep.start()
    out_send.start()
    grads[last_rows : last_rows + PAIR, :] = jnp.zeros((PAIR, full), jnp.bfloat16)

    def to_twin(b):
        slot = lax.rem(b, 2)
        return pltpu.make_async_remote_copy(
            send_t.at[slot], land_t.at[slot], tsem.at[slot], trsem.at[slot], device_id=twin, device_id_type=MESH
        )

    def take_twin(b):
        to_twin(b).wait_recv()
        slot = lax.rem(b, 2)

        def piece(i, carry):
            add_into(grads.at[rows_at(b * BLOCK + i * CHUNK, CHUNK)], land_t.at[slot, rows_at(i * CHUNK, CHUNK)])
            return carry

        lax.fori_loop(0, BLOCK // CHUNK, piece, 0)

    def backward_tile(b, carry):
        j = tiles - 1 - b
        slot = lax.rem(j, 2)
        mate = lax.rem(b, 2)

        @pl.when(b >= 2)
        def _():
            finish(fetch_made(j, slot) + fetch_in(j, slot) + fetch_back(j, slot))
            to_twin(b - 2).wait_send()

        base = b * BLOCK
        for c in range(0, full, half):
            made = dot_tn(buf_c[slot], buf_a[:, c : c + half]).astype(jnp.bfloat16)
            grads[rows_at(base, part), c : c + half] = made[:part]
            send_t[mate, :part, c : c + half] = made[part:]

        @pl.when(b >= 1)
        def _():
            take_twin(b - 1)
            tick(2 * b - 2)

        total = jnp.zeros((1, wide), jnp.float32)
        for r in range(0, tokens, half):
            rows = pl.ds(r, half)
            made = dot_nt(buf_a[rows, :], buf_f[slot]) * buf_d[slot, rows, :].astype(jnp.float32)
            made = made.astype(jnp.bfloat16)
            inner_g[rows, :] = made
            total = total + jnp.sum(made.astype(jnp.float32), axis=0, keepdims=True)
            acc[rows, :] += dot_nt(made, buf_e[slot])
        bias_in[pl.ds(j, 1), :] = total
        for c in range(0, full, part):
            made = dot_tn(low[:, c : c + part], inner_g[...]).astype(jnp.bfloat16)
            grads[rows_at(base + part, part), c : c + part] = made[:, :part]
            send_t[mate, part:, c : c + part] = made[:, part:]

        to_twin(b).start()

        @pl.when(b < 2)
        def _():
            finish(saves(j, slot))

        @pl.when(b < tiles - 2)
        def _():
            start(fetch_made(j - 2, slot) + fetch_in(j - 2, slot) + fetch_back(j - 2, slot))

        @pl.when(b >= 1)
        def _():
            tick(2 * b - 1)

        return carry

    lax.fori_loop(0, tiles, backward_tile, 0)
    t = 2 * tiles - 2

    second = [load(10, w_o, buf_f.at[0]), load(11, w_oo, buf_f.at[1])]
    start(second)

    def norm_back(i, sums):
        rows = pl.ds(pl.multiple_of(i * step, step), step)
        grad = acc[rows, :]
        normed = normed_b[rows, :].astype(jnp.float32)
        scaled = grad * nat[7:8, :]
        mean_one = jnp.mean(scaled, axis=1, keepdims=True)
        mean_two = jnp.mean(scaled * normed, axis=1, keepdims=True)
        back = inv_b[rows, 0:1] * (scaled - mean_one - normed * mean_two)
        acc[rows, :] = back
        buf_a[rows, :] = back.astype(jnp.bfloat16)
        return (
            sums[0] + jnp.sum(back, axis=0, keepdims=True),
            sums[1] + jnp.sum(grad * normed, axis=0, keepdims=True),
            sums[2] + jnp.sum(grad, axis=0, keepdims=True),
        )

    bias_o, gain_one, shift_one = lax.fori_loop(0, tokens // step, norm_back, (zero, zero, zero))
    tick(t)

    b = tiles
    to_twin(b - 2).wait_send()
    out_keep.wait()
    out_send.wait()
    finish(second)
    for h in (0, 1):
        for c in range(0, full, half):
            made = dot_tn(ctx[h], buf_a[:, c : c + half]).astype(jnp.bfloat16)
            if h == 0:
                grads[b * BLOCK : b * BLOCK + half, c : c + half] = made
            else:
                send_t[b % 2, :, c : c + half] = made
    take_twin(b - 1)
    to_twin(b).start()
    tick(t + 1)
    for h in (0, 1):
        for r in range(0, tokens, half):
            buf_e[h, r : r + half, :] = dot_nt(buf_a[r : r + half, :], buf_f[h]).astype(jnp.bfloat16)
    take_twin(b)
    tick(t + 2)
    t = t + 3

    def pair_backward(i, carry):
        page, pair = i // 8, lax.rem(i, 8)

        @pl.when(pair == 0)
        def _():
            kl[...] = key_lanes(lens[mp * pages + page], seq)

        side = pair // 4
        rows = pl.ds(pl.multiple_of(page * seq, seq), seq)
        cols = pl.ds(pl.multiple_of(lax.rem(pair, 4) * 128, 128), 128)
        qp = qkv[side, rows, cols] * jnp.bfloat16(0.125)
        kp = qkv[2 + side, rows, cols]
        vp = qkv[4 + side, rows, cols]
        extra = aux[side, rows, cols]
        gp = buf_e[side, rows, cols]
        cp = ctx[side, rows, cols]
        none = jnp.zeros_like(gp)
        made = []
        for h in (0, 1):
            mine = low_lanes if h == 0 else jnp.logical_not(low_lanes)
            scores = dot_nt(jnp.where(mine, qp, extra), jnp.where(mine, kp, kl[...]))
            probs = jnp.exp(scores)
            gh = jnp.where(mine, gp, none)
            grad_weights = dot_nt(gh, vp)
            delta = jnp.sum(gh.astype(jnp.float32) * cp.astype(jnp.float32), axis=1, keepdims=True)
            grad_scores = (probs * (grad_weights - delta)).astype(jnp.bfloat16)
            grad_v = dot_tn(probs.astype(jnp.bfloat16), gh)
            grad_q = jnp.dot(grad_scores, jnp.where(mine, kp, none), preferred_element_type=jnp.float32)
            grad_k = dot_tn(grad_scores, jnp.where(mine, qp, none))
            made.append((grad_q * 0.125, grad_k, grad_v))
        for n in range(3):
            qkv[2 * n + side, rows, cols] = (made[0][n] + made[1][n]).astype(jnp.bfloat16)
        tick(t + i)
        return carry

    lax.fori_loop(0, 8 * pages, pair_backward, 0)
    t = t + 8 * pages

    third = [load(12, w_q, buf_c.at[0]), load(13, w_k, buf_d.at[0]), load(14, w_v, buf_e.at[0])]
    third += [load(15 + n, w_other.at[n], ref.at[1]) for n, ref in enumerate((buf_c, buf_d, buf_e))]
    start(third)
    b = tiles + 1

    def weights_loop(i, carry):
        at = b + i
        slot = lax.rem(at, 2)
        to_twin(at - 2).wait_send()
        for r in range(0, full, half):
            made = dot_tn(xb[:, r : r + half], qkv[2 * i]).astype(jnp.bfloat16)
            grads[rows_at(at * BLOCK, BLOCK), r : r + half] = made
            made = dot_tn(xb[:, r : r + half], qkv[2 * i + 1]).astype(jnp.bfloat16)
            send_t[slot, :, r : r + half] = made

        @pl.when(i >= 1)
        def _():
            take_twin(at - 1)

        to_twin(at).start()
        tick(t + i)
        return carry

    lax.fori_loop(0, 3, weights_loop, 0)
    t = t + 3
    b = b + 3

    first_core = mp == 0
    owned, others = [], []
    for n in (0, 4):
        owned.append(jnp.sum(qkv[n].astype(jnp.float32), axis=0, keepdims=True))
        others.append(jnp.sum(qkv[n + 1].astype(jnp.float32), axis=0, keepdims=True))
    for row in (bias_o, gain_one, shift_one, sums_b[0:1, :], sums_b[1:2, :], sums_b[2:3, :]):
        owned.append(jnp.where(first_core, row[:, :half], row[:, half:]))
        others.append(jnp.where(first_core, row[:, half:], row[:, :half]))
    for n in range(0, tiles, 2):
        owned.append(jnp.concatenate([bias_in[n : n + 1, :part], bias_in[n + 1 : n + 2, :part]], axis=1))
        others.append(jnp.concatenate([bias_in[n : n + 1, part:], bias_in[n + 1 : n + 2, part:]], axis=1))
    fill = jnp.zeros((QUARTER - len(owned), half), jnp.float32)
    grads[last_rows : last_rows + QUARTER, :half] = jnp.concatenate(owned + [fill], axis=0).astype(jnp.bfloat16)
    send_v[...] = jnp.concatenate(others + [fill], axis=0).astype(jnp.bfloat16)
    vectors = pltpu.make_async_remote_copy(send_v, land_v, vsem, vrsem, device_id=twin, device_id_type=MESH)
    vectors.start()
    take_twin(b - 1)
    vectors.wait()
    add_into(grads.at[last_rows : last_rows + QUARTER, :half], land_v)
    to_twin(b - 2).wait_send()
    to_twin(b - 1).wait_send()
    tick(t)
    finish(third)

    def input_loop(i, carry):
        rows = pl.ds(pl.multiple_of(i * step, step), step)
        total = acc[rows, :]
        for n, ref in enumerate((buf_c, buf_d, buf_e)):
            for h in (0, 1):
                total = total + dot_nt(qkv[2 * n + h, rows, :], ref[h])
        buf_a[rows, :] = total.astype(jnp.bfloat16)
        tick(t + 1 + i)
        return carry

    lax.fori_loop(0, tokens // step, input_loop, 0)
    t = t + 1 + tokens // step
    ig_keep = pltpu.make_async_copy(buf_a.at[:, own_cols], ig_own, gsem.at[0])
    ig_send = pltpu.make_async_remote_copy(
        buf_a.at[:, other_cols], ig_recv, gsem.at[1], gsem.at[2], device_id=twin, device_id_type=MESH
    )
    ig_keep.start()
    ig_send.start()
    for gift in gifts:
        gift.wait_send()

    def end_gifts(j, carry):
        for gift in ff_gifts(j):
            gift.wait_send()
        return carry

    lax.fori_loop(0, tiles, end_gifts, 0)

    def rest(i, carry):
        tick(i)
        return carry

    lax.fori_loop(t, pairs + STAGES[-1], rest, 0)
    ig_keep.wait()
    ig_send.wait()


HBM = pl.BlockSpec(memory_space=pltpu.HBM)
VMEM = pl.BlockSpec(memory_space=pltpu.VMEM)
SMEM = pl.BlockSpec(memory_space=pltpu.SMEM)


def shape(dims, dtype=jnp.bfloat16):
    return jax.ShapeDtypeStruct(dims, dtype)


def run_layer(inputs, cotangent, w_q, w_k, w_v, w_o, w_in, w_back, vectors, lengths):
    tokens = inputs.shape[0] // 2
    half = inputs.shape[1]
    full = 2 * half
    seq = inputs.shape[0] // lengths.shape[0]
    ff_half = w_in.shape[1]
    tiles = ff_half // (BLOCK // 2)
    wide = BLOCK
    rows = (tiles + 4) * BLOCK + PAIR
    f32 = jnp.float32
    bf16 = jnp.bfloat16
    return pl.pallas_call(
        layer_kernel,
        name="layer",
        out_shape=(
            shape((rows, full)), shape((tokens, half)), shape((tokens, half)), shape((tokens, half)),
            shape((tokens, half)), shape((tiles, tokens, wide)), shape((tiles, tokens, wide)),
            shape((3, full, half)), shape((half, full)), shape((full, ff_half)), shape((ff_half, full)),
        ),
        in_specs=[HBM] * 8 + [VMEM] * 9 + [SMEM],
        out_specs=(HBM,) * 11,
        scratch_shapes=[
            pltpu.VMEM((rows, full), bf16),
            pltpu.VMEM((SLOTS, 2, 2 * QUARTER, full), bf16),
            pltpu.VMEM((SLOTS, 2, 2 * QUARTER, full), bf16),
            pltpu.VMEM((SLOTS, 2, QUARTER, full), bf16),
            pltpu.VMEM((SLOTS, 2, QUARTER, full), bf16),
            pltpu.VMEM((2, BLOCK, full), bf16),
            pltpu.VMEM((2, BLOCK, full), bf16),
            pltpu.VMEM((QUARTER, half), bf16),
            pltpu.VMEM((QUARTER, half), bf16),
            pltpu.VMEM((tokens, full), f32),
            pltpu.VMEM((tokens, full), bf16),
            pltpu.VMEM((tokens, full), bf16),
            pltpu.VMEM((2, tokens, half), bf16),
            pltpu.VMEM((2, tokens, half), bf16),
            pltpu.VMEM((2, tokens, half), bf16),
            pltpu.VMEM((2, half, full), bf16),
            pltpu.VMEM((tokens, wide), bf16),
            pltpu.VMEM((6, tokens, half), bf16),
            pltpu.VMEM((tokens, full), bf16),
            pltpu.VMEM((2, tokens, half), bf16),
            pltpu.VMEM((2, tokens, half), bf16),
            pltpu.VMEM((tokens, full), bf16),
            pltpu.VMEM((tokens, 128), f32),
            pltpu.VMEM((QUARTER, half), f32),
            pltpu.VMEM((QUARTER, half), f32),
            pltpu.VMEM((QUARTER, full), f32),
            pltpu.VMEM((8, full), f32),
            pltpu.VMEM((tiles, wide), f32),
            pltpu.VMEM((tiles, wide), f32),
            pltpu.VMEM((8, full), f32),
            pltpu.VMEM((seq, 128), bf16),
            pltpu.SemaphoreType.DMA((7, 2, SLOTS)),
            pltpu.SemaphoreType.DMA((7, 2, SLOTS)),
            pltpu.SemaphoreType.DMA((2, SLOTS)),
            pltpu.SemaphoreType.DMA((2,)),
            pltpu.SemaphoreType.DMA((2,)),
            pltpu.SemaphoreType.DMA,
            pltpu.SemaphoreType.DMA,
            pltpu.SemaphoreType.DMA((2, 6)),
            pltpu.SemaphoreType.DMA((2, 2)),
            pltpu.SemaphoreType.DMA((18,)),
            pltpu.SemaphoreType.DMA((6,)),
            pltpu.SemaphoreType.DMA((7,)),
            pltpu.SemaphoreType.DMA((7,)),
            pltpu.SemaphoreType.DMA((tiles, 2)),
            pltpu.SemaphoreType.DMA((tiles, 2)),
        ],
        compiler_params=pltpu.CompilerParams(
            collective_id=0, has_side_effects=True, vmem_limit_bytes=62 << 20
        ),
    )(inputs, cotangent, w_q, w_k, w_v, w_o, w_in, w_back, *vectors, lengths)


def unpack_kernel(
    packed, out_mine, out_got, ig_mine, ig_got,
    output, input_grad, g_q, g_k, g_v, g_o, g_in, g_back,
    loaded, wide, passed, isem, osem, csem,
):
    mp = lax.axis_index("mp")
    tokens, half = out_mine.shape
    mine = pl.ds(pl.multiple_of(mp * tokens, tokens), tokens)
    other = pl.ds(pl.multiple_of((1 - mp) * tokens, tokens), tokens)
    pieces = ((out_mine, output.at[mine]), (out_got, output.at[other]), (ig_mine, input_grad.at[mine]), (ig_got, input_grad.at[other]))
    moves = [pltpu.make_async_copy(src, passed.at[i], csem.at[0, i]) for i, (src, _) in enumerate(pieces)]
    leaves = [pltpu.make_async_copy(passed.at[i], dst, csem.at[1, i]) for i, (_, dst) in enumerate(pieces)]
    for move in moves:
        move.start()
    part = BLOCK // 2
    full = packed.shape[1]
    tiles = g_back.shape[0] // part
    blocks = tiles + 4

    def fetch(b):
        return pltpu.make_async_copy(packed.at[b * BLOCK : (b + 1) * BLOCK], loaded.at[b % 2], isem.at[b % 2])

    def stores(b):
        ref = wide.at[b % 2]
        if b < tiles:
            pieces = [(ref.at[:part], g_back.at[(tiles - 1 - b) * part : (tiles - b) * part])]
            for c in range(0, full, part):
                pieces.append((ref.at[part:, c : c + part], g_in.at[c : c + part, (tiles - 1 - b) * part : (tiles - b) * part]))
        elif b == tiles:
            pieces = [(ref, g_o)]
        else:
            target = (g_q, g_k, g_v)[b - tiles - 1]
            pieces = [(ref.at[:, :half], target.at[:half]), (ref.at[:, half:], target.at[half:])]
        return [pltpu.make_async_copy(src, dst, osem.at[b % 2, i]) for i, (src, dst) in enumerate(pieces)]

    fetch(0).start()
    for move, leave in zip(moves, leaves):
        move.wait()
        leave.start()
    for b in range(blocks):
        if b + 1 < blocks:
            fetch(b + 1).start()
        fetch(b).wait()
        if b >= 2:
            for store in stores(b - 2):
                store.wait()
        for r in range(0, BLOCK, CHUNK):
            wide[b % 2, r : r + CHUNK, :] = loaded[b % 2, r : r + CHUNK, :].astype(jnp.float32)
        for store in stores(b):
            store.start()
    for b in (blocks - 2, blocks - 1):
        for store in stores(b):
            store.wait()
    for leave in leaves:
        leave.wait()


def run_unpack(packed, out_mine, out_got, ig_mine, ig_got, tiles):
    tokens, half = out_mine.shape
    full = 2 * half
    ff_half = tiles * (BLOCK // 2)
    f32 = jnp.float32
    return pl.pallas_call(
        unpack_kernel,
        name="unpack",
        out_shape=(
            shape((2 * tokens, half)), shape((2 * tokens, half)),
            shape((full, half), f32), shape((full, half), f32), shape((full, half), f32), shape((half, full), f32),
            shape((full, ff_half), f32), shape((ff_half, full), f32),
        ),
        in_specs=[HBM] * 5,
        out_specs=(HBM,) * 8,
        scratch_shapes=[
            pltpu.VMEM((2, BLOCK, full), jnp.bfloat16),
            pltpu.VMEM((2, BLOCK, full), f32),
            pltpu.VMEM((4, tokens, half), jnp.bfloat16),
            pltpu.SemaphoreType.DMA((2,)),
            pltpu.SemaphoreType.DMA((2, 5)),
            pltpu.SemaphoreType.DMA((2, 4)),
        ],
        compiler_params=pltpu.CompilerParams(vmem_limit_bytes=60 << 20),
        cost_estimate=pl.CostEstimate(flops=0, bytes_accessed=60 << 20, transcendentals=0),
    )(packed, out_mine, out_got, ig_mine, ig_got)


def on_core(
    inputs, lengths, w_query, b_query, w_key, w_value, b_value, w_out, b_out, gain_one, shift_one, w_in, b_in, w_back,
    b_back, gain_two, shift_two, cotangent,
):
    half = inputs.shape[1]
    tiles = w_in.shape[1] // (BLOCK // 2)
    vectors = (b_query, b_value, b_in, b_out, gain_one, shift_one, b_back, gain_two, shift_two)
    packed, out_mine, out_got, ig_mine, ig_got, *_ = run_layer(
        inputs, cotangent, w_query, w_key, w_value, w_out, w_in, w_back, vectors, lengths
    )
    output, input_grad, g_q, g_k, g_v, g_o, g_in, g_back = run_unpack(packed, out_mine, out_got, ig_mine, ig_got, tiles)
    at = (tiles + 4) * BLOCK
    v = packed[at : at + 12, :half].astype(jnp.float32)
    return (
        output, input_grad, g_q, v[0], g_k, g_v, v[1], g_o, v[2], v[3], v[4], g_in, v[8:12].reshape(-1), g_back, v[5],
        v[6], v[7],
    )


def gelu_exact(ffn_inner):
    return jax.nn.gelu(ffn_inner, approximate=False)


def normalize_rows(summed, gain_vec, shift_vec):
    average = jnp.mean(summed, axis=-1, keepdims=True)
    centred = summed - average
    inv_std = lax.rsqrt(jnp.mean(centred * centred, axis=-1, keepdims=True) + eps)
    normed = centred * inv_std
    return (normed * gain_vec + shift_vec, normed, inv_std)


def normalize_back(grad_out, normed, inv_std, gain_vec):
    scaled = grad_out * gain_vec
    centred = scaled - jnp.mean(scaled, axis=-1, keepdims=True)
    return inv_std * (centred - normed * jnp.mean(scaled * normed, axis=-1, keepdims=True))


def on_device(
    inputs,
    lengths,
    w_query,
    b_query,
    w_key,
    w_value,
    b_value,
    w_out,
    b_out,
    gain_one,
    shift_one,
    w_in,
    b_in,
    w_back,
    b_back,
    gain_two,
    shift_two,
    cotangent,
):
    token_count, part_cols = inputs.shape
    page_count = lengths.shape[0]
    seq_len = token_count // page_count
    head_size = HDIM
    local_heads = w_query.shape[1] // head_size
    score_scale = head_size ** (-0.5)
    offset = lax.axis_index("mp") * part_cols

    def own_cols(full_array):
        return lax.dynamic_slice_in_dim(full_array, offset, part_cols, full_array.ndim - 1)

    vectors = jnp.stack([b_out, gain_one, shift_one, b_back, gain_two, shift_two])
    token_rows, vector_rows = (
        lax.all_gather(inputs, "mp", axis=1, tiled=True),
        lax.all_gather(vectors, "mp", axis=1, tiled=True),
    )
    vector_rows = vector_rows.astype(jnp.float32)
    full_b_out, full_gain_one, full_shift_one = (vector_rows[0], vector_rows[1], vector_rows[2])
    full_b_back, full_gain_two, full_shift_two = (vector_rows[3], vector_rows[4], vector_rows[5])
    positions = jnp.arange(seq_len, dtype=jnp.int32)
    key_valid = positions[None, :] < lengths[:, None]
    row_valid = key_valid.reshape(token_count, 1).astype(jnp.float32)
    head_shape = (page_count, seq_len, local_heads, head_size)
    queries = (
        (
            jnp.dot(token_rows, w_query, preferred_element_type=jnp.float32)
            + b_query.astype(jnp.float32)
        )
        .astype(jnp.bfloat16)
        .reshape(head_shape)
    )
    keys_all = (
        jnp.dot(token_rows, w_key, preferred_element_type=jnp.float32)
        .astype(jnp.bfloat16)
        .reshape(head_shape)
    )
    values = (
        (
            jnp.dot(token_rows, w_value, preferred_element_type=jnp.float32)
            + b_value.astype(jnp.float32)
        )
        .astype(jnp.bfloat16)
        .reshape(head_shape)
    )

    def masked_scores(page_queries, page_keys, page_valid):
        scores = (
            jnp.einsum("qhd,khd->hqk", page_queries, page_keys, preferred_element_type=jnp.float32)
            * score_scale
        )
        return jnp.where(page_valid[None, None, :], scores, -1e30)

    def attend(packed):
        page_queries, page_keys, page_values, page_valid = packed
        scores = masked_scores(page_queries, page_keys, page_valid)
        row_max = jnp.max(scores, axis=-1, keepdims=True)
        shifted = jnp.exp(scores - row_max)
        row_sum = jnp.sum(shifted, axis=-1, keepdims=True)
        weights = (shifted / row_sum).astype(jnp.bfloat16)
        context = jnp.einsum(
            "hqk,khd->qhd", weights, page_values, preferred_element_type=jnp.float32
        )
        return (context.astype(jnp.bfloat16), (row_max + jnp.log(row_sum))[..., 0])

    context, log_total = lax.map(attend, (queries, keys_all, values, key_valid))
    context = context.reshape(token_count, local_heads * head_size)
    attn_part = jnp.dot(context, w_out, preferred_element_type=jnp.float32)
    attended = token_rows.astype(jnp.float32) + lax.psum(attn_part, "mp") + full_b_out
    hidden_one, normed_one, inv_std_one = normalize_rows(attended, full_gain_one, full_shift_one)
    hidden_low = hidden_one.astype(jnp.bfloat16)
    ffn_inner = jnp.dot(hidden_low, w_in, preferred_element_type=jnp.float32) + b_in.astype(
        jnp.float32
    )
    gelu_value, gelu_pull = jax.vjp(gelu_exact, ffn_inner)
    activated = gelu_value.astype(jnp.bfloat16)
    ffn_part = jnp.dot(activated, w_back, preferred_element_type=jnp.float32)
    summed = hidden_one + lax.psum(ffn_part, "mp") + full_b_back
    out_full, normed_two, inv_std_two = normalize_rows(summed, full_gain_two, full_shift_two)
    output = own_cols(out_full).astype(jnp.bfloat16)
    grad_out = lax.all_gather(cotangent, "mp", axis=1, tiled=True).astype(jnp.float32) * row_valid
    grad_summed = normalize_back(grad_out, normed_two, inv_std_two, full_gain_two)
    grad_gain_two = own_cols(jnp.sum(grad_out * normed_two, axis=0))
    grad_shift_two = own_cols(jnp.sum(grad_out, axis=0))
    grad_b_back = own_cols(jnp.sum(grad_summed, axis=0))
    round_summed = grad_summed.astype(jnp.bfloat16)
    grad_act = jnp.einsum("rd,fd->rf", round_summed, w_back, preferred_element_type=jnp.float32)
    grad_inner = gelu_pull(grad_act)[0].astype(jnp.bfloat16)
    grad_w_back = jnp.einsum(
        "rf,rd->fd", activated, round_summed, preferred_element_type=jnp.float32
    )
    grad_w_in = jnp.einsum("rd,rf->df", hidden_low, grad_inner, preferred_element_type=jnp.float32)
    grad_b_in = jnp.sum(grad_inner.astype(jnp.float32), axis=0)
    ffn_grads = (grad_w_in, grad_b_in, grad_w_back, grad_b_back, grad_gain_two, grad_shift_two)
    back_part = jnp.einsum("rf,df->rd", grad_inner, w_in, preferred_element_type=jnp.float32)
    grad_hidden = lax.psum(back_part, "mp") + grad_summed
    grad_gain_one = own_cols(jnp.sum(grad_hidden * normed_one, axis=0))
    grad_shift_one = own_cols(jnp.sum(grad_hidden, axis=0))
    grad_attended = normalize_back(grad_hidden, normed_one, inv_std_one, full_gain_one)
    grad_b_out = own_cols(jnp.sum(grad_attended, axis=0))
    own_attended = own_cols(grad_attended)
    round_attended = grad_attended.astype(jnp.bfloat16)
    grad_w_out = jnp.einsum(
        "rc,rd->cd", context, round_attended, preferred_element_type=jnp.float32
    )
    grad_context = (
        jnp.einsum("rd,cd->rc", round_attended, w_out, preferred_element_type=jnp.float32)
        .astype(jnp.bfloat16)
        .reshape(head_shape)
    )

    def attend_back(packed):
        page_queries, page_keys, page_values, page_valid, page_total, page_grad = packed
        scores = masked_scores(page_queries, page_keys, page_valid)
        probabilities = jnp.exp(scores - page_total[..., None])
        weights = probabilities.astype(jnp.bfloat16)
        grad_values = jnp.einsum(
            "hqk,qhd->khd", weights, page_grad, preferred_element_type=jnp.float32
        )
        grad_weights = jnp.einsum(
            "qhd,khd->hqk", page_grad, page_values, preferred_element_type=jnp.float32
        )
        grad_scores = (
            probabilities
            * (grad_weights - jnp.sum(probabilities * grad_weights, axis=-1, keepdims=True))
        ).astype(jnp.bfloat16)
        grad_queries = (
            jnp.einsum("hqk,khd->qhd", grad_scores, page_keys, preferred_element_type=jnp.float32)
            * score_scale
        )
        grad_keys = (
            jnp.einsum(
                "hqk,qhd->khd", grad_scores, page_queries, preferred_element_type=jnp.float32
            )
            * score_scale
        )
        return (
            grad_queries.astype(jnp.bfloat16),
            grad_keys.astype(jnp.bfloat16),
            grad_values.astype(jnp.bfloat16),
        )

    grad_queries, grad_keys, grad_values = lax.map(
        attend_back, (queries, keys_all, values, key_valid, log_total, grad_context)
    )
    grad_queries = grad_queries.reshape(token_count, local_heads * head_size)
    grad_keys = grad_keys.reshape(token_count, local_heads * head_size)
    grad_values = grad_values.reshape(token_count, local_heads * head_size)
    grad_w_query = jnp.einsum(
        "rd,rc->dc", token_rows, grad_queries, preferred_element_type=jnp.float32
    )
    grad_w_key = jnp.einsum("rd,rc->dc", token_rows, grad_keys, preferred_element_type=jnp.float32)
    grad_w_value = jnp.einsum(
        "rd,rc->dc", token_rows, grad_values, preferred_element_type=jnp.float32
    )
    grad_b_query = jnp.sum(grad_queries.astype(jnp.float32), axis=0)
    grad_b_value = jnp.sum(grad_values.astype(jnp.float32), axis=0)
    input_part = (
        jnp.einsum("rc,dc->rd", grad_queries, w_query, preferred_element_type=jnp.float32)
        + jnp.einsum("rc,dc->rd", grad_keys, w_key, preferred_element_type=jnp.float32)
        + jnp.einsum("rc,dc->rd", grad_values, w_value, preferred_element_type=jnp.float32)
    )
    input_grad = (
        lax.psum_scatter(
            input_part.astype(jnp.bfloat16), "mp", scatter_dimension=1, tiled=True
        ).astype(jnp.float32)
        + own_attended
    ).astype(jnp.bfloat16)
    all_grads = (
        lax.psum(grad_w_query.astype(jnp.bfloat16), "dp").astype(jnp.float32),
        lax.psum(grad_b_query.astype(jnp.bfloat16), "dp").astype(jnp.float32),
        lax.psum(grad_w_key.astype(jnp.bfloat16), "dp").astype(jnp.float32),
        lax.psum(grad_w_value.astype(jnp.bfloat16), "dp").astype(jnp.float32),
        lax.psum(grad_b_value.astype(jnp.bfloat16), "dp").astype(jnp.float32),
        lax.psum(grad_w_out.astype(jnp.bfloat16), "dp").astype(jnp.float32),
        lax.psum(grad_b_out.astype(jnp.bfloat16), "dp").astype(jnp.float32),
        lax.psum(grad_gain_one.astype(jnp.bfloat16), "dp").astype(jnp.float32),
        lax.psum(grad_shift_one.astype(jnp.bfloat16), "dp").astype(jnp.float32),
        lax.psum(grad_w_in.astype(jnp.bfloat16), "dp").astype(jnp.float32),
        lax.psum(grad_b_in.astype(jnp.bfloat16), "dp").astype(jnp.float32),
        lax.psum(grad_w_back.astype(jnp.bfloat16), "dp").astype(jnp.float32),
        lax.psum(grad_b_back.astype(jnp.bfloat16), "dp").astype(jnp.float32),
        lax.psum(grad_gain_two.astype(jnp.bfloat16), "dp").astype(jnp.float32),
        lax.psum(grad_shift_two.astype(jnp.bfloat16), "dp").astype(jnp.float32),
    )
    attn_grads = all_grads[:9]
    ffn_grads = all_grads[9:]
    return (
        output,
        input_grad,
        attn_grads[0],
        attn_grads[1],
        attn_grads[2],
        attn_grads[3],
        attn_grads[4],
        attn_grads[5],
        attn_grads[6],
        attn_grads[7],
        attn_grads[8],
        ffn_grads[0],
        ffn_grads[1],
        ffn_grads[2],
        ffn_grads[3],
        ffn_grads[4],
        ffn_grads[5],
    )


def solution(mesh):
    placed = (
        P("dp", "mp"),
        P("dp"),
        P(None, "mp"),
        P("mp"),
        P(None, "mp"),
        P(None, "mp"),
        P("mp"),
        P("mp", None),
        P("mp"),
        P("mp"),
        P("mp"),
        P(None, "mp"),
        P("mp"),
        P("mp", None),
        P("mp"),
        P("mp"),
        P("mp"),
        P("dp", "mp"),
    )
    return jax.shard_map(
        on_core if dict(mesh.shape) == {"dp": 16, "mp": 2} else on_device,
        mesh=mesh,
        in_specs=placed,
        out_specs=(
            P("dp", "mp"),
            P("dp", "mp"),
            P(None, "mp"),
            P("mp"),
            P(None, "mp"),
            P(None, "mp"),
            P("mp"),
            P("mp", None),
            P("mp"),
            P("mp"),
            P("mp"),
            P(None, "mp"),
            P("mp"),
            P("mp", None),
            P("mp"),
            P("mp"),
            P("mp"),
        ),
        check_vma=False,
    )
```

```python
import functools

import jax
import jax.numpy as jnp
from jax import lax
from jax.experimental import pallas as pl
from jax.experimental.pallas import tpu as pltpu
from jax.sharding import PartitionSpec as P

MESH = pl.DeviceIdType.MESH
HDIM = 64
eps = 1e-05
LOG2_E = 1.4426950408889634
CDF_TERMS = (
    7.97884941e-01, 3.63330844e-02, -3.25946972e-05, -5.53063392e-05, 3.96477773e-06, -1.32266680e-07, 1.75628964e-09,
)


QUARTER = 16
CHUNK = 4 * QUARTER
PAIR = 2 * CHUNK
BLOCK = 4 * PAIR
SLOTS = (6, 6, 4, 6, 8, 6, 4, 6, 10)
KEEP_SLOTS = 4
HOPS = (3, 2, 2, 2, 2, 2, 2, 2, 3)


def rows_at(start, size):
    return pl.ds(pl.multiple_of(start, QUARTER), size)


def chip_sum(pairs, grads, out, lands, ssem, rsem, osem):
    dp = lax.axis_index("dp")
    mp = lax.axis_index("mp")
    z, y, x = dp // 4, (dp // 2) % 2, dp % 2
    inner = (z == 1) | (z == 2)
    outer = jnp.logical_not(inner)
    upper = z >= 2
    cols = grads.shape[1] // 4

    def chip(cz, cy, cx):
        return (cz * 4 + cy * 2 + cx, mp)

    first_peer = (chip(z, y, 1 - x), chip(z, 1 - y, x))
    second_peer = (chip(z, 1 - y, x), chip(z, y, 1 - x))
    side = (x, y)
    inward = chip(jnp.where(z == 0, 1, 2), y, x)
    outward = chip(jnp.where(z == 1, 0, 3), y, x)
    across = chip(3 - z, y, x)
    twin = (dp, 1 - mp)

    line_peer = chip(z + 1 - 2 * lax.rem(z, 2), y, x)

    def meet():
        barrier = pltpu.get_barrier_semaphore()
        for peer in first_peer + (twin, line_peer, across):
            pl.semaphore_signal(barrier, 1, device_id=peer, device_id_type=MESH)
        pl.semaphore_wait(barrier, 5)

    def at_cols(start, count):
        return pl.ds(pl.multiple_of(start * cols, cols), count * cols)

    mine = at_cols(z, 1)
    three = at_cols(jnp.where(upper, 0, 1), 3)
    near_two = at_cols(jnp.where(upper, 2, 0), 2)
    far_two = at_cols(jnp.where(upper, 0, 2), 2)
    end_one = at_cols(jnp.where(upper, 3, 0), 1)

    def half(ref, kind, k, which):
        return ref.at[rows_at(k * PAIR + kind * CHUNK + which * 2 * QUARTER, 2 * QUARTER)]

    def own(kind, k):
        return half(grads, kind, k, side[kind])

    def own_out(kind, k):
        return half(out, kind, k, side[kind])

    def keep(kind, k):
        return pltpu.make_async_copy(
            own(kind, k).at[:, mine], own_out(kind, k).at[:, mine], osem.at[kind, lax.rem(k, KEEP_SLOTS)]
        )

    def land(stage, kind, k):
        return lands[stage].at[lax.rem(k, SLOTS[stage]), kind]

    def send(stage, kind, k, source, target, peer):
        slot = sum(SLOTS[:stage]) + lax.rem(k, SLOTS[stage])
        return pltpu.make_async_remote_copy(
            source,
            target,
            ssem.at[kind, slot],
            rsem.at[kind, slot],
            device_id=peer,
            device_id_type=MESH,
        )

    def scatter_first(kind, k):
        return send(0, kind, k, half(grads, kind, k, 1 - side[kind]), land(0, kind, k), first_peer[kind])

    def go_in(kind, k):
        return send(1, kind, k, own(kind, k).at[:, three], land(1, kind, k).at[:, three], inward)

    def go_across(kind, k):
        return send(2, kind, k, own(kind, k).at[:, far_two], land(2, kind, k), across)

    def go_out(kind, k):
        return send(3, kind, k, own(kind, k).at[:, end_one], land(3, kind, k), outward)

    def swap_second(kind, k):
        return send(4, kind, k, own(kind, k).at[:, mine], land(4, kind, k), second_peer[kind])

    def back_in(kind, k):
        return send(5, kind, k, own_out(kind, k).at[:, mine], own_out(kind, k).at[:, mine], inward)

    def back_across(kind, k):
        return send(6, kind, k, own_out(kind, k).at[:, near_two], own_out(kind, k).at[:, near_two], across)

    def back_out(kind, k):
        return send(7, kind, k, own_out(kind, k).at[:, three], own_out(kind, k).at[:, three], outward)

    def gather_first(kind, k):
        return send(8, kind, k, own_out(kind, k), own_out(kind, k), first_peer[kind])

    offsets = [0]
    for hop in HOPS:
        offsets.append(offsets[-1] + hop)

    def step(t):
        ks = [t - offset for offset in offsets]
        live = [(k >= 0) & (k < pairs) for k in ks]

        def when(n, who=None):
            return pl.when(live[n] if who is None else live[n] & who)

        @when(9)
        def _():
            for kind in (0, 1):
                gather_first(kind, ks[9]).wait()

        @when(8, inner)
        def _():
            for kind in (0, 1):
                back_out(kind, ks[8]).wait_send()

        @when(8, outer)
        def _():
            for kind in (0, 1):
                back_out(kind, ks[8]).wait_recv()
                gather_first(kind, ks[8]).start()

        @when(7, inner)
        def _():
            for kind in (0, 1):
                back_across(kind, ks[7]).wait()
                back_out(kind, ks[7]).start()
                gather_first(kind, ks[7]).start()

        @when(6, inner)
        def _():
            for kind in (0, 1):
                back_in(kind, ks[6]).wait_recv()
                keep(kind, ks[6]).wait()
                back_across(kind, ks[6]).start()

        @when(6, outer)
        def _():
            for kind in (0, 1):
                back_in(kind, ks[6]).wait_send()

        @when(5)
        def _():
            for kind in (0, 1):
                swap_second(kind, ks[5]).wait()
                add_into(own(kind, ks[5]).at[:, mine], land(4, kind, ks[5]))
                keep(kind, ks[5]).start()

        @when(5, outer)
        def _():
            for kind in (0, 1):
                keep(kind, ks[5]).wait()
                back_in(kind, ks[5]).start()

        @when(4, outer)
        def _():
            for kind in (0, 1):
                go_out(kind, ks[4]).wait_recv()
                add_into(own(kind, ks[4]).at[:, mine], land(3, kind, ks[4]))
                swap_second(kind, ks[4]).start()

        @when(4, inner)
        def _():
            for kind in (0, 1):
                go_out(kind, ks[4]).wait_send()

        @when(3, inner)
        def _():
            for kind in (0, 1):
                go_across(kind, ks[3]).wait()
                add_into(own(kind, ks[3]).at[:, near_two], land(2, kind, ks[3]))
                go_out(kind, ks[3]).start()
                swap_second(kind, ks[3]).start()

        @when(2, inner)
        def _():
            for kind in (0, 1):
                go_in(kind, ks[2]).wait_recv()
                add_into(own(kind, ks[2]).at[:, three], land(1, kind, ks[2]).at[:, three])
                go_across(kind, ks[2]).start()

        @when(2, outer)
        def _():
            for kind in (0, 1):
                go_in(kind, ks[2]).wait_send()

        @when(1)
        def _():
            for kind in (0, 1):
                scatter_first(kind, ks[1]).wait()
                add_into(own(kind, ks[1]), land(0, kind, ks[1]))

        @when(1, outer)
        def _():
            for kind in (0, 1):
                go_in(kind, ks[1]).start()

        @when(0)
        def _():
            for kind in (0, 1):
                scatter_first(kind, ks[0]).start()

    return meet, step, pairs + offsets[-1], (twin,) + first_peer + (line_peer, across)


def add_into(target, arrived):
    total = target[...].astype(jnp.float32) + arrived[...].astype(jnp.float32)
    target[...] = total.astype(jnp.bfloat16)


def land_shapes(full):
    two = 2 * QUARTER
    wide = (full, full, full // 2, full // 4, full // 4)
    return [pltpu.VMEM((slots, 2, two, n), jnp.bfloat16) for slots, n in zip(SLOTS, wide)]


def dot_tn(left, right):
    return lax.dot_general(left, right, (((0,), (0,)), ((), ())), preferred_element_type=jnp.float32)


def dot_nt(left, right):
    return lax.dot_general(left, right, (((1,), (1,)), ((), ())), preferred_element_type=jnp.float32)


def gelu_and_slope(v):
    square = v * v
    q = CDF_TERMS[-1] * square + CDF_TERMS[-2]
    for term in CDF_TERMS[-3::-1]:
        q = q * square + term
    cdf = 0.5 * jnp.tanh(v * q) + 0.5
    pdf = jnp.exp2(square * (-0.5 * LOG2_E)) * 0.3989422804014327
    return v * cdf, cdf + v * pdf


def lane_of(rows):
    return lax.broadcasted_iota(jnp.int32, (rows, 128), 1)


def spread_lanes(value, lane, other):
    first = value.astype(jnp.bfloat16)
    rest = value - first.astype(jnp.float32)
    second = rest.astype(jnp.bfloat16)
    third = (rest - second.astype(jnp.float32)).astype(jnp.bfloat16)
    at = lane % 64
    return jnp.where(at == 0, first, jnp.where(at == 1, second, jnp.where(at == 2, third, other)))


def key_lanes(length, rows):
    lane = lane_of(rows) % 64
    slot = lax.broadcasted_iota(jnp.int32, (rows, 128), 0)
    bias = jnp.where(slot < length, 0.0, -1e30)
    return jnp.where(lane < 3, 1.0, jnp.where(lane == 3, bias, 0.0)).astype(jnp.bfloat16)


def layer_kernel(
    inputs, cotangent, w_q, w_k, w_v, w_o, w_in, w_back,
    b_q, b_v, b_in, b_o, g_one, s_one, b_back, g_two, s_two, lens,
    out, vec_out, out_own, out_recv, ig_own, ig_recv, act_hbm, slope_hbm, w_other, w_oo, w_ino, w_backo,
    grads, land_0, land_1, land_2, land_3, land_4, send_t, land_t, vec_sum, vec_land, acc, buf_a, low, buf_c, buf_d, buf_e,
    buf_f, inner_g, qkv, xb, ctx, aux, normed_b, inv_b, vec_own, vec_oth, nat, bias_qkv, bias_ff, bias_in, sums_b, kl,
    ssem, rsem, osem, tsem, trsem, vsem, vrsem, isem, psem, lsem, gsem, xsem, xrsem, fsem, frsem,
):
    dp = lax.axis_index("dp")
    mp = lax.axis_index("mp")
    lands = (land_0, land_1, land_2, land_3, land_4)
    tokens, full = buf_a.shape
    half = full // 2
    tiles = act_hbm.shape[0]
    wide = act_hbm.shape[2]
    part = wide // 2
    seq = kl.shape[0]
    pages = tokens // seq
    pairs = grads.shape[0] // PAIR
    meet, tick, last_tick, swap_peers = chip_sum(pairs, grads, out, lands, ssem, rsem, osem)
    own_cols = pl.ds(pl.multiple_of(mp * half, half), half)
    other_cols = pl.ds(pl.multiple_of((1 - mp) * half, half), half)
    own_tokens = pl.ds(pl.multiple_of(mp * tokens, tokens), tokens)
    other_tokens = pl.ds(pl.multiple_of((1 - mp) * tokens, tokens), tokens)
    twin = (dp, 1 - mp)

    def load(i, src, dst):
        return pltpu.make_async_copy(src, dst, lsem.at[i])

    def give(i, src, dst, sends, gets):
        return pltpu.make_async_remote_copy(
            src, dst, sends.at[i], gets.at[i], device_id=twin, device_id_type=MESH
        )

    def weight_rows(n):
        return pl.ds(n * full, full)

    loads = [load(0, inputs.at[own_tokens], xb.at[:, own_cols])]
    loads += [load(1 + n, w, grads.at[weight_rows(n), pl.ds(0, half)]) for n, w in enumerate((w_q, w_k, w_v))]
    loads += [load(4, w_o, buf_f.at[0]), load(5, cotangent.at[own_tokens], buf_a.at[:, own_cols])]
    for copy in loads:
        copy.start()
    vec_own[...] = jnp.zeros_like(vec_own)
    at_row = 0
    for ref in (b_q, b_v, b_in, b_o, g_one, s_one, b_back, g_two, s_two):
        for c in range(0, ref.shape[0], half):
            vec_own[at_row : at_row + 1, :] = ref[c : c + half].astype(jnp.float32).reshape(1, half)
            at_row += 1
    meet()
    gifts = [
        give(0, inputs.at[other_tokens], xb.at[:, own_cols], xsem, xrsem),
        give(1, vec_own, vec_oth, xsem, xrsem),
    ]
    gifts += [
        give(2 + n, w, grads.at[weight_rows(n), pl.ds(half, half)], xsem, xrsem)
        for n, w in enumerate((w_q, w_k, w_v))
    ]
    gifts += [
        give(5, w_o, buf_f.at[1], xsem, xrsem),
        give(6, cotangent.at[other_tokens], buf_a.at[:, own_cols], xsem, xrsem),
    ]
    for gift in gifts:
        gift.start()

    def ff_gifts(j):
        at = pl.ds(pl.multiple_of(j * part, part), part)
        return (
            pltpu.make_async_remote_copy(
                w_in.at[:, at], w_ino.at[:, at], fsem.at[j, 0], frsem.at[j, 0], device_id=twin, device_id_type=MESH
            ),
            pltpu.make_async_remote_copy(
                w_back.at[at], w_backo.at[at], fsem.at[j, 1], frsem.at[j, 1], device_id=twin, device_id_type=MESH
            ),
        )

    gifts[1].wait_recv()
    nat[:, own_cols] = vec_own[...]
    nat[:, other_cols] = vec_oth[...]
    for n, row in enumerate((0, None, 1)):
        for h, ref in enumerate((vec_own, vec_oth)):
            at = slice(h * half, (h + 1) * half)
            if row is None:
                bias_qkv[n : n + 1, at] = jnp.zeros((1, half), jnp.float32)
            else:
                bias_qkv[n : n + 1, at] = ref[row : row + 1, :]
    for j in range(tiles):
        at = slice((j % 2) * part, (j % 2 + 1) * part)
        row = 2 + j // 2
        bias_ff[j : j + 1, :part] = vec_own[row : row + 1, at]
        bias_ff[j : j + 1, part:] = vec_oth[row : row + 1, at]
    loads[0].wait()
    gifts[0].wait_recv()

    def project(n, h):
        at = slice(h * half, (h + 1) * half)
        made = jnp.dot(xb[...], grads[n * full : (n + 1) * full, at], preferred_element_type=jnp.float32)
        qkv[2 * n + h] = (made + bias_qkv[n : n + 1, at]).astype(jnp.bfloat16)

    for n in range(3):
        loads[1 + n].wait()
        project(n, 0)
    for n in range(3):
        gifts[2 + n].wait_recv()
        project(n, 1)

    def start_gifts(j, carry):
        for gift in ff_gifts(j):
            gift.start()
        return carry

    lax.fori_loop(0, tiles, start_gifts, 0)

    keeps = [load(6 + n, grads.at[weight_rows(n), pl.ds(half, half)], w_other.at[n]) for n in range(3)]
    for copy in keeps:
        copy.start()
    gifts[5].wait_recv()
    keeps.append(load(9, buf_f.at[1], w_oo))
    keeps[3].start()
    loads[4].wait()

    lane = lane_of(seq)
    low_lanes = lane < 64
    high_lanes = lane >= 64
    q_one = jnp.where(lane % 64 == 3, 1.0, 0.0).astype(jnp.bfloat16)

    def pair_forward(i, carry):
        page, pair = i // 8, lax.rem(i, 8)

        @pl.when(pair == 0)
        def _():
            kl[...] = key_lanes(lens[mp * pages + page], seq)

        rows = pl.ds(pl.multiple_of(page * seq, seq), seq)
        side = pair // 4
        cols = pl.ds(pl.multiple_of(lax.rem(pair, 4) * 128, 128), 128)
        kp = qkv[2 + side, rows, cols]
        vp = qkv[4 + side, rows, cols]
        qp = qkv[side, rows, cols] * jnp.bfloat16(0.125)
        one = jnp.ones_like(vp)
        outs = []
        for h in (0, 1):
            mine = low_lanes if h == 0 else jnp.logical_not(low_lanes)
            scores = dot_nt(jnp.where(mine, qp, q_one), jnp.where(mine, kp, kl[...]))
            top = jnp.max(scores, axis=1, keepdims=True)
            weights = jnp.exp(scores - top).astype(jnp.bfloat16)
            outs.append((top, jnp.dot(weights, jnp.where(mine, vp, one), preferred_element_type=jnp.float32)))
        (top0, out0), (top1, out1) = outs
        total = jnp.where(low_lanes, out1, out0)
        value = jnp.where(low_lanes, out0, out1) / pltpu.roll(total, 64, 1)
        neg = -(jnp.where(low_lanes, top1, top0) + jnp.log(total))
        mixed = spread_lanes(neg, lane, q_one)
        ctx[side, rows, cols] = value.astype(jnp.bfloat16)
        aux[side, rows, cols] = mixed
        return carry

    lax.fori_loop(0, 8 * pages, pair_forward, 0)

    def fetch_in(j, slot):
        at = pl.ds(pl.multiple_of(j * part, part), part)
        return [
            pltpu.make_async_copy(w_in.at[:, at], buf_e.at[slot, :, pl.ds(0, part)], isem.at[slot, 2]),
            pltpu.make_async_copy(w_ino.at[:, at], buf_e.at[slot, :, pl.ds(part, part)], isem.at[slot, 3]),
        ]

    def fetch_back(j, slot):
        at = pl.ds(pl.multiple_of(j * part, part), part)
        return [
            pltpu.make_async_copy(w_back.at[at], buf_f.at[slot, pl.ds(0, part)], isem.at[slot, 4]),
            pltpu.make_async_copy(w_backo.at[at], buf_f.at[slot, pl.ds(part, part)], isem.at[slot, 5]),
        ]

    def fetch_made(j, slot):
        return [
            pltpu.make_async_copy(act_hbm.at[j], buf_c.at[slot], isem.at[slot, 0]),
            pltpu.make_async_copy(slope_hbm.at[j], buf_d.at[slot], isem.at[slot, 1]),
        ]

    def start(copies):
        for copy in copies:
            copy.start()

    def finish(copies):
        for copy in copies:
            copy.wait()

    def got_gifts(j):
        for gift in ff_gifts(j):
            gift.wait_recv()

    got_gifts(0)
    start(fetch_in(0, 0))
    step = 256

    def norm_one(i, carry):
        rows = pl.ds(pl.multiple_of(i * step, step), step)
        attended = (
            xb[rows, :].astype(jnp.float32)
            + jnp.dot(ctx[0, rows, :], buf_f[0], preferred_element_type=jnp.float32)
            + jnp.dot(ctx[1, rows, :], buf_f[1], preferred_element_type=jnp.float32)
            + nat[6:7, :]
        )
        average = jnp.mean(attended, axis=1, keepdims=True)
        centred = attended - average
        inv = lax.rsqrt(jnp.mean(centred * centred, axis=1, keepdims=True) + eps)
        normed = centred * inv
        hidden = normed * nat[7:8, :] + nat[8:9, :]
        acc[rows, :] = hidden
        low[rows, :] = hidden.astype(jnp.bfloat16)
        normed_b[rows, :] = normed.astype(jnp.bfloat16)
        inv_b[rows, :] = jnp.broadcast_to(inv, (step, 128))
        return carry

    lax.fori_loop(0, tokens // step, norm_one, 0)
    keeps[3].wait()
    start(fetch_back(0, 0))

    def saves(j, slot):
        return [
            pltpu.make_async_copy(buf_c.at[slot], act_hbm.at[j], psem.at[slot, 0]),
            pltpu.make_async_copy(buf_d.at[slot], slope_hbm.at[j], psem.at[slot, 1]),
        ]

    def forward_tile(j, carry):
        slot = lax.rem(j, 2)

        @pl.when(j + 1 < tiles)
        def _():
            got_gifts(j + 1)
            start(fetch_in(j + 1, 1 - slot) + fetch_back(j + 1, 1 - slot))

        finish(fetch_in(j, slot) + fetch_back(j, slot))

        @pl.when(j >= 2)
        def _():
            finish(saves(j - 2, slot))

        inner = jnp.dot(low[...], buf_e[slot], preferred_element_type=jnp.float32) + bias_ff[pl.ds(j, 1), :]
        value, grad = gelu_and_slope(inner)
        value = value.astype(jnp.bfloat16)
        buf_c[slot] = value
        buf_d[slot] = grad.astype(jnp.bfloat16)
        acc[...] += jnp.dot(value, buf_f[slot], preferred_element_type=jnp.float32)
        start(saves(j, slot))
        return carry

    lax.fori_loop(0, tiles, forward_tile, 0)
    loads[5].wait()
    gifts[6].wait_recv()
    stage_rows = tiles * BLOCK

    def norm_two(i, sums):
        at = pl.multiple_of(i * step, step)
        rows = pl.ds(at, step)
        summed = acc[rows, :] + nat[9:10, :]
        average = jnp.mean(summed, axis=1, keepdims=True)
        centred = summed - average
        inv = lax.rsqrt(jnp.mean(centred * centred, axis=1, keepdims=True) + eps)
        normed = centred * inv
        grads[pl.ds(pl.multiple_of(stage_rows + i * step, step), step), :] = (
            normed * nat[10:11, :] + nat[11:12, :]
        ).astype(jnp.bfloat16)
        page = (i * step) // seq
        slots = lax.broadcasted_iota(jnp.int32, (step, 1), 0) + lax.rem(i * step, seq)
        valid = jnp.where(slots < lens[mp * pages + page], 1.0, 0.0)
        grad = buf_a[rows, :].astype(jnp.float32) * valid
        scaled = grad * nat[10:11, :]
        mean_one = jnp.mean(scaled, axis=1, keepdims=True)
        mean_two = jnp.mean(scaled * normed, axis=1, keepdims=True)
        back = inv * (scaled - mean_one - normed * mean_two)
        acc[rows, :] = back
        buf_a[rows, :] = back.astype(jnp.bfloat16)
        return (
            sums[0] + jnp.sum(back, axis=0, keepdims=True),
            sums[1] + jnp.sum(grad * normed, axis=0, keepdims=True),
            sums[2] + jnp.sum(grad, axis=0, keepdims=True),
        )

    zero = jnp.zeros((1, full), jnp.float32)
    for n, row in enumerate(lax.fori_loop(0, tokens // step, norm_two, (zero, zero, zero))):
        sums_b[n : n + 1, :] = row
    finish(keeps[:3])
    staged = grads.at[pl.ds(stage_rows, tokens)]
    out_keep = pltpu.make_async_copy(staged.at[:, own_cols], out_own, gsem.at[3])
    out_send = pltpu.make_async_remote_copy(
        staged.at[:, other_cols], out_recv, gsem.at[4], gsem.at[5], device_id=twin, device_id_type=MESH
    )
    out_keep.start()
    out_send.start()

    def to_twin(b, which):
        slot = lax.rem(b, 2)
        at = pl.ds(which * part, part)
        return pltpu.make_async_remote_copy(
            send_t.at[slot, at],
            land_t.at[slot, at],
            tsem.at[slot, which],
            trsem.at[slot, which],
            device_id=twin,
            device_id_type=MESH,
        )

    def give_twin(b):
        for which in (0, 1):
            to_twin(b, which).start()

    def gave_twin(b):
        for which in (0, 1):
            to_twin(b, which).wait_send()

    def take_half(b, which):
        to_twin(b, which).wait_recv()
        slot = lax.rem(b, 2)

        def piece(i, carry):
            at = which * part + i * CHUNK
            add_into(grads.at[rows_at(b * BLOCK + at, CHUNK)], land_t.at[slot, rows_at(at, CHUNK)])
            return carry

        lax.fori_loop(0, part // CHUNK, piece, 0)

    def take_twin(b):
        for which in (0, 1):
            take_half(b, which)

    def backward_tile(b, carry):
        j = tiles - 1 - b
        slot = lax.rem(j, 2)
        mate = lax.rem(b, 2)

        @pl.when(b >= 2)
        def _():
            finish(fetch_made(j, slot) + fetch_in(j, slot) + fetch_back(j, slot))
            gave_twin(b - 2)

        base = b * BLOCK
        for c in range(0, full, half):
            made = dot_tn(buf_c[slot], buf_a[:, c : c + half]).astype(jnp.bfloat16)
            grads[rows_at(base, part), c : c + half] = made[:part]
            send_t[mate, :part, c : c + half] = made[part:]

        to_twin(b, 0).start()
        made = dot_nt(buf_a[...], buf_f[slot]) * buf_d[slot].astype(jnp.float32)
        made = made.astype(jnp.bfloat16)
        inner_g[...] = made
        bias_in[pl.ds(j, 1), :] = jnp.sum(made.astype(jnp.float32), axis=0, keepdims=True)

        @pl.when(b >= 1)
        def _():
            take_half(b - 1, 1)
            tick(3 * b - 2)

        acc[...] += dot_nt(inner_g[...], buf_e[slot])
        take_half(b, 0)

        @pl.when(b >= 1)
        def _():
            tick(3 * b - 1)

        for c in range(0, full, part):
            made = dot_tn(low[:, c : c + part], inner_g[...]).astype(jnp.bfloat16)
            grads[rows_at(base + part, part), c : c + part] = made[:, :part]
            send_t[mate, part:, c : c + part] = made[:, part:]

        to_twin(b, 1).start()

        @pl.when(b < 2)
        def _():
            finish(saves(j, slot))

        @pl.when(b < tiles - 2)
        def _():
            start(fetch_made(j - 2, slot) + fetch_in(j - 2, slot) + fetch_back(j - 2, slot))

        tick(3 * b)
        return carry

    lax.fori_loop(0, tiles, backward_tile, 0)
    t = 3 * tiles - 2

    second = [load(10, w_o, buf_f.at[0]), load(11, w_oo, buf_f.at[1])]
    start(second)

    def norm_back(i, sums):
        rows = pl.ds(pl.multiple_of(i * step, step), step)
        grad = acc[rows, :]
        normed = normed_b[rows, :].astype(jnp.float32)
        scaled = grad * nat[7:8, :]
        mean_one = jnp.mean(scaled, axis=1, keepdims=True)
        mean_two = jnp.mean(scaled * normed, axis=1, keepdims=True)
        back = inv_b[rows, 0:1] * (scaled - mean_one - normed * mean_two)
        acc[rows, :] = back
        buf_a[rows, :] = back.astype(jnp.bfloat16)
        return (
            sums[0] + jnp.sum(back, axis=0, keepdims=True),
            sums[1] + jnp.sum(grad * normed, axis=0, keepdims=True),
            sums[2] + jnp.sum(grad, axis=0, keepdims=True),
        )

    bias_o, gain_one, shift_one = lax.fori_loop(0, tokens // step, norm_back, (zero, zero, zero))
    tick(t)

    b = tiles
    gave_twin(b - 2)
    out_keep.wait()
    out_send.wait()
    finish(second)
    for h in (0, 1):
        for c in range(0, full, half):
            made = dot_tn(ctx[h], buf_a[:, c : c + half]).astype(jnp.bfloat16)
            if h == 0:
                grads[b * BLOCK : b * BLOCK + half, c : c + half] = made
            else:
                send_t[b % 2, :, c : c + half] = made
    take_half(b - 1, 1)
    give_twin(b)
    tick(t + 1)
    for h in (0, 1):
        for r in range(0, tokens, half):
            buf_e[h, r : r + half, :] = dot_nt(buf_a[r : r + half, :], buf_f[h]).astype(jnp.bfloat16)
    take_twin(b)
    tick(t + 2)
    t = t + 3

    def pair_backward(i, carry):
        page, pair = i // 8, lax.rem(i, 8)

        @pl.when(pair == 0)
        def _():
            kl[...] = key_lanes(lens[mp * pages + page], seq)

        side = pair // 4
        rows = pl.ds(pl.multiple_of(page * seq, seq), seq)
        cols = pl.ds(pl.multiple_of(lax.rem(pair, 4) * 128, 128), 128)
        qp = qkv[side, rows, cols] * jnp.bfloat16(0.125)
        kp = qkv[2 + side, rows, cols]
        vp = qkv[4 + side, rows, cols]
        extra = aux[side, rows, cols]
        gp = buf_e[side, rows, cols]
        cp = ctx[side, rows, cols]
        none = jnp.zeros_like(gp)
        product = gp.astype(jnp.float32) * cp.astype(jnp.float32)
        sums = [jnp.sum(jnp.where(mine, product, 0.0), axis=1, keepdims=True) for mine in (low_lanes, high_lanes)]
        shift = spread_lanes(-jnp.where(low_lanes, sums[1], sums[0]), lane, none)
        made = []
        for mine in (low_lanes, high_lanes):
            qh = jnp.where(mine, qp, none)
            gh = jnp.where(mine, gp, none)
            probs = jnp.exp(dot_nt(jnp.where(mine, kp, kl[...]), jnp.where(mine, qp, extra)))
            grad_weights = dot_nt(jnp.where(mine, vp, kl[...]), jnp.where(mine, gp, shift))
            grad_scores = (probs * grad_weights).astype(jnp.bfloat16)
            grad_v = jnp.dot(probs.astype(jnp.bfloat16), gh, preferred_element_type=jnp.float32)
            grad_k = jnp.dot(grad_scores, qh, preferred_element_type=jnp.float32)
            grad_q = dot_tn(grad_scores, jnp.where(mine, kp, none))
            made.append((grad_q * 0.125, grad_k, grad_v))
        for n in range(3):
            qkv[2 * n + side, rows, cols] = (made[0][n] + made[1][n]).astype(jnp.bfloat16)

        @pl.when(lax.rem(i, 3) != 2)
        def _():
            tick(t + i - (i + 1) // 3)

        return carry

    lax.fori_loop(0, 8 * pages, pair_backward, 0)
    t = t + 8 * pages - 8 * pages // 3

    third = [load(12, w_q, buf_c.at[0]), load(13, w_k, buf_d.at[0]), load(14, w_v, buf_e.at[0])]
    third += [load(15 + n, w_other.at[n], ref.at[1]) for n, ref in enumerate((buf_c, buf_d, buf_e))]
    start(third)
    b = tiles + 1

    def weights_loop(i, carry):
        at = b + i
        slot = lax.rem(at, 2)
        gave_twin(at - 2)
        for r in range(0, full, half):
            made = dot_tn(xb[:, r : r + half], qkv[2 * i]).astype(jnp.bfloat16)
            grads[rows_at(at * BLOCK, BLOCK), r : r + half] = made
            made = dot_tn(xb[:, r : r + half], qkv[2 * i + 1]).astype(jnp.bfloat16)
            send_t[slot, :, r : r + half] = made

        @pl.when(i >= 1)
        def _():
            take_twin(at - 1)
            tick(t + i - 1)

        give_twin(at)
        return carry

    lax.fori_loop(0, 3, weights_loop, 0)
    t = t + 2
    b = b + 3

    first_core = mp == 0
    owned, others = [], []
    for n in (0, 4):
        owned.append(jnp.sum(qkv[n].astype(jnp.float32), axis=0, keepdims=True))
        others.append(jnp.sum(qkv[n + 1].astype(jnp.float32), axis=0, keepdims=True))
    for row in (bias_o, gain_one, shift_one, sums_b[0:1, :], sums_b[1:2, :], sums_b[2:3, :]):
        owned.append(jnp.where(first_core, row[:, :half], row[:, half:]))
        others.append(jnp.where(first_core, row[:, half:], row[:, :half]))
    for n in range(0, tiles, 2):
        owned.append(jnp.concatenate([bias_in[n : n + 1, :part], bias_in[n + 1 : n + 2, :part]], axis=1))
        others.append(jnp.concatenate([bias_in[n : n + 1, part:], bias_in[n + 1 : n + 2, part:]], axis=1))
    fill = jnp.zeros((QUARTER - len(owned), half), jnp.float32)
    vec_sum[0] = jnp.concatenate(others + [fill], axis=0)
    vec_sum[1] = jnp.concatenate(owned + [fill], axis=0)

    def swap_vectors(n):
        return pltpu.make_async_remote_copy(
            vec_sum.at[n], vec_land.at[n], vsem.at[n], vrsem.at[n], device_id=swap_peers[n], device_id_type=MESH
        )

    swap_vectors(0).start()
    take_twin(b - 1)
    gave_twin(b - 2)
    gave_twin(b - 1)
    tick(t)
    finish(third)

    def input_loop(i, carry):
        rows = pl.ds(pl.multiple_of(i * step, step), step)
        total = acc[rows, :]
        for n, ref in enumerate((buf_c, buf_d, buf_e)):
            for h in (0, 1):
                total = total + dot_nt(qkv[2 * n + h, rows, :], ref[h])
        buf_a[rows, :] = total.astype(jnp.bfloat16)
        tick(t + 1 + i)
        return carry

    lax.fori_loop(0, tokens // step, input_loop, 0)
    t = t + 1 + tokens // step
    ig_keep = pltpu.make_async_copy(buf_a.at[:, own_cols], ig_own, gsem.at[0])
    ig_send = pltpu.make_async_remote_copy(
        buf_a.at[:, other_cols], ig_recv, gsem.at[1], gsem.at[2], device_id=twin, device_id_type=MESH
    )
    ig_keep.start()
    ig_send.start()
    for gift in gifts:
        gift.wait_send()

    def end_gifts(j, carry):
        for gift in ff_gifts(j):
            gift.wait_send()
        return carry

    lax.fori_loop(0, tiles, end_gifts, 0)

    def rest(i, carry):
        for n in range(5):

            @pl.when(i == t + 2 * n)
            def _():
                swap_vectors(n).wait()
                total = vec_sum[max(n, 1)] + vec_land[n]
                if n == 4:
                    vec_out[...] = total
                else:
                    vec_sum[n + 1] = total
                    swap_vectors(n + 1).start()

        tick(i)
        return carry

    lax.fori_loop(t, last_tick, rest, 0)
    ig_keep.wait()
    ig_send.wait()


HBM = pl.BlockSpec(memory_space=pltpu.HBM)
VMEM = pl.BlockSpec(memory_space=pltpu.VMEM)
SMEM = pl.BlockSpec(memory_space=pltpu.SMEM)


def shape(dims, dtype=jnp.bfloat16):
    return jax.ShapeDtypeStruct(dims, dtype)


def run_layer(inputs, cotangent, w_q, w_k, w_v, w_o, w_in, w_back, vectors, lengths):
    tokens = inputs.shape[0] // 2
    half = inputs.shape[1]
    full = 2 * half
    seq = inputs.shape[0] // lengths.shape[0]
    ff_half = w_in.shape[1]
    tiles = ff_half // (BLOCK // 2)
    wide = BLOCK
    rows = (tiles + 4) * BLOCK
    f32 = jnp.float32
    bf16 = jnp.bfloat16
    return pl.pallas_call(
        layer_kernel,
        name="layer",
        out_shape=(
            shape((rows, full)), shape((QUARTER, half), f32), shape((tokens, half)), shape((tokens, half)),
            shape((tokens, half)), shape((tokens, half)), shape((tiles, tokens, wide)), shape((tiles, tokens, wide)),
            shape((3, full, half)), shape((half, full)), shape((full, ff_half)), shape((ff_half, full)),
        ),
        in_specs=[HBM] * 8 + [VMEM] * 9 + [SMEM],
        out_specs=(HBM, VMEM) + (HBM,) * 10,
        scratch_shapes=[
            pltpu.VMEM((rows, full), bf16),
            *land_shapes(full),
            pltpu.VMEM((2, BLOCK, full), bf16),
            pltpu.VMEM((2, BLOCK, full), bf16),
            pltpu.VMEM((6, QUARTER, half), f32),
            pltpu.VMEM((5, QUARTER, half), f32),
            pltpu.VMEM((tokens, full), f32),
            pltpu.VMEM((tokens, full), bf16),
            pltpu.VMEM((tokens, full), bf16),
            pltpu.VMEM((2, tokens, half), bf16),
            pltpu.VMEM((2, tokens, half), bf16),
            pltpu.VMEM((2, tokens, half), bf16),
            pltpu.VMEM((2, half, full), bf16),
            pltpu.VMEM((tokens, wide), bf16),
            pltpu.VMEM((6, tokens, half), bf16),
            pltpu.VMEM((tokens, full), bf16),
            pltpu.VMEM((2, tokens, half), bf16),
            pltpu.VMEM((2, tokens, half), bf16),
            pltpu.VMEM((tokens, full), bf16),
            pltpu.VMEM((tokens, 128), f32),
            pltpu.VMEM((QUARTER, half), f32),
            pltpu.VMEM((QUARTER, half), f32),
            pltpu.VMEM((QUARTER, full), f32),
            pltpu.VMEM((8, full), f32),
            pltpu.VMEM((tiles, wide), f32),
            pltpu.VMEM((tiles, wide), f32),
            pltpu.VMEM((8, full), f32),
            pltpu.VMEM((seq, 128), bf16),
            pltpu.SemaphoreType.DMA((2, sum(SLOTS))),
            pltpu.SemaphoreType.DMA((2, sum(SLOTS))),
            pltpu.SemaphoreType.DMA((2, KEEP_SLOTS)),
            pltpu.SemaphoreType.DMA((2, 2)),
            pltpu.SemaphoreType.DMA((2, 2)),
            pltpu.SemaphoreType.DMA((5,)),
            pltpu.SemaphoreType.DMA((5,)),
            pltpu.SemaphoreType.DMA((2, 6)),
            pltpu.SemaphoreType.DMA((2, 2)),
            pltpu.SemaphoreType.DMA((18,)),
            pltpu.SemaphoreType.DMA((6,)),
            pltpu.SemaphoreType.DMA((7,)),
            pltpu.SemaphoreType.DMA((7,)),
            pltpu.SemaphoreType.DMA((tiles, 2)),
            pltpu.SemaphoreType.DMA((tiles, 2)),
        ],
        compiler_params=pltpu.CompilerParams(
            collective_id=0, has_side_effects=True, vmem_limit_bytes=62 << 20
        ),
    )(inputs, cotangent, w_q, w_k, w_v, w_o, w_in, w_back, *vectors, lengths)


def unpack_kernel(
    packed, out_mine, out_got, ig_mine, ig_got, vectors,
    output, input_grad, g_q, g_k, g_v, g_o, g_in, g_back, v_q, v_v, v_o, v_g1, v_s1, v_b, v_g2, v_s2, v_in,
    loaded, wide, passed, isem, osem, csem,
):
    mp = lax.axis_index("mp")
    tokens, half = out_mine.shape
    mine = pl.ds(pl.multiple_of(mp * tokens, tokens), tokens)
    other = pl.ds(pl.multiple_of((1 - mp) * tokens, tokens), tokens)
    pieces = (
        (out_mine, output.at[mine]),
        (out_got, output.at[other]),
        (ig_mine, input_grad.at[mine]),
        (ig_got, input_grad.at[other]),
    )
    moves = [pltpu.make_async_copy(src, passed.at[i], csem.at[0, i]) for i, (src, _) in enumerate(pieces)]
    leaves = [pltpu.make_async_copy(passed.at[i], dst, csem.at[1, i]) for i, (_, dst) in enumerate(pieces)]
    part = BLOCK // 2
    full = packed.shape[1]
    tiles = g_back.shape[0] // part
    blocks = tiles + 4
    slots = wide.shape[0]

    def fetch(b):
        return pltpu.make_async_copy(packed.at[b * BLOCK : (b + 1) * BLOCK], loaded.at[b], isem.at[b])

    def stores(b):
        ref = wide.at[b % slots]
        j = tiles - 1 - b
        if b < tiles:
            pieces = [(ref.at[:part], g_back.at[j * part : (j + 1) * part])]
            for c in range(0, full, part):
                pieces.append((ref.at[part:, c : c + part], g_in.at[c : c + part, j * part : (j + 1) * part]))
        elif b == tiles:
            pieces = [(ref, g_o)]
        else:
            target = (g_q, g_k, g_v)[b - tiles - 1]
            pieces = [(ref.at[:, :half], target.at[:half]), (ref.at[:, half:], target.at[half:])]
        return [pltpu.make_async_copy(src, dst, osem.at[b % slots, i]) for i, (src, dst) in enumerate(pieces)]

    for b in range(blocks):
        fetch(b).start()
        if b < len(moves):
            moves[b].start()
    for n, ref in enumerate((v_q, v_v, v_o, v_g1, v_s1, v_b, v_g2, v_s2)):
        ref[...] = vectors[n, :]
    for n in range(4):
        v_in[n * half : (n + 1) * half] = vectors[8 + n, :]
    for b in range(blocks):
        fetch(b).wait()
        if b >= slots:
            for store in stores(b - slots):
                store.wait()
        for r in range(0, BLOCK, CHUNK):
            wide[b % slots, r : r + CHUNK, :] = loaded[b, r : r + CHUNK, :].astype(jnp.float32)
        for store in stores(b):
            store.start()
        if b < len(moves):
            moves[b].wait()
            leaves[b].start()
    for b in range(blocks - slots, blocks):
        for store in stores(b):
            store.wait()
    for leave in leaves:
        leave.wait()


def run_unpack(packed, out_mine, out_got, ig_mine, ig_got, vectors, tiles):
    tokens, half = out_mine.shape
    full = 2 * half
    ff_half = tiles * (BLOCK // 2)
    f32 = jnp.float32
    slots = 6
    return pl.pallas_call(
        unpack_kernel,
        name="unpack",
        out_shape=(
            shape((2 * tokens, half)), shape((2 * tokens, half)),
            shape((full, half), f32), shape((full, half), f32), shape((full, half), f32), shape((half, full), f32),
            shape((full, ff_half), f32), shape((ff_half, full), f32),
            *[shape((half,), f32)] * 8, shape((ff_half,), f32),
        ),
        in_specs=[HBM] * 5 + [VMEM],
        out_specs=(HBM,) * 8 + (VMEM,) * 9,
        scratch_shapes=[
            pltpu.VMEM((tiles + 4, BLOCK, full), jnp.bfloat16),
            pltpu.VMEM((slots, BLOCK, full), f32),
            pltpu.VMEM((4, tokens, half), jnp.bfloat16),
            pltpu.SemaphoreType.DMA((tiles + 4,)),
            pltpu.SemaphoreType.DMA((slots, 5)),
            pltpu.SemaphoreType.DMA((2, 4)),
        ],
        compiler_params=pltpu.CompilerParams(vmem_limit_bytes=60 << 20),
    )(packed, out_mine, out_got, ig_mine, ig_got, vectors)


def on_core(
    inputs, lengths, w_query, b_query, w_key, w_value, b_value, w_out, b_out, gain_one, shift_one, w_in, b_in, w_back,
    b_back, gain_two, shift_two, cotangent,
):
    tiles = w_in.shape[1] // (BLOCK // 2)
    given = (b_query, b_value, b_in, b_out, gain_one, shift_one, b_back, gain_two, shift_two)
    packed, vectors, out_mine, out_got, ig_mine, ig_got, *_ = run_layer(
        inputs, cotangent, w_query, w_key, w_value, w_out, w_in, w_back, given, lengths
    )
    output, input_grad, g_q, g_k, g_v, g_o, g_in, g_back, *v = run_unpack(
        packed, out_mine, out_got, ig_mine, ig_got, vectors, tiles
    )
    return (
        output, input_grad, g_q, v[0], g_k, g_v, v[1], g_o, v[2], v[3], v[4], g_in, v[8], g_back, v[5], v[6], v[7],
    )


def gelu_exact(ffn_inner):
    return jax.nn.gelu(ffn_inner, approximate=False)


def normalize_rows(summed, gain_vec, shift_vec):
    average = jnp.mean(summed, axis=-1, keepdims=True)
    centred = summed - average
    inv_std = lax.rsqrt(jnp.mean(centred * centred, axis=-1, keepdims=True) + eps)
    normed = centred * inv_std
    return (normed * gain_vec + shift_vec, normed, inv_std)


def normalize_back(grad_out, normed, inv_std, gain_vec):
    scaled = grad_out * gain_vec
    centred = scaled - jnp.mean(scaled, axis=-1, keepdims=True)
    return inv_std * (centred - normed * jnp.mean(scaled * normed, axis=-1, keepdims=True))


def on_device(
    inputs,
    lengths,
    w_query,
    b_query,
    w_key,
    w_value,
    b_value,
    w_out,
    b_out,
    gain_one,
    shift_one,
    w_in,
    b_in,
    w_back,
    b_back,
    gain_two,
    shift_two,
    cotangent,
):
    token_count, part_cols = inputs.shape
    page_count = lengths.shape[0]
    seq_len = token_count // page_count
    head_size = HDIM
    local_heads = w_query.shape[1] // head_size
    score_scale = head_size ** (-0.5)
    offset = lax.axis_index("mp") * part_cols

    def own_cols(full_array):
        return lax.dynamic_slice_in_dim(full_array, offset, part_cols, full_array.ndim - 1)

    vectors = jnp.stack([b_out, gain_one, shift_one, b_back, gain_two, shift_two])
    token_rows, vector_rows = (
        lax.all_gather(inputs, "mp", axis=1, tiled=True),
        lax.all_gather(vectors, "mp", axis=1, tiled=True),
    )
    vector_rows = vector_rows.astype(jnp.float32)
    full_b_out, full_gain_one, full_shift_one = (vector_rows[0], vector_rows[1], vector_rows[2])
    full_b_back, full_gain_two, full_shift_two = (vector_rows[3], vector_rows[4], vector_rows[5])
    positions = jnp.arange(seq_len, dtype=jnp.int32)
    key_valid = positions[None, :] < lengths[:, None]
    row_valid = key_valid.reshape(token_count, 1).astype(jnp.float32)
    head_shape = (page_count, seq_len, local_heads, head_size)
    queries = (
        (
            jnp.dot(token_rows, w_query, preferred_element_type=jnp.float32)
            + b_query.astype(jnp.float32)
        )
        .astype(jnp.bfloat16)
        .reshape(head_shape)
    )
    keys_all = (
        jnp.dot(token_rows, w_key, preferred_element_type=jnp.float32)
        .astype(jnp.bfloat16)
        .reshape(head_shape)
    )
    values = (
        (
            jnp.dot(token_rows, w_value, preferred_element_type=jnp.float32)
            + b_value.astype(jnp.float32)
        )
        .astype(jnp.bfloat16)
        .reshape(head_shape)
    )

    def masked_scores(page_queries, page_keys, page_valid):
        scores = (
            jnp.einsum("qhd,khd->hqk", page_queries, page_keys, preferred_element_type=jnp.float32)
            * score_scale
        )
        return jnp.where(page_valid[None, None, :], scores, -1e30)

    def attend(packed):
        page_queries, page_keys, page_values, page_valid = packed
        scores = masked_scores(page_queries, page_keys, page_valid)
        row_max = jnp.max(scores, axis=-1, keepdims=True)
        shifted = jnp.exp(scores - row_max)
        row_sum = jnp.sum(shifted, axis=-1, keepdims=True)
        weights = (shifted / row_sum).astype(jnp.bfloat16)
        context = jnp.einsum(
            "hqk,khd->qhd", weights, page_values, preferred_element_type=jnp.float32
        )
        return (context.astype(jnp.bfloat16), (row_max + jnp.log(row_sum))[..., 0])

    context, log_total = lax.map(attend, (queries, keys_all, values, key_valid))
    context = context.reshape(token_count, local_heads * head_size)
    attn_part = jnp.dot(context, w_out, preferred_element_type=jnp.float32)
    attended = token_rows.astype(jnp.float32) + lax.psum(attn_part, "mp") + full_b_out
    hidden_one, normed_one, inv_std_one = normalize_rows(attended, full_gain_one, full_shift_one)
    hidden_low = hidden_one.astype(jnp.bfloat16)
    ffn_inner = jnp.dot(hidden_low, w_in, preferred_element_type=jnp.float32) + b_in.astype(
        jnp.float32
    )
    gelu_value, gelu_pull = jax.vjp(gelu_exact, ffn_inner)
    activated = gelu_value.astype(jnp.bfloat16)
    ffn_part = jnp.dot(activated, w_back, preferred_element_type=jnp.float32)
    summed = hidden_one + lax.psum(ffn_part, "mp") + full_b_back
    out_full, normed_two, inv_std_two = normalize_rows(summed, full_gain_two, full_shift_two)
    output = own_cols(out_full).astype(jnp.bfloat16)
    grad_out = lax.all_gather(cotangent, "mp", axis=1, tiled=True).astype(jnp.float32) * row_valid
    grad_summed = normalize_back(grad_out, normed_two, inv_std_two, full_gain_two)
    grad_gain_two = own_cols(jnp.sum(grad_out * normed_two, axis=0))
    grad_shift_two = own_cols(jnp.sum(grad_out, axis=0))
    grad_b_back = own_cols(jnp.sum(grad_summed, axis=0))
    round_summed = grad_summed.astype(jnp.bfloat16)
    grad_act = jnp.einsum("rd,fd->rf", round_summed, w_back, preferred_element_type=jnp.float32)
    grad_inner = gelu_pull(grad_act)[0].astype(jnp.bfloat16)
    grad_w_back = jnp.einsum(
        "rf,rd->fd", activated, round_summed, preferred_element_type=jnp.float32
    )
    grad_w_in = jnp.einsum("rd,rf->df", hidden_low, grad_inner, preferred_element_type=jnp.float32)
    grad_b_in = jnp.sum(grad_inner.astype(jnp.float32), axis=0)
    ffn_grads = (grad_w_in, grad_b_in, grad_w_back, grad_b_back, grad_gain_two, grad_shift_two)
    back_part = jnp.einsum("rf,df->rd", grad_inner, w_in, preferred_element_type=jnp.float32)
    grad_hidden = lax.psum(back_part, "mp") + grad_summed
    grad_gain_one = own_cols(jnp.sum(grad_hidden * normed_one, axis=0))
    grad_shift_one = own_cols(jnp.sum(grad_hidden, axis=0))
    grad_attended = normalize_back(grad_hidden, normed_one, inv_std_one, full_gain_one)
    grad_b_out = own_cols(jnp.sum(grad_attended, axis=0))
    own_attended = own_cols(grad_attended)
    round_attended = grad_attended.astype(jnp.bfloat16)
    grad_w_out = jnp.einsum(
        "rc,rd->cd", context, round_attended, preferred_element_type=jnp.float32
    )
    grad_context = (
        jnp.einsum("rd,cd->rc", round_attended, w_out, preferred_element_type=jnp.float32)
        .astype(jnp.bfloat16)
        .reshape(head_shape)
    )

    def attend_back(packed):
        page_queries, page_keys, page_values, page_valid, page_total, page_grad = packed
        scores = masked_scores(page_queries, page_keys, page_valid)
        probabilities = jnp.exp(scores - page_total[..., None])
        weights = probabilities.astype(jnp.bfloat16)
        grad_values = jnp.einsum(
            "hqk,qhd->khd", weights, page_grad, preferred_element_type=jnp.float32
        )
        grad_weights = jnp.einsum(
            "qhd,khd->hqk", page_grad, page_values, preferred_element_type=jnp.float32
        )
        grad_scores = (
            probabilities
            * (grad_weights - jnp.sum(probabilities * grad_weights, axis=-1, keepdims=True))
        ).astype(jnp.bfloat16)
        grad_queries = (
            jnp.einsum("hqk,khd->qhd", grad_scores, page_keys, preferred_element_type=jnp.float32)
            * score_scale
        )
        grad_keys = (
            jnp.einsum(
                "hqk,qhd->khd", grad_scores, page_queries, preferred_element_type=jnp.float32
            )
            * score_scale
        )
        return (
            grad_queries.astype(jnp.bfloat16),
            grad_keys.astype(jnp.bfloat16),
            grad_values.astype(jnp.bfloat16),
        )

    grad_queries, grad_keys, grad_values = lax.map(
        attend_back, (queries, keys_all, values, key_valid, log_total, grad_context)
    )
    grad_queries = grad_queries.reshape(token_count, local_heads * head_size)
    grad_keys = grad_keys.reshape(token_count, local_heads * head_size)
    grad_values = grad_values.reshape(token_count, local_heads * head_size)
    grad_w_query = jnp.einsum(
        "rd,rc->dc", token_rows, grad_queries, preferred_element_type=jnp.float32
    )
    grad_w_key = jnp.einsum("rd,rc->dc", token_rows, grad_keys, preferred_element_type=jnp.float32)
    grad_w_value = jnp.einsum(
        "rd,rc->dc", token_rows, grad_values, preferred_element_type=jnp.float32
    )
    grad_b_query = jnp.sum(grad_queries.astype(jnp.float32), axis=0)
    grad_b_value = jnp.sum(grad_values.astype(jnp.float32), axis=0)
    input_part = (
        jnp.einsum("rc,dc->rd", grad_queries, w_query, preferred_element_type=jnp.float32)
        + jnp.einsum("rc,dc->rd", grad_keys, w_key, preferred_element_type=jnp.float32)
        + jnp.einsum("rc,dc->rd", grad_values, w_value, preferred_element_type=jnp.float32)
    )
    input_grad = (
        lax.psum_scatter(
            input_part.astype(jnp.bfloat16), "mp", scatter_dimension=1, tiled=True
        ).astype(jnp.float32)
        + own_attended
    ).astype(jnp.bfloat16)
    all_grads = (
        lax.psum(grad_w_query.astype(jnp.bfloat16), "dp").astype(jnp.float32),
        lax.psum(grad_b_query.astype(jnp.bfloat16), "dp").astype(jnp.float32),
        lax.psum(grad_w_key.astype(jnp.bfloat16), "dp").astype(jnp.float32),
        lax.psum(grad_w_value.astype(jnp.bfloat16), "dp").astype(jnp.float32),
        lax.psum(grad_b_value.astype(jnp.bfloat16), "dp").astype(jnp.float32),
        lax.psum(grad_w_out.astype(jnp.bfloat16), "dp").astype(jnp.float32),
        lax.psum(grad_b_out.astype(jnp.bfloat16), "dp").astype(jnp.float32),
        lax.psum(grad_gain_one.astype(jnp.bfloat16), "dp").astype(jnp.float32),
        lax.psum(grad_shift_one.astype(jnp.bfloat16), "dp").astype(jnp.float32),
        lax.psum(grad_w_in.astype(jnp.bfloat16), "dp").astype(jnp.float32),
        lax.psum(grad_b_in.astype(jnp.bfloat16), "dp").astype(jnp.float32),
        lax.psum(grad_w_back.astype(jnp.bfloat16), "dp").astype(jnp.float32),
        lax.psum(grad_b_back.astype(jnp.bfloat16), "dp").astype(jnp.float32),
        lax.psum(grad_gain_two.astype(jnp.bfloat16), "dp").astype(jnp.float32),
        lax.psum(grad_shift_two.astype(jnp.bfloat16), "dp").astype(jnp.float32),
    )
    attn_grads = all_grads[:9]
    ffn_grads = all_grads[9:]
    return (
        output,
        input_grad,
        attn_grads[0],
        attn_grads[1],
        attn_grads[2],
        attn_grads[3],
        attn_grads[4],
        attn_grads[5],
        attn_grads[6],
        attn_grads[7],
        attn_grads[8],
        ffn_grads[0],
        ffn_grads[1],
        ffn_grads[2],
        ffn_grads[3],
        ffn_grads[4],
        ffn_grads[5],
    )


def solution(mesh):
    placed = (
        P("dp", "mp"),
        P("dp"),
        P(None, "mp"),
        P("mp"),
        P(None, "mp"),
        P(None, "mp"),
        P("mp"),
        P("mp", None),
        P("mp"),
        P("mp"),
        P("mp"),
        P(None, "mp"),
        P("mp"),
        P("mp", None),
        P("mp"),
        P("mp"),
        P("mp"),
        P("dp", "mp"),
    )
    return jax.shard_map(
        on_core if dict(mesh.shape) == {"dp": 16, "mp": 2} else on_device,
        mesh=mesh,
        in_specs=placed,
        out_specs=(
            P("dp", "mp"),
            P("dp", "mp"),
            P(None, "mp"),
            P("mp"),
            P(None, "mp"),
            P(None, "mp"),
            P("mp"),
            P("mp", None),
            P("mp"),
            P("mp"),
            P("mp"),
            P(None, "mp"),
            P("mp"),
            P("mp", None),
            P("mp"),
            P("mp"),
            P("mp"),
        ),
        check_vma=False,
    )
```

```python
import functools

import jax
import jax.numpy as jnp
from jax import lax
from jax.experimental import pallas as pl
from jax.experimental.pallas import tpu as pltpu
from jax.sharding import PartitionSpec as P

MESH = pl.DeviceIdType.MESH
HDIM = 64
eps = 1e-05
LOG2_E = 1.4426950408889634
CDF_TERMS = (
    7.97884941e-01, 3.63330844e-02, -3.25946972e-05, -5.53063392e-05, 3.96477773e-06, -1.32266680e-07, 1.75628964e-09,
)


QUARTER = 16
CHUNK = 4 * QUARTER
PAIR = 2 * CHUNK
BLOCK = 4 * PAIR
SLOTS = (6, 6, 4, 6, 8, 6, 4, 6, 10)
KEEP_SLOTS = 4
HOPS = (3, 2, 2, 2, 2, 2, 2, 2, 3)


def rows_at(start, size):
    return pl.ds(pl.multiple_of(start, QUARTER), size)


def chip_sum(pairs, grads, out, lands, ssem, rsem, osem):
    dp = lax.axis_index("dp")
    mp = lax.axis_index("mp")
    z, y, x = dp // 4, (dp // 2) % 2, dp % 2
    inner = (z == 1) | (z == 2)
    outer = jnp.logical_not(inner)
    upper = z >= 2
    cols = grads.shape[1] // 4

    def chip(cz, cy, cx):
        return (cz * 4 + cy * 2 + cx, mp)

    first_peer = (chip(z, y, 1 - x), chip(z, 1 - y, x))
    second_peer = (chip(z, 1 - y, x), chip(z, y, 1 - x))
    side = (x, y)
    inward = chip(jnp.where(z == 0, 1, 2), y, x)
    outward = chip(jnp.where(z == 1, 0, 3), y, x)
    across = chip(3 - z, y, x)
    twin = (dp, 1 - mp)

    line_peer = chip(z + 1 - 2 * lax.rem(z, 2), y, x)

    def meet():
        barrier = pltpu.get_barrier_semaphore()
        for peer in first_peer + (twin, line_peer, across):
            pl.semaphore_signal(barrier, 1, device_id=peer, device_id_type=MESH)
        pl.semaphore_wait(barrier, 5)

    def at_cols(start, count):
        return pl.ds(pl.multiple_of(start * cols, cols), count * cols)

    mine = at_cols(z, 1)
    three = at_cols(jnp.where(upper, 0, 1), 3)
    near_two = at_cols(jnp.where(upper, 2, 0), 2)
    far_two = at_cols(jnp.where(upper, 0, 2), 2)
    end_one = at_cols(jnp.where(upper, 3, 0), 1)

    def half(ref, kind, k, which):
        return ref.at[rows_at(k * PAIR + kind * CHUNK + which * 2 * QUARTER, 2 * QUARTER)]

    def own(kind, k):
        return half(grads, kind, k, side[kind])

    def own_out(kind, k):
        return half(out, kind, k, side[kind])

    def keep(kind, k):
        return pltpu.make_async_copy(
            own(kind, k).at[:, mine], own_out(kind, k).at[:, mine], osem.at[kind, lax.rem(k, KEEP_SLOTS)]
        )

    def land(stage, kind, k):
        return lands[stage].at[lax.rem(k, SLOTS[stage]), kind]

    def send(stage, kind, k, source, target, peer):
        slot = sum(SLOTS[:stage]) + lax.rem(k, SLOTS[stage])
        return pltpu.make_async_remote_copy(
            source,
            target,
            ssem.at[kind, slot],
            rsem.at[kind, slot],
            device_id=peer,
            device_id_type=MESH,
        )

    def scatter_first(kind, k):
        return send(0, kind, k, half(grads, kind, k, 1 - side[kind]), land(0, kind, k), first_peer[kind])

    def go_in(kind, k):
        return send(1, kind, k, own(kind, k).at[:, three], land(1, kind, k).at[:, three], inward)

    def go_across(kind, k):
        return send(2, kind, k, own(kind, k).at[:, far_two], land(2, kind, k), across)

    def go_out(kind, k):
        return send(3, kind, k, own(kind, k).at[:, end_one], land(3, kind, k), outward)

    def swap_second(kind, k):
        return send(4, kind, k, own(kind, k).at[:, mine], land(4, kind, k), second_peer[kind])

    def back_in(kind, k):
        return send(5, kind, k, own_out(kind, k).at[:, mine], own_out(kind, k).at[:, mine], inward)

    def back_across(kind, k):
        return send(6, kind, k, own_out(kind, k).at[:, near_two], own_out(kind, k).at[:, near_two], across)

    def back_out(kind, k):
        return send(7, kind, k, own_out(kind, k).at[:, three], own_out(kind, k).at[:, three], outward)

    def gather_first(kind, k):
        return send(8, kind, k, own_out(kind, k), own_out(kind, k), first_peer[kind])

    offsets = [0]
    for hop in HOPS:
        offsets.append(offsets[-1] + hop)

    def step(t):
        ks = [t - offset for offset in offsets]
        live = [(k >= 0) & (k < pairs) for k in ks]

        def when(n, who=None):
            return pl.when(live[n] if who is None else live[n] & who)

        @when(9)
        def _():
            for kind in (0, 1):
                gather_first(kind, ks[9]).wait()

        @when(8, inner)
        def _():
            for kind in (0, 1):
                back_out(kind, ks[8]).wait_send()

        @when(8, outer)
        def _():
            for kind in (0, 1):
                back_out(kind, ks[8]).wait_recv()
                gather_first(kind, ks[8]).start()

        @when(7, inner)
        def _():
            for kind in (0, 1):
                back_across(kind, ks[7]).wait()
                back_out(kind, ks[7]).start()
                gather_first(kind, ks[7]).start()

        @when(6, inner)
        def _():
            for kind in (0, 1):
                back_in(kind, ks[6]).wait_recv()
                keep(kind, ks[6]).wait()
                back_across(kind, ks[6]).start()

        @when(6, outer)
        def _():
            for kind in (0, 1):
                back_in(kind, ks[6]).wait_send()

        @when(5)
        def _():
            for kind in (0, 1):
                swap_second(kind, ks[5]).wait()
                add_into(own(kind, ks[5]).at[:, mine], land(4, kind, ks[5]))
                keep(kind, ks[5]).start()

        @when(5, outer)
        def _():
            for kind in (0, 1):
                keep(kind, ks[5]).wait()
                back_in(kind, ks[5]).start()

        @when(4, outer)
        def _():
            for kind in (0, 1):
                go_out(kind, ks[4]).wait_recv()
                add_into(own(kind, ks[4]).at[:, mine], land(3, kind, ks[4]))
                swap_second(kind, ks[4]).start()

        @when(4, inner)
        def _():
            for kind in (0, 1):
                go_out(kind, ks[4]).wait_send()

        @when(3, inner)
        def _():
            for kind in (0, 1):
                go_across(kind, ks[3]).wait()
                add_into(own(kind, ks[3]).at[:, near_two], land(2, kind, ks[3]))
                go_out(kind, ks[3]).start()
                swap_second(kind, ks[3]).start()

        @when(2, inner)
        def _():
            for kind in (0, 1):
                go_in(kind, ks[2]).wait_recv()
                add_into(own(kind, ks[2]).at[:, three], land(1, kind, ks[2]).at[:, three])
                go_across(kind, ks[2]).start()

        @when(2, outer)
        def _():
            for kind in (0, 1):
                go_in(kind, ks[2]).wait_send()

        @when(1)
        def _():
            for kind in (0, 1):
                scatter_first(kind, ks[1]).wait()
                add_into(own(kind, ks[1]), land(0, kind, ks[1]))

        @when(1, outer)
        def _():
            for kind in (0, 1):
                go_in(kind, ks[1]).start()

        @when(0)
        def _():
            for kind in (0, 1):
                scatter_first(kind, ks[0]).start()

    return meet, step, pairs + offsets[-1], (twin,) + first_peer + (line_peer, across)


def add_into(target, arrived):
    total = target[...].astype(jnp.float32) + arrived[...].astype(jnp.float32)
    target[...] = total.astype(jnp.bfloat16)


def land_shapes(full):
    two = 2 * QUARTER
    wide = (full, full, full // 2, full // 4, full // 4)
    return [pltpu.VMEM((slots, 2, two, n), jnp.bfloat16) for slots, n in zip(SLOTS, wide)]


def dot_tn(left, right):
    return lax.dot_general(left, right, (((0,), (0,)), ((), ())), preferred_element_type=jnp.float32)


def dot_nt(left, right):
    return lax.dot_general(left, right, (((1,), (1,)), ((), ())), preferred_element_type=jnp.float32)


def gelu_and_slope(v):
    square = v * v
    q = CDF_TERMS[-1] * square + CDF_TERMS[-2]
    for term in CDF_TERMS[-3::-1]:
        q = q * square + term
    cdf = 0.5 * jnp.tanh(v * q) + 0.5
    pdf = jnp.exp2(square * (-0.5 * LOG2_E)) * 0.3989422804014327
    return v * cdf, cdf + v * pdf


def lane_of(rows):
    return lax.broadcasted_iota(jnp.int32, (rows, 128), 1)


def spread_lanes(value, lane, other):
    first = value.astype(jnp.bfloat16)
    rest = value - first.astype(jnp.float32)
    second = rest.astype(jnp.bfloat16)
    third = (rest - second.astype(jnp.float32)).astype(jnp.bfloat16)
    at = lane % 64
    return jnp.where(at == 0, first, jnp.where(at == 1, second, jnp.where(at == 2, third, other)))


def key_lanes(length, rows):
    lane = lane_of(rows) % 64
    slot = lax.broadcasted_iota(jnp.int32, (rows, 128), 0)
    bias = jnp.where(slot < length, 0.0, -1e30)
    return jnp.where(lane < 3, 1.0, jnp.where(lane == 3, bias, 0.0)).astype(jnp.bfloat16)


def layer_kernel(
    inputs, cotangent, w_q, w_k, w_v, w_o, w_in, w_back,
    b_q, b_v, b_in, b_o, g_one, s_one, b_back, g_two, s_two, lens,
    out, vec_out, out_own, out_recv, ig_own, ig_recv, act_hbm, slope_hbm, w_other, w_oo, w_ino, w_backo,
    grads, land_0, land_1, land_2, land_3, land_4, send_t, land_t, vec_sum, vec_land, acc, buf_a, low, buf_c, buf_d, buf_e,
    buf_f, inner_g, qkv, xb, ctx, aux, normed_b, inv_b, vec_own, vec_oth, nat, bias_qkv, bias_ff, bias_in, sums_b, kl,
    ssem, rsem, osem, tsem, trsem, vsem, vrsem, isem, psem, lsem, gsem, xsem, xrsem, fsem, frsem,
):
    dp = lax.axis_index("dp")
    mp = lax.axis_index("mp")
    lands = (land_0, land_1, land_2, land_3, land_4)
    tokens, full = buf_a.shape
    half = full // 2
    tiles = act_hbm.shape[0]
    wide = act_hbm.shape[2]
    part = wide // 2
    seq = kl.shape[0]
    pages = tokens // seq
    pairs = grads.shape[0] // PAIR
    meet, tick, last_tick, swap_peers = chip_sum(pairs, grads, out, lands, ssem, rsem, osem)
    own_cols = pl.ds(pl.multiple_of(mp * half, half), half)
    other_cols = pl.ds(pl.multiple_of((1 - mp) * half, half), half)
    own_tokens = pl.ds(pl.multiple_of(mp * tokens, tokens), tokens)
    other_tokens = pl.ds(pl.multiple_of((1 - mp) * tokens, tokens), tokens)
    twin = (dp, 1 - mp)

    def load(i, src, dst):
        return pltpu.make_async_copy(src, dst, lsem.at[i])

    def give(i, src, dst, sends, gets):
        return pltpu.make_async_remote_copy(
            src, dst, sends.at[i], gets.at[i], device_id=twin, device_id_type=MESH
        )

    def weight_rows(n):
        return pl.ds(n * full, full)

    loads = [load(0, inputs.at[own_tokens], xb.at[:, own_cols])]
    loads += [load(1 + n, w, grads.at[weight_rows(n), pl.ds(0, half)]) for n, w in enumerate((w_q, w_k, w_v))]
    loads += [load(4, w_o, buf_f.at[0]), load(5, cotangent.at[own_tokens], buf_a.at[:, own_cols])]
    for copy in loads:
        copy.start()
    vec_own[...] = jnp.zeros_like(vec_own)
    at_row = 0
    for ref in (b_q, b_v, b_in, b_o, g_one, s_one, b_back, g_two, s_two):
        for c in range(0, ref.shape[0], half):
            vec_own[at_row : at_row + 1, :] = ref[c : c + half].astype(jnp.float32).reshape(1, half)
            at_row += 1
    meet()
    gifts = [
        give(0, inputs.at[other_tokens], xb.at[:, own_cols], xsem, xrsem),
        give(1, vec_own, vec_oth, xsem, xrsem),
    ]
    gifts += [
        give(2 + n, w, grads.at[weight_rows(n), pl.ds(half, half)], xsem, xrsem)
        for n, w in enumerate((w_q, w_k, w_v))
    ]
    gifts += [
        give(5, w_o, buf_f.at[1], xsem, xrsem),
        give(6, cotangent.at[other_tokens], buf_a.at[:, own_cols], xsem, xrsem),
    ]
    for gift in gifts:
        gift.start()

    def ff_gifts(j):
        at = pl.ds(pl.multiple_of(j * part, part), part)
        return (
            pltpu.make_async_remote_copy(
                w_in.at[:, at], w_ino.at[:, at], fsem.at[j, 0], frsem.at[j, 0], device_id=twin, device_id_type=MESH
            ),
            pltpu.make_async_remote_copy(
                w_back.at[at], w_backo.at[at], fsem.at[j, 1], frsem.at[j, 1], device_id=twin, device_id_type=MESH
            ),
        )

    gifts[1].wait_recv()
    nat[:, own_cols] = vec_own[...]
    nat[:, other_cols] = vec_oth[...]
    for n, row in enumerate((0, None, 1)):
        for h, ref in enumerate((vec_own, vec_oth)):
            at = slice(h * half, (h + 1) * half)
            if row is None:
                bias_qkv[n : n + 1, at] = jnp.zeros((1, half), jnp.float32)
            else:
                bias_qkv[n : n + 1, at] = ref[row : row + 1, :]
    for j in range(tiles):
        at = slice((j % 2) * part, (j % 2 + 1) * part)
        row = 2 + j // 2
        bias_ff[j : j + 1, :part] = vec_own[row : row + 1, at]
        bias_ff[j : j + 1, part:] = vec_oth[row : row + 1, at]
    loads[0].wait()
    gifts[0].wait_recv()

    def project(n, h):
        at = slice(h * half, (h + 1) * half)
        made = jnp.dot(xb[...], grads[n * full : (n + 1) * full, at], preferred_element_type=jnp.float32)
        qkv[2 * n + h] = (made + bias_qkv[n : n + 1, at]).astype(jnp.bfloat16)

    for n in range(3):
        loads[1 + n].wait()
        project(n, 0)
    for n in range(3):
        gifts[2 + n].wait_recv()
        project(n, 1)

    def start_gifts(j, carry):
        for gift in ff_gifts(j):
            gift.start()
        return carry

    lax.fori_loop(0, tiles, start_gifts, 0)

    keeps = [load(6 + n, grads.at[weight_rows(n), pl.ds(half, half)], w_other.at[n]) for n in range(3)]
    for copy in keeps:
        copy.start()
    gifts[5].wait_recv()
    keeps.append(load(9, buf_f.at[1], w_oo))
    keeps[3].start()
    loads[4].wait()

    lane = lane_of(seq)
    low_lanes = lane < 64
    high_lanes = lane >= 64
    q_one = jnp.where(lane % 64 == 3, 1.0, 0.0).astype(jnp.bfloat16)

    def pair_forward(i, carry):
        page, first_pair = i // 2, 4 * lax.rem(i, 2)

        @pl.when(first_pair == 0)
        def _():
            kl[...] = key_lanes(lens[mp * pages + page], seq)

        rows = pl.ds(pl.multiple_of(page * seq, seq), seq)
        for pair in [first_pair + n for n in range(4)]:
            side = pair // 4
            cols = pl.ds(pl.multiple_of(lax.rem(pair, 4) * 128, 128), 128)
            kp = qkv[2 + side, rows, cols]
            vp = qkv[4 + side, rows, cols]
            qp = qkv[side, rows, cols] * jnp.bfloat16(0.125)
            one = jnp.ones_like(vp)
            outs = []
            for h in (0, 1):
                mine = low_lanes if h == 0 else jnp.logical_not(low_lanes)
                scores = dot_nt(jnp.where(mine, qp, q_one), jnp.where(mine, kp, kl[...]))
                top = jnp.max(scores, axis=1, keepdims=True)
                weights = jnp.exp(scores - top).astype(jnp.bfloat16)
                outs.append((top, jnp.dot(weights, jnp.where(mine, vp, one), preferred_element_type=jnp.float32)))
            (top0, out0), (top1, out1) = outs
            total = jnp.where(low_lanes, out1, out0)
            value = jnp.where(low_lanes, out0, out1) / pltpu.roll(total, 64, 1)
            neg = -(jnp.where(low_lanes, top1, top0) + jnp.log(total))
            mixed = spread_lanes(neg, lane, q_one)
            ctx[side, rows, cols] = value.astype(jnp.bfloat16)
            aux[side, rows, cols] = mixed
        return carry

    lax.fori_loop(0, 2 * pages, pair_forward, 0)

    def fetch_in(j, slot):
        at = pl.ds(pl.multiple_of(j * part, part), part)
        return [
            pltpu.make_async_copy(w_in.at[:, at], buf_e.at[slot, :, pl.ds(0, part)], isem.at[slot, 2]),
            pltpu.make_async_copy(w_ino.at[:, at], buf_e.at[slot, :, pl.ds(part, part)], isem.at[slot, 3]),
        ]

    def fetch_back(j, slot):
        at = pl.ds(pl.multiple_of(j * part, part), part)
        return [
            pltpu.make_async_copy(w_back.at[at], buf_f.at[slot, pl.ds(0, part)], isem.at[slot, 4]),
            pltpu.make_async_copy(w_backo.at[at], buf_f.at[slot, pl.ds(part, part)], isem.at[slot, 5]),
        ]

    def fetch_made(j, slot):
        return [
            pltpu.make_async_copy(act_hbm.at[j], buf_c.at[slot], isem.at[slot, 0]),
            pltpu.make_async_copy(slope_hbm.at[j], buf_d.at[slot], isem.at[slot, 1]),
        ]

    def start(copies):
        for copy in copies:
            copy.start()

    def finish(copies):
        for copy in copies:
            copy.wait()

    def got_gifts(j):
        for gift in ff_gifts(j):
            gift.wait_recv()

    got_gifts(0)
    start(fetch_in(0, 0))
    step = 512

    def norm_one(i, carry):
        rows = pl.ds(pl.multiple_of(i * step, step), step)
        attended = (
            xb[rows, :].astype(jnp.float32)
            + jnp.dot(ctx[0, rows, :], buf_f[0], preferred_element_type=jnp.float32)
            + jnp.dot(ctx[1, rows, :], buf_f[1], preferred_element_type=jnp.float32)
            + nat[6:7, :]
        )
        average = jnp.mean(attended, axis=1, keepdims=True)
        centred = attended - average
        inv = lax.rsqrt(jnp.mean(centred * centred, axis=1, keepdims=True) + eps)
        normed = centred * inv
        hidden = normed * nat[7:8, :] + nat[8:9, :]
        acc[rows, :] = hidden
        low[rows, :] = hidden.astype(jnp.bfloat16)
        normed_b[rows, :] = normed.astype(jnp.bfloat16)
        inv_b[rows, :] = jnp.broadcast_to(inv, (step, 128))
        return carry

    lax.fori_loop(0, tokens // step, norm_one, 0)
    keeps[3].wait()
    start(fetch_back(0, 0))

    def saves(j, slot):
        return [
            pltpu.make_async_copy(buf_c.at[slot], act_hbm.at[j], psem.at[slot, 0]),
            pltpu.make_async_copy(buf_d.at[slot], slope_hbm.at[j], psem.at[slot, 1]),
        ]

    def forward_tile(j, carry):
        slot = lax.rem(j, 2)

        @pl.when(j + 1 < tiles)
        def _():
            got_gifts(j + 1)
            start(fetch_in(j + 1, 1 - slot) + fetch_back(j + 1, 1 - slot))

        finish(fetch_in(j, slot) + fetch_back(j, slot))

        @pl.when(j >= 2)
        def _():
            finish(saves(j - 2, slot))

        inner = jnp.dot(low[...], buf_e[slot], preferred_element_type=jnp.float32) + bias_ff[pl.ds(j, 1), :]
        value, grad = gelu_and_slope(inner)
        value = value.astype(jnp.bfloat16)
        buf_c[slot] = value
        buf_d[slot] = grad.astype(jnp.bfloat16)
        acc[...] += jnp.dot(value, buf_f[slot], preferred_element_type=jnp.float32)
        start(saves(j, slot))
        return carry

    lax.fori_loop(0, tiles, forward_tile, 0)
    loads[5].wait()
    gifts[6].wait_recv()
    stage_rows = tiles * BLOCK

    def norm_two(i, sums):
        at = pl.multiple_of(i * step, step)
        rows = pl.ds(at, step)
        summed = acc[rows, :] + nat[9:10, :]
        average = jnp.mean(summed, axis=1, keepdims=True)
        centred = summed - average
        inv = lax.rsqrt(jnp.mean(centred * centred, axis=1, keepdims=True) + eps)
        normed = centred * inv
        grads[pl.ds(pl.multiple_of(stage_rows + i * step, step), step), :] = (
            normed * nat[10:11, :] + nat[11:12, :]
        ).astype(jnp.bfloat16)
        page = (i * step) // seq
        slots = lax.broadcasted_iota(jnp.int32, (step, 1), 0) + lax.rem(i * step, seq)
        valid = jnp.where(slots < lens[mp * pages + page], 1.0, 0.0)
        grad = buf_a[rows, :].astype(jnp.float32) * valid
        scaled = grad * nat[10:11, :]
        mean_one = jnp.mean(scaled, axis=1, keepdims=True)
        mean_two = jnp.mean(scaled * normed, axis=1, keepdims=True)
        back = inv * (scaled - mean_one - normed * mean_two)
        acc[rows, :] = back
        buf_a[rows, :] = back.astype(jnp.bfloat16)
        return (
            sums[0] + jnp.sum(back, axis=0, keepdims=True),
            sums[1] + jnp.sum(grad * normed, axis=0, keepdims=True),
            sums[2] + jnp.sum(grad, axis=0, keepdims=True),
        )

    zero = jnp.zeros((1, full), jnp.float32)
    for n, row in enumerate(lax.fori_loop(0, tokens // step, norm_two, (zero, zero, zero))):
        sums_b[n : n + 1, :] = row
    finish(keeps[:3])
    staged = grads.at[pl.ds(stage_rows, tokens)]
    out_keep = pltpu.make_async_copy(staged.at[:, own_cols], out_own, gsem.at[3])
    out_send = pltpu.make_async_remote_copy(
        staged.at[:, other_cols], out_recv, gsem.at[4], gsem.at[5], device_id=twin, device_id_type=MESH
    )
    out_keep.start()
    out_send.start()

    def to_twin(b, which):
        slot = lax.rem(b, 2)
        at = pl.ds(which * part, part)
        return pltpu.make_async_remote_copy(
            send_t.at[slot, at],
            land_t.at[slot, at],
            tsem.at[slot, which],
            trsem.at[slot, which],
            device_id=twin,
            device_id_type=MESH,
        )

    def give_twin(b):
        for which in (0, 1):
            to_twin(b, which).start()

    def gave_twin(b):
        for which in (0, 1):
            to_twin(b, which).wait_send()

    def take_half(b, which):
        to_twin(b, which).wait_recv()
        slot = lax.rem(b, 2)

        def piece(i, carry):
            at = which * part + i * CHUNK
            add_into(grads.at[rows_at(b * BLOCK + at, CHUNK)], land_t.at[slot, rows_at(at, CHUNK)])
            return carry

        lax.fori_loop(0, part // CHUNK, piece, 0)

    def take_twin(b):
        for which in (0, 1):
            take_half(b, which)

    def backward_tile(b, carry):
        j = tiles - 1 - b
        slot = lax.rem(j, 2)
        mate = lax.rem(b, 2)

        @pl.when(b >= 2)
        def _():
            finish(fetch_made(j, slot) + fetch_in(j, slot) + fetch_back(j, slot))
            gave_twin(b - 2)

        base = b * BLOCK
        for c in range(0, full, half):
            made = dot_tn(buf_c[slot], buf_a[:, c : c + half]).astype(jnp.bfloat16)
            grads[rows_at(base, part), c : c + half] = made[:part]
            send_t[mate, :part, c : c + half] = made[part:]

        to_twin(b, 0).start()
        made = dot_nt(buf_a[...], buf_f[slot]) * buf_d[slot].astype(jnp.float32)
        made = made.astype(jnp.bfloat16)
        inner_g[...] = made
        bias_in[pl.ds(j, 1), :] = jnp.sum(made.astype(jnp.float32), axis=0, keepdims=True)

        @pl.when(b >= 1)
        def _():
            take_half(b - 1, 1)
            tick(3 * b - 1)

        acc[...] += dot_nt(inner_g[...], buf_e[slot])
        take_half(b, 0)
        tick(3 * b)
        for c in range(0, full, part):
            made = dot_tn(low[:, c : c + part], inner_g[...]).astype(jnp.bfloat16)
            grads[rows_at(base + part, part), c : c + part] = made[:, :part]
            send_t[mate, part:, c : c + part] = made[:, part:]

        to_twin(b, 1).start()

        @pl.when(b < 2)
        def _():
            finish(saves(j, slot))

        @pl.when(b < tiles - 2)
        def _():
            start(fetch_made(j - 2, slot) + fetch_in(j - 2, slot) + fetch_back(j - 2, slot))

        tick(3 * b + 1)
        return carry

    lax.fori_loop(0, tiles, backward_tile, 0)
    t = 3 * tiles - 1

    second = [load(10, w_o, buf_f.at[0]), load(11, w_oo, buf_f.at[1])]
    start(second)

    def norm_back(i, sums):
        rows = pl.ds(pl.multiple_of(i * step, step), step)
        grad = acc[rows, :]
        normed = normed_b[rows, :].astype(jnp.float32)
        scaled = grad * nat[7:8, :]
        mean_one = jnp.mean(scaled, axis=1, keepdims=True)
        mean_two = jnp.mean(scaled * normed, axis=1, keepdims=True)
        back = inv_b[rows, 0:1] * (scaled - mean_one - normed * mean_two)
        acc[rows, :] = back
        buf_a[rows, :] = back.astype(jnp.bfloat16)
        return (
            sums[0] + jnp.sum(back, axis=0, keepdims=True),
            sums[1] + jnp.sum(grad * normed, axis=0, keepdims=True),
            sums[2] + jnp.sum(grad, axis=0, keepdims=True),
        )

    bias_o, gain_one, shift_one = lax.fori_loop(0, tokens // step, norm_back, (zero, zero, zero))
    tick(t)

    b = tiles
    gave_twin(b - 2)
    out_keep.wait()
    out_send.wait()
    finish(second)
    for h in (0, 1):
        for c in range(0, full, half):
            made = dot_tn(ctx[h], buf_a[:, c : c + half]).astype(jnp.bfloat16)
            if h == 0:
                grads[b * BLOCK : b * BLOCK + half, c : c + half] = made
            else:
                send_t[b % 2, :, c : c + half] = made
    take_half(b - 1, 1)
    give_twin(b)
    tick(t + 1)
    for h in (0, 1):
        for r in range(0, tokens, half):
            buf_e[h, r : r + half, :] = dot_nt(buf_a[r : r + half, :], buf_f[h]).astype(jnp.bfloat16)
    take_twin(b)
    tick(t + 2)
    t = t + 3

    def pair_backward(i, carry):
        page, first_pair = i // 4, 2 * lax.rem(i, 4)

        @pl.when(first_pair == 0)
        def _():
            kl[...] = key_lanes(lens[mp * pages + page], seq)

        for pair in (first_pair, first_pair + 1):
            side = pair // 4
            rows = pl.ds(pl.multiple_of(page * seq, seq), seq)
            cols = pl.ds(pl.multiple_of(lax.rem(pair, 4) * 128, 128), 128)
            qp = qkv[side, rows, cols] * jnp.bfloat16(0.125)
            kp = qkv[2 + side, rows, cols]
            vp = qkv[4 + side, rows, cols]
            extra = aux[side, rows, cols]
            gp = buf_e[side, rows, cols]
            cp = ctx[side, rows, cols]
            none = jnp.zeros_like(gp)
            product = gp.astype(jnp.float32) * cp.astype(jnp.float32)
            sums = [jnp.sum(jnp.where(mine, product, 0.0), axis=1, keepdims=True) for mine in (low_lanes, high_lanes)]
            shift = spread_lanes(-jnp.where(low_lanes, sums[1], sums[0]), lane, none)
            made = []
            for mine in (low_lanes, high_lanes):
                qh = jnp.where(mine, qp, none)
                gh = jnp.where(mine, gp, none)
                probs = jnp.exp(dot_nt(jnp.where(mine, kp, kl[...]), jnp.where(mine, qp, extra)))
                grad_weights = dot_nt(jnp.where(mine, vp, kl[...]), jnp.where(mine, gp, shift))
                grad_scores = (probs * grad_weights).astype(jnp.bfloat16)
                grad_v = jnp.dot(probs.astype(jnp.bfloat16), gh, preferred_element_type=jnp.float32)
                grad_k = jnp.dot(grad_scores, qh, preferred_element_type=jnp.float32)
                grad_q = dot_tn(grad_scores, jnp.where(mine, kp, none))
                made.append((grad_q * 0.125, grad_k, grad_v))
            for n in range(3):
                qkv[2 * n + side, rows, cols] = (made[0][n] + made[1][n]).astype(jnp.bfloat16)

        tick(t + i + i // 4)

        @pl.when(lax.rem(i, 4) == 3)
        def _():
            tick(t + i + 1 + i // 4)

        return carry

    lax.fori_loop(0, 4 * pages, pair_backward, 0)
    t = t + 10

    third = [load(12, w_q, buf_c.at[0]), load(13, w_k, buf_d.at[0]), load(14, w_v, buf_e.at[0])]
    third += [load(15 + n, w_other.at[n], ref.at[1]) for n, ref in enumerate((buf_c, buf_d, buf_e))]
    start(third)
    b = tiles + 1

    def weights_loop(i, carry):
        at = b + i
        slot = lax.rem(at, 2)
        gave_twin(at - 2)
        for r in range(0, full, half):
            made = dot_tn(xb[:, r : r + half], qkv[2 * i]).astype(jnp.bfloat16)
            grads[rows_at(at * BLOCK, BLOCK), r : r + half] = made
            made = dot_tn(xb[:, r : r + half], qkv[2 * i + 1]).astype(jnp.bfloat16)
            send_t[slot, :, r : r + half] = made

        @pl.when(i >= 1)
        def _():
            take_twin(at - 1)
            tick(t + i - 1)

        give_twin(at)
        return carry

    lax.fori_loop(0, 3, weights_loop, 0)
    t = t + 2
    b = b + 3

    first_core = mp == 0
    owned, others = [], []
    for n in (0, 4):
        owned.append(jnp.sum(qkv[n].astype(jnp.float32), axis=0, keepdims=True))
        others.append(jnp.sum(qkv[n + 1].astype(jnp.float32), axis=0, keepdims=True))
    for row in (bias_o, gain_one, shift_one, sums_b[0:1, :], sums_b[1:2, :], sums_b[2:3, :]):
        owned.append(jnp.where(first_core, row[:, :half], row[:, half:]))
        others.append(jnp.where(first_core, row[:, half:], row[:, :half]))
    for n in range(0, tiles, 2):
        owned.append(jnp.concatenate([bias_in[n : n + 1, :part], bias_in[n + 1 : n + 2, :part]], axis=1))
        others.append(jnp.concatenate([bias_in[n : n + 1, part:], bias_in[n + 1 : n + 2, part:]], axis=1))
    fill = jnp.zeros((QUARTER - len(owned), half), jnp.float32)
    vec_sum[0] = jnp.concatenate(others + [fill], axis=0)
    vec_sum[1] = jnp.concatenate(owned + [fill], axis=0)

    def swap_vectors(n):
        return pltpu.make_async_remote_copy(
            vec_sum.at[n], vec_land.at[n], vsem.at[n], vrsem.at[n], device_id=swap_peers[n], device_id_type=MESH
        )

    swap_vectors(0).start()
    take_twin(b - 1)
    gave_twin(b - 2)
    gave_twin(b - 1)
    tick(t)
    finish(third)

    def input_loop(i, carry):
        rows = pl.ds(pl.multiple_of(i * step, step), step)
        total = acc[rows, :]
        for n, ref in enumerate((buf_c, buf_d, buf_e)):
            for h in (0, 1):
                total = total + dot_nt(qkv[2 * n + h, rows, :], ref[h])
        buf_a[rows, :] = total.astype(jnp.bfloat16)
        tick(t + 1 + i)
        return carry

    lax.fori_loop(0, tokens // step, input_loop, 0)
    t = t + 1 + tokens // step
    ig_keep = pltpu.make_async_copy(buf_a.at[:, own_cols], ig_own, gsem.at[0])
    ig_send = pltpu.make_async_remote_copy(
        buf_a.at[:, other_cols], ig_recv, gsem.at[1], gsem.at[2], device_id=twin, device_id_type=MESH
    )
    ig_keep.start()
    ig_send.start()
    for gift in gifts:
        gift.wait_send()

    def end_gifts(j, carry):
        for gift in ff_gifts(j):
            gift.wait_send()
        return carry

    lax.fori_loop(0, tiles, end_gifts, 0)

    def rest(i, carry):
        for n in range(5):

            @pl.when(i == t + 2 * n)
            def _():
                swap_vectors(n).wait()
                total = vec_sum[max(n, 1)] + vec_land[n]
                if n == 4:
                    vec_out[...] = total
                else:
                    vec_sum[n + 1] = total
                    swap_vectors(n + 1).start()

        tick(i)
        return carry

    lax.fori_loop(t, last_tick, rest, 0)
    ig_keep.wait()
    ig_send.wait()


HBM = pl.BlockSpec(memory_space=pltpu.HBM)
VMEM = pl.BlockSpec(memory_space=pltpu.VMEM)
SMEM = pl.BlockSpec(memory_space=pltpu.SMEM)


def shape(dims, dtype=jnp.bfloat16):
    return jax.ShapeDtypeStruct(dims, dtype)


def run_layer(inputs, cotangent, w_q, w_k, w_v, w_o, w_in, w_back, vectors, lengths):
    tokens = inputs.shape[0] // 2
    half = inputs.shape[1]
    full = 2 * half
    seq = inputs.shape[0] // lengths.shape[0]
    ff_half = w_in.shape[1]
    tiles = ff_half // (BLOCK // 2)
    wide = BLOCK
    rows = (tiles + 4) * BLOCK
    f32 = jnp.float32
    bf16 = jnp.bfloat16
    return pl.pallas_call(
        layer_kernel,
        name="layer",
        out_shape=(
            shape((rows, full)), shape((QUARTER, half), f32), shape((tokens, half)), shape((tokens, half)),
            shape((tokens, half)), shape((tokens, half)), shape((tiles, tokens, wide)), shape((tiles, tokens, wide)),
            shape((3, full, half)), shape((half, full)), shape((full, ff_half)), shape((ff_half, full)),
        ),
        in_specs=[HBM] * 8 + [VMEM] * 9 + [SMEM],
        out_specs=(HBM, VMEM) + (HBM,) * 10,
        scratch_shapes=[
            pltpu.VMEM((rows, full), bf16),
            *land_shapes(full),
            pltpu.VMEM((2, BLOCK, full), bf16),
            pltpu.VMEM((2, BLOCK, full), bf16),
            pltpu.VMEM((6, QUARTER, half), f32),
            pltpu.VMEM((5, QUARTER, half), f32),
            pltpu.VMEM((tokens, full), f32),
            pltpu.VMEM((tokens, full), bf16),
            pltpu.VMEM((tokens, full), bf16),
            pltpu.VMEM((2, tokens, half), bf16),
            pltpu.VMEM((2, tokens, half), bf16),
            pltpu.VMEM((2, tokens, half), bf16),
            pltpu.VMEM((2, half, full), bf16),
            pltpu.VMEM((tokens, wide), bf16),
            pltpu.VMEM((6, tokens, half), bf16),
            pltpu.VMEM((tokens, full), bf16),
            pltpu.VMEM((2, tokens, half), bf16),
            pltpu.VMEM((2, tokens, half), bf16),
            pltpu.VMEM((tokens, full), bf16),
            pltpu.VMEM((tokens, 128), f32),
            pltpu.VMEM((QUARTER, half), f32),
            pltpu.VMEM((QUARTER, half), f32),
            pltpu.VMEM((QUARTER, full), f32),
            pltpu.VMEM((8, full), f32),
            pltpu.VMEM((tiles, wide), f32),
            pltpu.VMEM((tiles, wide), f32),
            pltpu.VMEM((8, full), f32),
            pltpu.VMEM((seq, 128), bf16),
            pltpu.SemaphoreType.DMA((2, sum(SLOTS))),
            pltpu.SemaphoreType.DMA((2, sum(SLOTS))),
            pltpu.SemaphoreType.DMA((2, KEEP_SLOTS)),
            pltpu.SemaphoreType.DMA((2, 2)),
            pltpu.SemaphoreType.DMA((2, 2)),
            pltpu.SemaphoreType.DMA((5,)),
            pltpu.SemaphoreType.DMA((5,)),
            pltpu.SemaphoreType.DMA((2, 6)),
            pltpu.SemaphoreType.DMA((2, 2)),
            pltpu.SemaphoreType.DMA((18,)),
            pltpu.SemaphoreType.DMA((6,)),
            pltpu.SemaphoreType.DMA((7,)),
            pltpu.SemaphoreType.DMA((7,)),
            pltpu.SemaphoreType.DMA((tiles, 2)),
            pltpu.SemaphoreType.DMA((tiles, 2)),
        ],
        compiler_params=pltpu.CompilerParams(
            collective_id=0, has_side_effects=True, vmem_limit_bytes=62 << 20
        ),
    )(inputs, cotangent, w_q, w_k, w_v, w_o, w_in, w_back, *vectors, lengths)


def unpack_kernel(
    packed, out_mine, out_got, ig_mine, ig_got, vectors,
    output, input_grad, g_q, g_k, g_v, g_o, g_in, g_back, v_q, v_v, v_o, v_g1, v_s1, v_b, v_g2, v_s2, v_in,
    loaded, wide, passed, isem, osem, csem,
):
    mp = lax.axis_index("mp")
    tokens, half = out_mine.shape
    mine = pl.ds(pl.multiple_of(mp * tokens, tokens), tokens)
    other = pl.ds(pl.multiple_of((1 - mp) * tokens, tokens), tokens)
    pieces = (
        (out_mine, output.at[mine]),
        (out_got, output.at[other]),
        (ig_mine, input_grad.at[mine]),
        (ig_got, input_grad.at[other]),
    )
    moves = [pltpu.make_async_copy(src, passed.at[i], csem.at[0, i]) for i, (src, _) in enumerate(pieces)]
    leaves = [pltpu.make_async_copy(passed.at[i], dst, csem.at[1, i]) for i, (_, dst) in enumerate(pieces)]
    part = BLOCK // 2
    full = packed.shape[1]
    tiles = g_back.shape[0] // part
    blocks = tiles + 4
    slots = wide.shape[0]

    def fetch(b):
        return pltpu.make_async_copy(packed.at[b * BLOCK : (b + 1) * BLOCK], loaded.at[b], isem.at[b])

    def stores(b):
        ref = wide.at[b % slots]
        j = tiles - 1 - b
        if b < tiles:
            pieces = [(ref.at[:part], g_back.at[j * part : (j + 1) * part])]
            for c in range(0, full, part):
                pieces.append((ref.at[part:, c : c + part], g_in.at[c : c + part, j * part : (j + 1) * part]))
        elif b == tiles:
            pieces = [(ref, g_o)]
        else:
            target = (g_q, g_k, g_v)[b - tiles - 1]
            pieces = [(ref.at[:, :half], target.at[:half]), (ref.at[:, half:], target.at[half:])]
        return [pltpu.make_async_copy(src, dst, osem.at[b % slots, i]) for i, (src, dst) in enumerate(pieces)]

    for b in range(blocks):
        fetch(b).start()
        if b < len(moves):
            moves[b].start()
    for n, ref in enumerate((v_q, v_v, v_o, v_g1, v_s1, v_b, v_g2, v_s2)):
        ref[...] = vectors[n, :]
    for n in range(4):
        v_in[n * half : (n + 1) * half] = vectors[8 + n, :]
    for b in range(blocks):
        fetch(b).wait()
        if b >= slots:
            for store in stores(b - slots):
                store.wait()
        for r in range(0, BLOCK, CHUNK):
            wide[b % slots, r : r + CHUNK, :] = loaded[b, r : r + CHUNK, :].astype(jnp.float32)
        for store in stores(b):
            store.start()
        if b < len(moves):
            moves[b].wait()
            leaves[b].start()
    for b in range(blocks - slots, blocks):
        for store in stores(b):
            store.wait()
    for leave in leaves:
        leave.wait()


def run_unpack(packed, out_mine, out_got, ig_mine, ig_got, vectors, tiles):
    tokens, half = out_mine.shape
    full = 2 * half
    ff_half = tiles * (BLOCK // 2)
    f32 = jnp.float32
    slots = 6
    return pl.pallas_call(
        unpack_kernel,
        name="unpack",
        out_shape=(
            shape((2 * tokens, half)), shape((2 * tokens, half)),
            shape((full, half), f32), shape((full, half), f32), shape((full, half), f32), shape((half, full), f32),
            shape((full, ff_half), f32), shape((ff_half, full), f32),
            *[shape((half,), f32)] * 8, shape((ff_half,), f32),
        ),
        in_specs=[HBM] * 5 + [VMEM],
        out_specs=(HBM,) * 8 + (VMEM,) * 9,
        scratch_shapes=[
            pltpu.VMEM((tiles + 4, BLOCK, full), jnp.bfloat16),
            pltpu.VMEM((slots, BLOCK, full), f32),
            pltpu.VMEM((4, tokens, half), jnp.bfloat16),
            pltpu.SemaphoreType.DMA((tiles + 4,)),
            pltpu.SemaphoreType.DMA((slots, 5)),
            pltpu.SemaphoreType.DMA((2, 4)),
        ],
        compiler_params=pltpu.CompilerParams(vmem_limit_bytes=60 << 20),
    )(packed, out_mine, out_got, ig_mine, ig_got, vectors)


def on_core(
    inputs, lengths, w_query, b_query, w_key, w_value, b_value, w_out, b_out, gain_one, shift_one, w_in, b_in, w_back,
    b_back, gain_two, shift_two, cotangent,
):
    tiles = w_in.shape[1] // (BLOCK // 2)
    given = (b_query, b_value, b_in, b_out, gain_one, shift_one, b_back, gain_two, shift_two)
    packed, vectors, out_mine, out_got, ig_mine, ig_got, *_ = run_layer(
        inputs, cotangent, w_query, w_key, w_value, w_out, w_in, w_back, given, lengths
    )
    output, input_grad, g_q, g_k, g_v, g_o, g_in, g_back, *v = run_unpack(
        packed, out_mine, out_got, ig_mine, ig_got, vectors, tiles
    )
    return (
        output, input_grad, g_q, v[0], g_k, g_v, v[1], g_o, v[2], v[3], v[4], g_in, v[8], g_back, v[5], v[6], v[7],
    )


def gelu_exact(ffn_inner):
    return jax.nn.gelu(ffn_inner, approximate=False)


def normalize_rows(summed, gain_vec, shift_vec):
    average = jnp.mean(summed, axis=-1, keepdims=True)
    centred = summed - average
    inv_std = lax.rsqrt(jnp.mean(centred * centred, axis=-1, keepdims=True) + eps)
    normed = centred * inv_std
    return (normed * gain_vec + shift_vec, normed, inv_std)


def normalize_back(grad_out, normed, inv_std, gain_vec):
    scaled = grad_out * gain_vec
    centred = scaled - jnp.mean(scaled, axis=-1, keepdims=True)
    return inv_std * (centred - normed * jnp.mean(scaled * normed, axis=-1, keepdims=True))


def on_device(
    inputs,
    lengths,
    w_query,
    b_query,
    w_key,
    w_value,
    b_value,
    w_out,
    b_out,
    gain_one,
    shift_one,
    w_in,
    b_in,
    w_back,
    b_back,
    gain_two,
    shift_two,
    cotangent,
):
    token_count, part_cols = inputs.shape
    page_count = lengths.shape[0]
    seq_len = token_count // page_count
    head_size = HDIM
    local_heads = w_query.shape[1] // head_size
    score_scale = head_size ** (-0.5)
    offset = lax.axis_index("mp") * part_cols

    def own_cols(full_array):
        return lax.dynamic_slice_in_dim(full_array, offset, part_cols, full_array.ndim - 1)

    vectors = jnp.stack([b_out, gain_one, shift_one, b_back, gain_two, shift_two])
    token_rows, vector_rows = (
        lax.all_gather(inputs, "mp", axis=1, tiled=True),
        lax.all_gather(vectors, "mp", axis=1, tiled=True),
    )
    vector_rows = vector_rows.astype(jnp.float32)
    full_b_out, full_gain_one, full_shift_one = (vector_rows[0], vector_rows[1], vector_rows[2])
    full_b_back, full_gain_two, full_shift_two = (vector_rows[3], vector_rows[4], vector_rows[5])
    positions = jnp.arange(seq_len, dtype=jnp.int32)
    key_valid = positions[None, :] < lengths[:, None]
    row_valid = key_valid.reshape(token_count, 1).astype(jnp.float32)
    head_shape = (page_count, seq_len, local_heads, head_size)
    queries = (
        (
            jnp.dot(token_rows, w_query, preferred_element_type=jnp.float32)
            + b_query.astype(jnp.float32)
        )
        .astype(jnp.bfloat16)
        .reshape(head_shape)
    )
    keys_all = (
        jnp.dot(token_rows, w_key, preferred_element_type=jnp.float32)
        .astype(jnp.bfloat16)
        .reshape(head_shape)
    )
    values = (
        (
            jnp.dot(token_rows, w_value, preferred_element_type=jnp.float32)
            + b_value.astype(jnp.float32)
        )
        .astype(jnp.bfloat16)
        .reshape(head_shape)
    )

    def masked_scores(page_queries, page_keys, page_valid):
        scores = (
            jnp.einsum("qhd,khd->hqk", page_queries, page_keys, preferred_element_type=jnp.float32)
            * score_scale
        )
        return jnp.where(page_valid[None, None, :], scores, -1e30)

    def attend(packed):
        page_queries, page_keys, page_values, page_valid = packed
        scores = masked_scores(page_queries, page_keys, page_valid)
        row_max = jnp.max(scores, axis=-1, keepdims=True)
        shifted = jnp.exp(scores - row_max)
        row_sum = jnp.sum(shifted, axis=-1, keepdims=True)
        weights = (shifted / row_sum).astype(jnp.bfloat16)
        context = jnp.einsum(
            "hqk,khd->qhd", weights, page_values, preferred_element_type=jnp.float32
        )
        return (context.astype(jnp.bfloat16), (row_max + jnp.log(row_sum))[..., 0])

    context, log_total = lax.map(attend, (queries, keys_all, values, key_valid))
    context = context.reshape(token_count, local_heads * head_size)
    attn_part = jnp.dot(context, w_out, preferred_element_type=jnp.float32)
    attended = token_rows.astype(jnp.float32) + lax.psum(attn_part, "mp") + full_b_out
    hidden_one, normed_one, inv_std_one = normalize_rows(attended, full_gain_one, full_shift_one)
    hidden_low = hidden_one.astype(jnp.bfloat16)
    ffn_inner = jnp.dot(hidden_low, w_in, preferred_element_type=jnp.float32) + b_in.astype(
        jnp.float32
    )
    gelu_value, gelu_pull = jax.vjp(gelu_exact, ffn_inner)
    activated = gelu_value.astype(jnp.bfloat16)
    ffn_part = jnp.dot(activated, w_back, preferred_element_type=jnp.float32)
    summed = hidden_one + lax.psum(ffn_part, "mp") + full_b_back
    out_full, normed_two, inv_std_two = normalize_rows(summed, full_gain_two, full_shift_two)
    output = own_cols(out_full).astype(jnp.bfloat16)
    grad_out = lax.all_gather(cotangent, "mp", axis=1, tiled=True).astype(jnp.float32) * row_valid
    grad_summed = normalize_back(grad_out, normed_two, inv_std_two, full_gain_two)
    grad_gain_two = own_cols(jnp.sum(grad_out * normed_two, axis=0))
    grad_shift_two = own_cols(jnp.sum(grad_out, axis=0))
    grad_b_back = own_cols(jnp.sum(grad_summed, axis=0))
    round_summed = grad_summed.astype(jnp.bfloat16)
    grad_act = jnp.einsum("rd,fd->rf", round_summed, w_back, preferred_element_type=jnp.float32)
    grad_inner = gelu_pull(grad_act)[0].astype(jnp.bfloat16)
    grad_w_back = jnp.einsum(
        "rf,rd->fd", activated, round_summed, preferred_element_type=jnp.float32
    )
    grad_w_in = jnp.einsum("rd,rf->df", hidden_low, grad_inner, preferred_element_type=jnp.float32)
    grad_b_in = jnp.sum(grad_inner.astype(jnp.float32), axis=0)
    ffn_grads = (grad_w_in, grad_b_in, grad_w_back, grad_b_back, grad_gain_two, grad_shift_two)
    back_part = jnp.einsum("rf,df->rd", grad_inner, w_in, preferred_element_type=jnp.float32)
    grad_hidden = lax.psum(back_part, "mp") + grad_summed
    grad_gain_one = own_cols(jnp.sum(grad_hidden * normed_one, axis=0))
    grad_shift_one = own_cols(jnp.sum(grad_hidden, axis=0))
    grad_attended = normalize_back(grad_hidden, normed_one, inv_std_one, full_gain_one)
    grad_b_out = own_cols(jnp.sum(grad_attended, axis=0))
    own_attended = own_cols(grad_attended)
    round_attended = grad_attended.astype(jnp.bfloat16)
    grad_w_out = jnp.einsum(
        "rc,rd->cd", context, round_attended, preferred_element_type=jnp.float32
    )
    grad_context = (
        jnp.einsum("rd,cd->rc", round_attended, w_out, preferred_element_type=jnp.float32)
        .astype(jnp.bfloat16)
        .reshape(head_shape)
    )

    def attend_back(packed):
        page_queries, page_keys, page_values, page_valid, page_total, page_grad = packed
        scores = masked_scores(page_queries, page_keys, page_valid)
        probabilities = jnp.exp(scores - page_total[..., None])
        weights = probabilities.astype(jnp.bfloat16)
        grad_values = jnp.einsum(
            "hqk,qhd->khd", weights, page_grad, preferred_element_type=jnp.float32
        )
        grad_weights = jnp.einsum(
            "qhd,khd->hqk", page_grad, page_values, preferred_element_type=jnp.float32
        )
        grad_scores = (
            probabilities
            * (grad_weights - jnp.sum(probabilities * grad_weights, axis=-1, keepdims=True))
        ).astype(jnp.bfloat16)
        grad_queries = (
            jnp.einsum("hqk,khd->qhd", grad_scores, page_keys, preferred_element_type=jnp.float32)
            * score_scale
        )
        grad_keys = (
            jnp.einsum(
                "hqk,qhd->khd", grad_scores, page_queries, preferred_element_type=jnp.float32
            )
            * score_scale
        )
        return (
            grad_queries.astype(jnp.bfloat16),
            grad_keys.astype(jnp.bfloat16),
            grad_values.astype(jnp.bfloat16),
        )

    grad_queries, grad_keys, grad_values = lax.map(
        attend_back, (queries, keys_all, values, key_valid, log_total, grad_context)
    )
    grad_queries = grad_queries.reshape(token_count, local_heads * head_size)
    grad_keys = grad_keys.reshape(token_count, local_heads * head_size)
    grad_values = grad_values.reshape(token_count, local_heads * head_size)
    grad_w_query = jnp.einsum(
        "rd,rc->dc", token_rows, grad_queries, preferred_element_type=jnp.float32
    )
    grad_w_key = jnp.einsum("rd,rc->dc", token_rows, grad_keys, preferred_element_type=jnp.float32)
    grad_w_value = jnp.einsum(
        "rd,rc->dc", token_rows, grad_values, preferred_element_type=jnp.float32
    )
    grad_b_query = jnp.sum(grad_queries.astype(jnp.float32), axis=0)
    grad_b_value = jnp.sum(grad_values.astype(jnp.float32), axis=0)
    input_part = (
        jnp.einsum("rc,dc->rd", grad_queries, w_query, preferred_element_type=jnp.float32)
        + jnp.einsum("rc,dc->rd", grad_keys, w_key, preferred_element_type=jnp.float32)
        + jnp.einsum("rc,dc->rd", grad_values, w_value, preferred_element_type=jnp.float32)
    )
    input_grad = (
        lax.psum_scatter(
            input_part.astype(jnp.bfloat16), "mp", scatter_dimension=1, tiled=True
        ).astype(jnp.float32)
        + own_attended
    ).astype(jnp.bfloat16)
    all_grads = (
        lax.psum(grad_w_query.astype(jnp.bfloat16), "dp").astype(jnp.float32),
        lax.psum(grad_b_query.astype(jnp.bfloat16), "dp").astype(jnp.float32),
        lax.psum(grad_w_key.astype(jnp.bfloat16), "dp").astype(jnp.float32),
        lax.psum(grad_w_value.astype(jnp.bfloat16), "dp").astype(jnp.float32),
        lax.psum(grad_b_value.astype(jnp.bfloat16), "dp").astype(jnp.float32),
        lax.psum(grad_w_out.astype(jnp.bfloat16), "dp").astype(jnp.float32),
        lax.psum(grad_b_out.astype(jnp.bfloat16), "dp").astype(jnp.float32),
        lax.psum(grad_gain_one.astype(jnp.bfloat16), "dp").astype(jnp.float32),
        lax.psum(grad_shift_one.astype(jnp.bfloat16), "dp").astype(jnp.float32),
        lax.psum(grad_w_in.astype(jnp.bfloat16), "dp").astype(jnp.float32),
        lax.psum(grad_b_in.astype(jnp.bfloat16), "dp").astype(jnp.float32),
        lax.psum(grad_w_back.astype(jnp.bfloat16), "dp").astype(jnp.float32),
        lax.psum(grad_b_back.astype(jnp.bfloat16), "dp").astype(jnp.float32),
        lax.psum(grad_gain_two.astype(jnp.bfloat16), "dp").astype(jnp.float32),
        lax.psum(grad_shift_two.astype(jnp.bfloat16), "dp").astype(jnp.float32),
    )
    attn_grads = all_grads[:9]
    ffn_grads = all_grads[9:]
    return (
        output,
        input_grad,
        attn_grads[0],
        attn_grads[1],
        attn_grads[2],
        attn_grads[3],
        attn_grads[4],
        attn_grads[5],
        attn_grads[6],
        attn_grads[7],
        attn_grads[8],
        ffn_grads[0],
        ffn_grads[1],
        ffn_grads[2],
        ffn_grads[3],
        ffn_grads[4],
        ffn_grads[5],
    )


def solution(mesh):
    placed = (
        P("dp", "mp"),
        P("dp"),
        P(None, "mp"),
        P("mp"),
        P(None, "mp"),
        P(None, "mp"),
        P("mp"),
        P("mp", None),
        P("mp"),
        P("mp"),
        P("mp"),
        P(None, "mp"),
        P("mp"),
        P("mp", None),
        P("mp"),
        P("mp"),
        P("mp"),
        P("dp", "mp"),
    )
    return jax.shard_map(
        on_core if dict(mesh.shape) == {"dp": 16, "mp": 2} else on_device,
        mesh=mesh,
        in_specs=placed,
        out_specs=(
            P("dp", "mp"),
            P("dp", "mp"),
            P(None, "mp"),
            P("mp"),
            P(None, "mp"),
            P(None, "mp"),
            P("mp"),
            P("mp", None),
            P("mp"),
            P("mp"),
            P("mp"),
            P(None, "mp"),
            P("mp"),
            P("mp", None),
            P("mp"),
            P("mp"),
            P("mp"),
        ),
        check_vma=False,
    )
```
